32 devices in a mesh: dp: 8 (over z, y), col: 4 (over x, core).
Axes of the slice: x: 2, y: 2, z: 4, core: 2. Of those that a mesh axis runs over, the one named last changes fastest.
Arguments:
- bin_index: int32 [4096, 16], P('dp'), may hold values from 0 to 47
- bin_fraction: float32 [4096, 16], P('dp'), may hold values from 0 to 1
- row_mask: int32 [4096], P('dp'), may hold values from 0 to 1, as said below
- targets: int32 [4096], P('dp'), may hold values from 0 to 15
- w_first: float32 [768, 512], P('dp', 'col'), may hold values from -0.21875 to 0.21875
- w_second: float32 [512, 512], P('dp', 'col'), may hold values from -0.25 to 0.25
- w_head: float32 [32, 512, 16], P(None, 'dp'), may hold values from -0.5 to 0.5
- adapters: float32 [5, 32, 512], P(None, None, 'col'), may hold values from -1.5 to 1.5, as said below
- gains: float32 [32, 768], replicated, may hold values from 0.5 to 2
- head_bias: float32 [32, 16], replicated, may hold values from -3 to 3
- first_row: float32 [768], P('dp'), may hold values from 2.4414062e-09 to 1.8310548e-08
- first_col: float32 [512], P('col'), may hold values from 2.4414062e-09 to 1.8310548e-08
- second_row: float32 [512], P('dp'), may hold values from 1.4648438e-09 to 1.0986328e-08
- second_col: float32 [512], P('col'), may hold values from 1.4648438e-09 to 1.0986328e-08
- head_row: float32 [32, 512], P(None, 'dp'), may hold values from 1.953125e-09 to 1.4648437e-08
- head_col: float32 [32, 16], replicated, may hold values from 1.953125e-09 to 1.4648437e-08
- adapter_sq: float32 [5, 32, 512], P(None, None, 'col'), may hold values from 4.8828126e-11 to 3.6621095e-10
- gain_sq: float32 [32, 768], replicated, may hold values from 4.8828126e-11 to 3.6621095e-10
- bias_sq: float32 [32, 16], replicated, may hold values from 1.4648438e-09 to 1.0986328e-08
Outputs:
- first_grad: float32 [768, 512], P('dp', 'col')
- first_row_new: float32 [768], P('dp')
- first_col_new: float32 [512], P('col')
- first_new: float32 [768, 512], P('dp', 'col')
- second_grad: float32 [512, 512], P('dp', 'col')
- second_row_new: float32 [512], P('dp')
- second_col_new: float32 [512], P('col')
- second_new: float32 [512, 512], P('dp', 'col')
- head_grad: float32 [32, 512, 16], P(None, 'dp')
- head_row_new: float32 [32, 512], P(None, 'dp')
- head_col_new: float32 [32, 16], replicated
- head_new: float32 [32, 512, 16], P(None, 'dp')
- adapter_grad: float32 [5, 32, 512], P(None, None, 'col')
- adapter_sq_new: float32 [5, 32, 512], P(None, None, 'col')
- adapter_new: float32 [5, 32, 512], P(None, None, 'col')
- gain_grad: float32 [32, 768], replicated
- gain_sq_new: float32 [32, 768], replicated
- gain_new: float32 [32, 768], replicated
- bias_grad: float32 [32, 16], replicated
- bias_sq_new: float32 [32, 16], replicated
- bias_new: float32 [32, 16], replicated
- loss_sum: float32 [], replicated
- row_total: float32 [], replicated
- residual_rms: float32 [], replicated
- branch_rms: float32 [], replicated
The draws below stay inside these ranges and needn't reach their ends.
Inputs may be any that keep to these rules, and one draw needn't show every extreme that they name: `row_mask`: in each aligned block of 512 rows the ones form a leading run, longer on average in later blocks; the last block is all ones. `adapters`: scales (kinds 0, 2, 3) lie in 0.5 to 1.5; biases (kinds 1, 4) in -1.5 to 1.5.
All inputs are finite; a program needn't handle non-finite values.
Results may differ from the reference program's by a relative error of at most 0.0066.
The reference program's roundings to bfloat16 on the way count: a program that leaves them out, or rounds other values in their place, can miss the bound.
Values may be sent and summed in bfloat16 or wider, within the bound.
A program may use at most 256 MiB of HBM per device.

```python
import math
import jax
import jax.numpy as jnp
from jax import lax

D = 512
MEMBERS = 32
FEATS = 16
BINS = 48
CLASSES = 16
STEP = 10
TOK_DEV = 512
ENC = 768
TOKENS = 4096


def draw_row_mask(key, part):
    key = jax.random.fold_in(key, 5)
    blocks = TOKENS // TOK_DEV
    index = jnp.arange(blocks, dtype=jnp.int32)
    base = TOK_DEV * (blocks - 1 + 2 * index) // (3 * (blocks - 1))
    jitter = jax.random.randint(key, (blocks,), 0, TOK_DEV // 8 + 1, dtype=jnp.int32)
    length = jnp.where(index == blocks - 1, TOK_DEV, jnp.maximum(base - jitter, 1))
    places = jnp.arange(TOK_DEV, dtype=jnp.int32)
    return (places[None, :] < length[:, None]).astype(jnp.int32).reshape(TOKENS)


def draw_adapters(key, part):
    key = jax.random.fold_in(key, 3)
    scale_key, bias_key = jax.random.split(key)
    scales = jax.random.uniform(scale_key, (5, MEMBERS, D), jnp.float32, 0.5, 1.5)
    biases = jnp.clip(0.3 * jax.random.normal(bias_key, (5, MEMBERS, D), jnp.float32), -1.5, 1.5)
    kinds = jnp.arange(5, dtype=jnp.int32)[:, None, None]
    is_bias = (kinds == 1) | (kinds == 4)
    return jnp.where(is_bias, biases, scales)


def set_ends(drawn, key, least, largest):
    longest = drawn.shape.index(max(drawn.shape))
    spots = []
    for shift in (0, 1):
        where = [jax.random.randint(jax.random.fold_in(key, axis), (), 0, length) for axis, length in enumerate(drawn.shape)]
        where[longest] = (where[longest] + shift) % drawn.shape[longest]
        spots.append(tuple(where))
    return drawn.at[spots[0]].set(least).at[spots[1]].set(largest)


def level_of(key, extent, shards, low, high):
    factor_of = 1.0
    for dim, parts in shards:
        heights = jax.random.uniform(jax.random.fold_in(jax.random.fold_in(key, 6), dim), (parts,), jnp.float32, low / len(shards), high / len(shards))
        factor_of = factor_of * jnp.repeat(jnp.exp(heights), extent[dim] // parts).reshape((-1,) + (1,) * (len(extent) - 1 - dim))
    return factor_of


def bell_draw(stream_key, dims, scale, limit, cuts=(), held_as=jnp.bfloat16):
    level = level_of(stream_key, dims, cuts, -0.22, 0.18) if cuts else 1.0
    drawn = jax.random.normal(stream_key, dims, jnp.float32) * scale * level
    return jnp.minimum(jnp.maximum(drawn, -limit), limit).astype(held_as)


def setup_inputs(seed: int = 0) -> dict:
    seeds = jax.random.split(jax.random.key(seed), 20)
    return {
        "bin_index": set_ends(jax.random.randint(seeds[0], (TOKENS, FEATS), 0, BINS), jax.random.fold_in(seeds[0], 1), 0, BINS - 1).astype(jnp.int32),
        "bin_fraction": jnp.clip(1.0 * jax.random.uniform(seeds[1], (TOKENS, FEATS), jnp.float32) ** level_of(seeds[1], (TOKENS, FEATS), ((0, 8),), -0.2, 0.2), 0.0, 1.0),
        "row_mask": draw_row_mask(jax.random.fold_in(seeds[19], 71), 0),
        "targets": set_ends(jax.random.randint(seeds[3], (TOKENS,), 0, CLASSES), jax.random.fold_in(seeds[3], 1), 0, CLASSES - 1).astype(jnp.int32),
        "w_first": bell_draw(seeds[4], (ENC, D), ENC ** -0.5, 0.21875, ((0, 8), (1, 4)), jnp.float32),
        "w_second": bell_draw(seeds[5], (D, D), D ** -0.5, 0.25, ((0, 8), (1, 4)), jnp.float32),
        "w_head": bell_draw(seeds[6], (MEMBERS, D, CLASSES), (D // 4) ** -0.5, 0.5, ((1, 8),), jnp.float32),
        "adapters": draw_adapters(jax.random.fold_in(seeds[19], 71), 0),
        "gains": jnp.clip(jnp.exp(jax.random.uniform(seeds[8], (MEMBERS, ENC), jnp.float32, math.log(0.5), math.log(2.0))), 0.5, 2.0),
        "head_bias": bell_draw(seeds[9], (MEMBERS, CLASSES), 0.5, 3.0, (), jnp.float32),
        "first_row": jnp.clip(jnp.exp(math.log(1.831054774470431e-08) - 2.014903 * jax.random.uniform(seeds[10], (ENC,), jnp.float32) ** level_of(seeds[10], (ENC,), ((0, 8),), -0.2, 0.2)), 2.4414061883248905e-09, 1.831054774470431e-08),
        "first_col": jnp.clip(jnp.exp(math.log(1.831054774470431e-08) - 2.014903 * jax.random.uniform(seeds[11], (D,), jnp.float32) ** level_of(seeds[11], (D,), ((0, 4),), -0.2, 0.2)), 2.4414061883248905e-09, 1.831054774470431e-08),
        "second_row": jnp.clip(jnp.exp(math.log(1.0986328291551217e-08) - 2.014903 * jax.random.uniform(seeds[12], (D,), jnp.float32) ** level_of(seeds[12], (D,), ((0, 8),), -0.2, 0.2)), 1.4648438018127763e-09, 1.0986328291551217e-08),
        "second_col": jnp.clip(jnp.exp(math.log(1.0986328291551217e-08) - 2.014903 * jax.random.uniform(seeds[13], (D,), jnp.float32) ** level_of(seeds[13], (D,), ((0, 4),), -0.2, 0.2)), 1.4648438018127763e-09, 1.0986328291551217e-08),
        "head_row": jnp.clip(jnp.exp(math.log(1.4648437129949343e-08) - 2.014903 * jax.random.uniform(seeds[14], (MEMBERS, D), jnp.float32) ** level_of(seeds[14], (MEMBERS, D), ((1, 8),), -0.2, 0.2)), 1.9531249950688334e-09, 1.4648437129949343e-08),
        "head_col": jnp.clip(jnp.exp(jax.random.uniform(seeds[15], (MEMBERS, CLASSES), jnp.float32, math.log(1.9531249950688334e-09), math.log(1.4648437129949343e-08))), 1.9531249950688334e-09, 1.4648437129949343e-08),
        "adapter_sq": jnp.clip(jnp.exp(math.log(3.6621095045319407e-10) - 2.014903 * jax.random.uniform(seeds[16], (5, MEMBERS, D), jnp.float32) ** level_of(seeds[16], (5, MEMBERS, D), ((2, 4),), -0.2, 0.2)), 4.8828125570610226e-11, 3.6621095045319407e-10),
        "gain_sq": jnp.clip(jnp.exp(jax.random.uniform(seeds[17], (MEMBERS, ENC), jnp.float32, math.log(4.8828125570610226e-11), math.log(3.6621095045319407e-10))), 4.8828125570610226e-11, 3.6621095045319407e-10),
        "bias_sq": jnp.clip(jnp.exp(jax.random.uniform(seeds[18], (MEMBERS, CLASSES), jnp.float32, math.log(1.4648438018127763e-09), math.log(1.0986328291551217e-08))), 1.4648438018127763e-09, 1.0986328291551217e-08),
    }


@jax.custom_vjp
def low(v):
    return lax.optimization_barrier(v.astype(jnp.bfloat16)).astype(jnp.float32)

@jax.custom_vjp
def low_back(v):
    return v

def low_keep(v):
    return (low(v), None)

def low_pass(kept, grad):
    return (grad,)

def back_keep(v):
    return (v, None)

def back_low(kept, grad):
    return (low(grad),)
low.defvjp(low_keep, low_pass)
low_back.defvjp(back_keep, back_low)
EPS_SQUARE = 1e-30
CLIP_LIMIT = 1.0
RELATIVE_RATE = 0.4
RATE_FLOOR = 0.001
HIGH = lax.Precision.HIGHEST

def encode(bin_index, bin_fraction):
    levels = jnp.arange(BINS, dtype=jnp.int32)
    under_bin = levels[None, None, :] < bin_index[:, :, None]
    at_bin = levels[None, None, :] == bin_index[:, :, None]
    fraction = bin_fraction[:, :, None].astype(jnp.float32)
    encoded = jnp.where(under_bin, jnp.ones_like(fraction), jnp.where(at_bin, fraction, jnp.zeros_like(fraction)))
    return encoded.reshape(bin_index.shape[0], FEATS * BINS)

def forward(params, bin_index, bin_fraction, row_mask, targets, row_total):
    w_first, w_second, w_head, adapters, gains, head_bias = params
    encoded = encode(bin_index, bin_fraction)
    first_in = low(encoded[:, None, :] * gains[None])
    first_out = low_back(jnp.einsum('rmk,kd->rmd', first_in, low(w_first), precision=HIGH))
    stream_one = jax.nn.silu(first_out * adapters[0] + adapters[1])
    second_in = low(stream_one * adapters[2])
    second_out = low_back(jnp.einsum('rmk,kd->rmd', second_in, low(w_second), precision=HIGH))
    branch = jax.nn.silu(second_out * adapters[3] + adapters[4])
    stream_two = stream_one + branch
    logits = low_back(jnp.einsum('rmd,mdc->rmc', low(stream_two), low(w_head), precision=HIGH) + head_bias)
    log_total = jax.nn.logsumexp(logits, axis=-1)
    chosen = lax.optimization_barrier(jnp.sum(logits * jax.nn.one_hot(targets, CLASSES, dtype=logits.dtype)[:, None, :], axis=-1))
    weight = row_mask.astype(logits.dtype)[:, None]
    loss_terms = jnp.sum((log_total - chosen) * weight)
    loss = loss_terms / (MEMBERS * row_total)
    residual_sq = jnp.sum(stream_one * stream_one * weight[:, :, None])
    branch_sq = jnp.sum(branch * branch * weight[:, :, None])
    return (loss, (loss_terms, residual_sq, branch_sq))

def clipped(weight, update, axes):
    rms_update = jnp.sqrt(lax.optimization_barrier(jnp.mean(update * update, axis=axes, keepdims=True)))
    rms_weight = jnp.sqrt(lax.optimization_barrier(jnp.mean(weight * weight, axis=axes, keepdims=True)))
    update = update / jnp.maximum(1.0, rms_update / CLIP_LIMIT)
    return weight - RELATIVE_RATE * jnp.maximum(RATE_FLOOR, rms_weight) * update

def factored(weight, grad, row, column, decay):
    square = grad * grad + EPS_SQUARE
    row_new = decay * row + (1.0 - decay) * lax.optimization_barrier(jnp.mean(square, axis=-1))
    col_new = decay * column + (1.0 - decay) * lax.optimization_barrier(jnp.mean(square, axis=-2))
    estimate = row_new[..., :, None] * col_new[..., None, :] / lax.optimization_barrier(jnp.mean(row_new, axis=-1))[..., None, None]
    return (row_new, col_new, clipped(weight, grad * lax.rsqrt(estimate), None))

def unfactored(weight, grad, state, decay, axes):
    state_new = decay * state + (1.0 - decay) * (grad * grad + EPS_SQUARE)
    return (state_new, clipped(weight, grad * lax.rsqrt(state_new), axes))

def reference(bin_index, bin_fraction, row_mask, targets, w_first, w_second, w_head, adapters, gains, head_bias, first_row, first_col, second_row, second_col, head_row, head_col, adapter_sq, gain_sq, bias_sq):
    params = (w_first, w_second, w_head, adapters, gains, head_bias)
    row_total = jnp.sum(row_mask).astype(jnp.float32)
    count_blocks = TOKENS // TOK_DEV

    def split_rows(array):
        return array.reshape((count_blocks, TOK_DEV) + array.shape[1:])

    def one_block(carry, pieces):
        grads_sum, aux_sum = carry

        def loss_of(values):
            return forward(values, pieces[0], pieces[1], pieces[2], pieces[3], row_total)
        loss, pull, aux = jax.vjp(loss_of, params, has_aux=True)
        grads, = pull(jnp.ones_like(loss))
        return ((jax.tree.map(jnp.add, grads_sum, grads), jax.tree.map(jnp.add, aux_sum, aux)), None)
    zero_grads = jax.tree.map(jnp.zeros_like, params)
    zero_aux = (jnp.zeros((), jnp.float32), jnp.zeros((), jnp.float32), jnp.zeros((), jnp.float32))
    pieces = (split_rows(bin_index), split_rows(bin_fraction), split_rows(row_mask), split_rows(targets))
    (grads, aux), _ = lax.scan(one_block, (zero_grads, zero_aux), pieces)
    first_grad, second_grad, head_grad, adapter_grad, gain_grad, bias_grad = grads
    loss_sum, residual_sq, branch_sq = aux
    decay = 1.0 - STEP ** (-0.8)
    first_row_new, first_col_new, first_new = factored(w_first, first_grad, first_row, first_col, decay)
    second_row_new, second_col_new, second_new = factored(w_second, second_grad, second_row, second_col, decay)
    head_row_new, head_col_new, head_new = factored(w_head, head_grad, head_row, head_col, decay)
    adapter_sq_new, adapter_new = unfactored(adapters, adapter_grad, adapter_sq, decay, (1, 2))
    gain_sq_new, gain_new = unfactored(gains, gain_grad, gain_sq, decay, None)
    bias_sq_new, bias_new = unfactored(head_bias, bias_grad, bias_sq, decay, None)
    residual_rms = jnp.sqrt(residual_sq / (row_total * MEMBERS * D))
    branch_rms = jnp.sqrt(branch_sq / (row_total * MEMBERS * D))
    return (first_grad, first_row_new, first_col_new, first_new, second_grad, second_row_new, second_col_new, second_new, head_grad, head_row_new, head_col_new, head_new, adapter_grad, adapter_sq_new, adapter_new, gain_grad, gain_sq_new, gain_new, bias_grad, bias_sq_new, bias_new, loss_sum, row_total, residual_rms, branch_rms)
```

```python
import functools
import jax, jax.numpy as jnp
from jax import lax
from jax.experimental import pallas as pl
from jax.experimental.pallas import tpu as pltpu
from jax.sharding import PartitionSpec as P

FEATS, BINS, CLASSES = 16, 48, 16
STEP = 10
EPS_SQUARE = 1e-30
CLIP_LIMIT = 1.0
RELATIVE_RATE = 0.4
RATE_FLOOR = 0.001
R = 32
f32, bf16 = jnp.float32, jnp.bfloat16

def dot(a, b):
    return jnp.dot(a, b, preferred_element_type=f32)
def dot_t(a, b):
    return lax.dot_general(a, b, (((1,), (1,)), ((), ())), preferred_element_type=f32)
def t_dot(a, b):
    return lax.dot_general(a, b, (((0,), (0,)), ((), ())), preferred_element_type=f32)

MESH = pl.DeviceIdType.MESH


def far(array):
    return pltpu.with_memory_space_constraint(array, pltpu.HBM)


HIGH = lax.Precision.HIGHEST
VM = pl.BlockSpec(memory_space=pltpu.VMEM)
FAR = pl.BlockSpec(memory_space=pltpu.HBM)


def place():
    d, c = lax.axis_index("dp"), lax.axis_index("col")
    return d // 2, d % 2, c // 2, c % 2


def z_other(z, k):
    if k == 0:
        return z
    return [None, z + 1 - 2 * (z % 2), (z + 2) % 4, 3 - z][k]


def other(b, k):
    return 1 - b if k else b


def device(z, y, x, core):
    return (2 * z + y, 2 * x + core)


PLANE = ((0, 1), (1, 0), (1, 1))
DP_PEERS = tuple((kz, ky) for kz in range(4) for ky in range(2))[1:]
COL_PEERS = ((0, 1), (1, 0), (1, 1))
SPLIT = 112


class Sender:
    def __init__(self, send_sem, recv_sem):
        self.send_sem, self.recv_sem, self.count = send_sem, recv_sem, 0
        self.all = []

    def __call__(self, src, dst, target):
        i = self.count
        self.count += 1
        copy = pltpu.make_async_remote_copy(
            src_ref=src, dst_ref=dst, send_sem=self.send_sem.at[i], recv_sem=self.recv_sem.at[i],
            device_id=target, device_id_type=MESH)
        copy.start()
        self.all.append(copy)
        return copy


def greet(targets):
    barrier = pltpu.get_barrier_semaphore()
    for target in targets:
        pl.semaphore_signal(barrier, inc=1, device_id=target, device_id_type=MESH)
    return barrier, len(targets)


def hdot(a, b, dims=((1,), (0,))):
    return lax.dot_general(a, b, (dims, ((), ())), precision=HIGH, preferred_element_type=f32)


def gather_kernel(bin_index, bin_fraction, row_mask, targets, w_first, w_second, w_head, adapters_far,
                  buf, hbuf, adbuf, comp, info, table, recv,
                  w_first_v, w_second_v, w_head_v, adapters, bin_index_v, bin_fraction_v, row_mask_v, targets_v,
                  load_sem, send_sem, recv_sem):
    z, y, x, core = place()
    loads = [pltpu.make_async_copy(src, dst, load_sem.at[i]) for i, (src, dst) in enumerate((
        (w_first, w_first_v), (w_second, w_second_v), (w_head, w_head_v), (adapters_far, adapters),
        (bin_index, bin_index_v), (bin_fraction, bin_fraction_v), (row_mask, row_mask_v), (targets, targets_v)))]
    for load in loads:
        load.start()
    rows = bin_index.shape[1]
    rf, rs = w_first.shape[0], w_second.shape[0]
    me_c = 2 * x + core
    mem = adbuf.shape[2]
    near = [device(z_other(z, kz), other(y, ky), x, core) for kz, ky in DP_PEERS]
    near += [device(z, y, other(x, kx), other(core, kc)) for kx, kc in COL_PEERS]
    near += [device(z, 1 - y, 1 - x, core)]
    barrier, count = greet(near)
    loads[0].wait()
    loads[1].wait()
    buf[z, y, x, core, 0:rf, :] = w_first_v[...].astype(bf16)
    buf[z, y, x, core, rf:rf + rs, :] = w_second_v[...].astype(bf16)
    pl.semaphore_wait(barrier, count)
    send = Sender(send_sem, recv_sem)
    s0, s1 = pl.ds(0, SPLIT), pl.ds(SPLIT, rf + rs - SPLIT)
    own0, own1 = buf.at[z, y, x, core, s0], buf.at[z, y, x, core, s1]
    a0 = [send(own0, own0, device(z_other(z, k), y, x, core)) for k in (1, 2, 3)]
    a1 = [send(own1, own1, device(z, other(y, ky), other(x, kx), core)) for ky, kx in PLANE]
    for load in loads[2:]:
        load.wait()
    hbuf[z, y] = w_head_v[pl.ds(me_c * mem, mem)].reshape(mem * CLASSES, rs).T.astype(bf16)
    adbuf[me_c] = adapters[:, pl.ds(pl.multiple_of(me_c * mem, mem), mem), :]
    slot = rows // 8
    i_row = lax.broadcasted_iota(jnp.int32, (rows, rows), 0)
    i_col = lax.broadcasted_iota(jnp.int32, (rows, rows), 1)
    me_d = 2 * z + y
    wanted = (i_row % slot) * 8 + (i_row // slot + me_d) % 8
    deal = (i_col == wanted).astype(bf16)
    frac = bin_fraction_v[...]
    hi = frac.astype(bf16).astype(f32)
    mask = row_mask_v[...].astype(f32)
    length = jnp.sum(mask, axis=1, keepdims=True)
    high = jnp.floor(length * (1.0 / 16.0))
    c_i = lax.broadcasted_iota(jnp.int32, (CLASSES, rows), 0)
    m_i = lax.broadcasted_iota(jnp.int32, (64, rows), 0)
    marks = jnp.where(m_i == 0, mask, jnp.where(m_i == 1, high, jnp.where(m_i == 2, length - 16.0 * high, 0.0)))
    columns = jnp.concatenate([bin_index_v[...].astype(f32), hi, frac - hi, jnp.where(c_i == targets_v[...], mask, 0.0), marks], axis=0)
    table[...] = dot_t(deal, columns.astype(bf16)).astype(bf16)
    own_rows = pl.ds(pl.multiple_of(me_d * slot, slot), slot)
    recv[own_rows, :] = table[own_rows, :]
    t = []
    for kz, ky in DP_PEERS:
        pz, py = z_other(z, kz), other(y, ky)
        theirs = pl.ds(pl.multiple_of((2 * pz + py) * slot, slot), slot)
        t.append(send(table.at[theirs], recv.at[own_rows], device(pz, py, x, core)))
    h = [send(hbuf.at[z, y], hbuf.at[z, y], device(z_other(z, k), y, x, core)) for k in (1, 2, 3)]
    for kx, kc in COL_PEERS:
        px, pc = other(x, kx), other(core, kc)
        theirs = pl.ds(pl.multiple_of((2 * px + pc) * mem, mem), mem)
        send(adapters.at[:, theirs, :], adbuf.at[me_c], device(z, y, px, pc))
    ad = send.all[-3:]
    for cp in a0:
        cp.wait_recv()
    b0 = [send(buf.at[:, y, x, core, s0], buf.at[:, y, x, core, s0], device(z, other(y, ky), other(x, kx), core))
          for ky, kx in PLANE]
    mate = device(z, y, x, 1 - core)
    for cp in a1:
        cp.wait_recv()
    b1 = [send(buf.at[z, :, :, core, s1], buf.at[z, :, :, core, s1], device(z_other(z, k), y, x, core))
          for k in (1, 2, 3)]
    last = [send(buf.at[:, y, x, core, s0], buf.at[:, y, x, core, s0], mate),
            send(buf.at[z, :, :, core, s1], buf.at[z, :, :, core, s1], mate)]
    for cp in h:
        cp.wait_recv()
    h2 = send(hbuf.at[:, y], hbuf.at[:, y], device(z, 1 - y, x, core))
    for cp in t:
        cp.wait_recv()
    lane8 = lax.broadcasted_iota(jnp.int32, (8, 128), 1)
    got = recv[...]
    mask_row = dot_t((lane8 == 64).astype(bf16), got)
    pos = dot(mask_row.astype(bf16), (i_row < i_col).astype(bf16))
    spot = jnp.where(mask_row > 0.5, pos, -1.0)[0:1]
    perm = (i_row.astype(f32) == spot).astype(bf16)
    comp[...] = dot(perm, got).astype(bf16)
    lane = lax.broadcasted_iota(jnp.int32, (1, 128), 1)
    per_row = jnp.where(lane == 65, 16.0, jnp.where(lane == 66, 1.0, 0.0))
    total = jnp.sum(jnp.sum(got.astype(f32), axis=0, keepdims=True) * per_row, axis=1, keepdims=True) / slot
    info[0:1, :] = jnp.zeros((1, 128), f32) + jnp.sum(mask_row[0:1], axis=1, keepdims=True)
    info[1:2, :] = jnp.zeros((1, 128), f32) + total
    info[2:8, :] = jnp.zeros((6, 128), f32)
    for cp, k in zip(b1, (1, 2, 3)):
        cp.wait_recv()
        pz = z_other(z, k)
        last.append(send(buf.at[pz, :, :, core, s1], buf.at[pz, :, :, core, s1], mate))
    for cp, (ky, kx) in zip(b0, PLANE):
        cp.wait_recv()
        py, px = other(y, ky), other(x, kx)
        last.append(send(buf.at[:, py, px, core, s0], buf.at[:, py, px, core, s0], mate))
    for cp in last + ad + [h2]:
        cp.wait_recv()
    for cp in send.all:
        cp.wait_send()


def call_gather(bin_index, bin_fraction, row_mask, targets, w_first, w_second, w_head, adapters, mem):
    rows = bin_index.shape[1]
    both = w_first.shape[0] + w_second.shape[0]
    return pl.pallas_call(
        gather_kernel,
        out_shape=(
            jax.ShapeDtypeStruct((4, 2, 2, 2, both, 128), bf16),
            jax.ShapeDtypeStruct((4, 2, w_head.shape[2], 128), bf16),
            jax.ShapeDtypeStruct((4, 5, mem, 128), f32),
            jax.ShapeDtypeStruct((rows, 128), bf16),
            jax.ShapeDtypeStruct((8, 128), f32),
        ),
        in_specs=[FAR] * 8, out_specs=(VM,) * 5,
        scratch_shapes=[pltpu.VMEM((rows, 128), bf16), pltpu.VMEM((rows, 128), bf16),
                        pltpu.VMEM(w_first.shape, f32), pltpu.VMEM(w_second.shape, f32),
                        pltpu.VMEM(w_head.shape, f32), pltpu.VMEM(adapters.shape, f32),
                        pltpu.VMEM(bin_index.shape, jnp.int32), pltpu.VMEM(bin_fraction.shape, f32),
                        pltpu.VMEM((1, rows), jnp.int32), pltpu.VMEM((1, rows), jnp.int32),
                        pltpu.SemaphoreType.DMA((8,)),
                        pltpu.SemaphoreType.DMA((40,)), pltpu.SemaphoreType.DMA((40,))],
        compiler_params=pltpu.CompilerParams(collective_id=0, has_side_effects=True, vmem_limit_bytes=16 << 20),
    )(*map(far, (bin_index, bin_fraction, row_mask.reshape(1, -1), targets.reshape(1, -1),
                 w_first, w_second, w_head, adapters)))


def seg_max(x):
    lane = lax.broadcasted_iota(jnp.int32, x.shape, 1)
    n = x.shape[1]
    for s in (1, 2, 4, 8):
        up = pltpu.roll(x, n - s, 1)
        dn = pltpu.roll(x, s, 1)
        x = jnp.maximum(x, jnp.where((lane & s) == 0, up, dn))
    return x


def compute_kernel(members, buf, hbuf, adbuf, comp, info, gains_far, bias_far,
                   gbuf, hb, small,
                   w1, w2, w2t, head, headt, adapters, gains, enc_all, fog_all,
                   first_acc, second_acc, head_acc, adapt, gain_acc, sums, gains_all, bias_all, load_sem):
    rows_all = comp.shape[0]
    enc_w, width = w1.shape
    mem = adbuf.shape[2]
    hw = mem * CLASSES
    rf, rs = enc_w // 8, width // 8
    me_c = lax.axis_index("col")
    loads = [pltpu.make_async_copy(gains_far, gains_all, load_sem.at[0]),
             pltpu.make_async_copy(bias_far, bias_all, load_sem.at[1])]
    for load in loads:
        load.start()
    for d in range(8):
        for c in range(4):
            lanes = slice(128 * c, 128 * c + 128)
            w1[rf * d:rf * (d + 1), lanes] = buf[d // 2, d % 2, c // 2, c % 2, 0:rf, :]
            w2[rs * d:rs * (d + 1), lanes] = buf[d // 2, d % 2, c // 2, c % 2, rf:rf + rs, :]
        head[rs * d:rs * (d + 1), :] = hbuf[d // 2, d % 2]
    for c in range(4):
        adapters[:, :, 128 * c:128 * c + 128] = adbuf[c]
    w2t[...] = w2[...].T
    headt[...] = head[...].T
    for load in loads:
        load.wait()
    own = pl.ds(pl.multiple_of(me_c * mem, mem), mem)
    gains[...] = gains_all[own, :]
    owner = lax.broadcasted_iota(jnp.int32, (1, hw), 1) // CLASSES
    fold = (lax.broadcasted_iota(jnp.int32, (CLASSES, hw), 1) % CLASSES
            == lax.broadcasted_iota(jnp.int32, (CLASSES, hw), 0)).astype(f32)
    wide = hdot(bias_all[...], fold, ((0,), (0,)))
    at = lax.broadcasted_iota(jnp.int32, (members, hw), 0)
    bias = jnp.sum(jnp.where(at == me_c * mem + owner, wide, 0.0), axis=0, keepdims=True)
    n_rows = jnp.max(info[0:1, :]).astype(jnp.int32)
    loss_scale = 1.0 / (members * info[1:2, :])
    tiles = (n_rows + (R - 1)) // R
    fog_all[...] = jnp.zeros_like(fog_all)
    enc_all[...] = jnp.zeros_like(enc_all)
    second_acc[...] = jnp.zeros_like(second_acc)
    head_acc[...] = jnp.zeros_like(head_acc)
    adapt[...] = jnp.zeros_like(adapt)
    sums[...] = jnp.zeros_like(sums)

    kk = lax.broadcasted_iota(jnp.int32, (128, enc_w), 1)
    ll = lax.broadcasted_iota(jnp.int32, (128, enc_w), 0)
    ff = ll & (FEATS - 1)
    spread = ((ll < 48) & (kk >= ff * BINS) & (kk < (ff + 1) * BINS)).astype(bf16)
    lev = (lax.broadcasted_iota(jnp.int32, (1, enc_w), 1) % BINS).astype(f32)
    l2 = lax.broadcasted_iota(jnp.int32, (128, 2 * hw), 0)
    c2 = lax.broadcasted_iota(jnp.int32, (128, 2 * hw), 1)
    oh_spread = (l2 == jnp.where(c2 < hw, 48 + (c2 & (CLASSES - 1)), 64)).astype(bf16)
    s_i = lax.broadcasted_iota(jnp.int32, (hw, hw), 0) // CLASSES
    s_j = lax.broadcasted_iota(jnp.int32, (hw, hw), 1) // CLASSES
    seg = (s_i == s_j).astype(bf16)

    def tile(t, carry):
        rows = pl.ds(pl.multiple_of(t * R, R), R)
        T = comp[rows, :]
        enc = jnp.clip(dot(T, spread) - lev, 0.0, 1.0)
        enc_all[rows, :] = enc.astype(bf16)
        fin = jnp.concatenate([(enc * gains[m:m + 1, :]).astype(bf16) for m in range(mem)], axis=0)
        fo = dot(fin, w1[...])
        hs, us, sos, sins = [], [], [], []
        res = jnp.zeros((R, width), f32)
        for m in range(mem):
            h = fo[m * R:(m + 1) * R] * (0.5 * adapters[0, m:m + 1, :]) + 0.5 * adapters[1, m:m + 1, :]
            u = 1.0 + jnp.tanh(h)
            so = h * u
            res += so * so
            hs.append(h)
            us.append(u)
            sos.append(so)
            sins.append((so * adapters[2, m:m + 1, :]).astype(bf16))
        sin = jnp.concatenate(sins, axis=0)
        s2 = dot(sin, w2[...])
        h2s, u2s, brs, sts = [], [], [], []
        bres = jnp.zeros((R, width), f32)
        for m in range(mem):
            h = s2[m * R:(m + 1) * R] * (0.5 * adapters[3, m:m + 1, :]) + 0.5 * adapters[4, m:m + 1, :]
            u = 1.0 + jnp.tanh(h)
            br = h * u
            bres += br * br
            h2s.append(h)
            u2s.append(u)
            brs.append(br)
            sts.append((sos[m] + br).astype(bf16))
        st = jnp.concatenate(sts, axis=0)
        lo = dot(st, head[...])
        logits = bias
        for m in range(mem):
            logits = logits + jnp.where(owner == m, lo[m * R:(m + 1) * R], 0.0)
        top = seg_max(logits)
        ex = jnp.exp(logits - top)
        exh = ex.astype(bf16)
        exl = (ex - exh.astype(f32)).astype(bf16)
        tot = dot(exh, seg) + dot(exl, seg)
        ohm = dot(T, oh_spread)
        oh, mk = ohm[:, :hw], ohm[:, hw:]
        loss_c = (top + jnp.log(tot) - logits) * oh
        lgf = ((ex / tot * mk - oh) * loss_scale).astype(bf16).astype(f32)
        lgm = jnp.concatenate([jnp.where(owner == m, lgf, 0.0).astype(bf16) for m in range(mem)], axis=0)
        head_acc[...] += t_dot(lgm, st)
        sg = dot(lgm, headt[...])
        ogs = []
        for m in range(mem):
            pg = sg[m * R:(m + 1) * R] * (u2s[m] + brs[m] * (2.0 - u2s[m]))
            adapt[3, m:m + 1, :] += jnp.sum(pg * h2s[m], axis=0, keepdims=True)
            adapt[4, m:m + 1, :] += jnp.sum(pg, axis=0, keepdims=True)
            ogs.append((pg * (0.5 * adapters[3, m:m + 1, :])).astype(bf16))
        og = jnp.concatenate(ogs, axis=0)
        second_acc[...] += t_dot(sin, og)
        ig = dot(og, w2t[...])
        for m in range(mem):
            igm = ig[m * R:(m + 1) * R]
            adapt[2, m:m + 1, :] += jnp.sum(igm * sos[m], axis=0, keepdims=True)
            one = sg[m * R:(m + 1) * R] + igm * adapters[2, m:m + 1, :]
            low = one * (us[m] + sos[m] * (2.0 - us[m]))
            adapt[0, m:m + 1, :] += jnp.sum(low * hs[m], axis=0, keepdims=True)
            adapt[1, m:m + 1, :] += jnp.sum(low, axis=0, keepdims=True)
            fog_all[m, rows, :] = (low * (0.5 * adapters[0, m:m + 1, :])).astype(bf16)
        spare = jnp.maximum((t + 1) * R - n_rows, 0).astype(f32)
        sums[0:1, :hw] += jnp.sum(lgf, axis=0, keepdims=True)
        sums[1:2, :hw] += jnp.sum(loss_c, axis=0, keepdims=True)
        sums[2:3, :] += jnp.sum(res, axis=0, keepdims=True) - spare * res[R - 1:R]
        sums[3:4, :] += jnp.sum(bres, axis=0, keepdims=True) - spare * bres[R - 1:R]
        return carry

    lax.fori_loop(0, tiles, tile, 0)
    enct = enc_all[...].T
    gcol = jnp.concatenate([gains[...], jnp.zeros((128 - mem, enc_w), f32)], axis=0).T
    for m in range(mem):
        g = dot(enct, fog_all[m])
        gain_acc[:, m:m + 1] = jnp.sum(g * w1[...].astype(f32), axis=1, keepdims=True)
        if m == 0:
            first_acc[...] = g * gcol[:, m:m + 1]
        else:
            first_acc[...] += g * gcol[:, m:m + 1]
    gain_rows = gain_acc[...].T
    for d in range(8):
        for c in range(4):
            lanes = slice(128 * c, 128 * c + 128)
            gbuf[d // 2, d % 2, c // 2, c % 2, 0:rf, :] = first_acc[rf * d:rf * (d + 1), lanes].astype(bf16)
            gbuf[d // 2, d % 2, c // 2, c % 2, rf:rf + rs, :] = second_acc[rs * d:rs * (d + 1), lanes].astype(bf16)
    head_t = head_acc[...].T
    for d in range(8):
        hb[d // 2, d % 2] = head_t[rs * d:rs * (d + 1), :].astype(bf16)
    small[...] = jnp.zeros_like(small)
    a0, a1, a2 = adapt[0], adapt[1], adapt[2]
    a3, a4 = adapt[3], adapt[4]
    fixed = ((a0 - 0.5 * adapters[1] * a1) / adapters[0], 0.5 * a1, a2,
             (a3 - 0.5 * adapters[4] * a4) / adapters[3], 0.5 * a4)
    for m in range(mem):
        for k in range(4):
            for j in range(5):
                small[m, 8 * k + j:8 * k + j + 1, :] = fixed[j][m:m + 1, 128 * k:128 * k + 128]
        for i in range(enc_w // 128):
            small[m, 32 + i:33 + i, :] = gain_rows[m:m + 1, 128 * i:128 * i + 128]
    def four(row):
        return row[:, 0:128] + row[:, 128:256] + row[:, 256:384] + row[:, 384:512]
    small[0, 39:40, :] = sums[1:2, 0:128]
    small[1, 39:40, :] = four(sums[2:3, :])
    small[2, 39:40, :] = four(sums[3:4, :])
    small[3, 39:40, :] = sums[0:1, 0:128]


def call_compute(members, buf, hbuf, adbuf, comp, info, gains, bias):
    rows = comp.shape[0]
    enc_w = gains.shape[1]
    mem = adbuf.shape[2]
    width = adbuf.shape[0] * 128
    hw = mem * CLASSES
    return pl.pallas_call(
        functools.partial(compute_kernel, members),
        out_shape=(
            jax.ShapeDtypeStruct(buf.shape, bf16),
            jax.ShapeDtypeStruct(hbuf.shape, bf16),
            jax.ShapeDtypeStruct((8, 40, 128), f32),
        ),
        in_specs=[VM] * 5 + [FAR] * 2, out_specs=(VM,) * 3,
        scratch_shapes=[
            pltpu.VMEM((enc_w, width), bf16), pltpu.VMEM((width, width), bf16), pltpu.VMEM((width, width), bf16),
            pltpu.VMEM((width, hw), bf16), pltpu.VMEM((hw, width), bf16),
            pltpu.VMEM((5, mem, width), f32), pltpu.VMEM((mem, enc_w), f32),
            pltpu.VMEM((rows, enc_w), bf16), pltpu.VMEM((mem, rows, width), bf16),
            pltpu.VMEM((enc_w, width), f32), pltpu.VMEM((width, width), f32), pltpu.VMEM((hw, width), f32),
            pltpu.VMEM((5, mem, width), f32), pltpu.VMEM((enc_w, 128), f32), pltpu.VMEM((8, width), f32),
            pltpu.VMEM(gains.shape, f32), pltpu.VMEM(bias.shape, f32), pltpu.SemaphoreType.DMA((2,)),
        ],
        compiler_params=pltpu.CompilerParams(vmem_limit_bytes=30 << 20),
    )(buf, hbuf, adbuf, comp, info, far(gains), far(bias))


def reduce_kernel(enc_w, width, members,
                  gbuf, hb, small, info, w_first, w_second, w_head, adapters, gains, head_bias,
                  first_row, first_col, second_row, second_col, head_row, head_col, adapter_sq, gain_sq, bias_sq,
                  o_first_grad, o_first_row, o_first_col, o_first_new,
                  o_second_grad, o_second_row, o_second_col, o_second_new,
                  o_head_grad, o_head_row, o_head_col, o_head_new,
                  o_adapter_grad, o_adapter_sq, o_adapter_new,
                  o_gain_grad, o_gain_sq, o_gain_new,
                  o_bias_grad, o_bias_sq, o_bias_new,
                  o_loss, o_rows, o_residual, o_branch,
                  cbuf, sbuf, plane0, held0, zed0, zed1, held1, plane1, hy, hsum, hz, hcol,
                  fr, gall, ca, cg, colmsg, colall, rowmsg, rowall, msg, msgall, send_sem, recv_sem):
    z, y, x, core = place()
    me_c = 2 * x + core
    rf, rs = w_first.shape[0], w_second.shape[0]
    mem = members // 4
    hw = mem * CLASSES
    decay = 1.0 - STEP ** (-0.8)
    everyone = []
    for kz in range(4):
        for ky in range(2):
            for kx in range(2):
                for kc in range(2):
                    if kz or ky or kx or kc:
                        everyone.append(device(z_other(z, kz), other(y, ky), other(x, kx), other(core, kc)))
    barrier, count = greet(everyone)
    pl.semaphore_wait(barrier, count)
    send = Sender(send_sem, recv_sem)
    s0, s1 = pl.ds(0, SPLIT), pl.ds(SPLIT, rf + rs - SPLIT)
    mate = device(z, y, x, 1 - core)
    swap1 = send(gbuf.at[:, :, :, 1 - core, s1], cbuf.at[:, :, :, s1], mate)
    swap0 = send(gbuf.at[:, :, :, 1 - core, s0], cbuf.at[:, :, :, s0], mate)
    head1 = send(hb.at[:, 1 - y], hy, device(z, 1 - y, x, core))
    deal = [send(small.at[2 * z_other(z, kz) + other(y, ky)], fr.at[i], device(z_other(z, kz), other(y, ky), x, core))
            for i, (kz, ky) in enumerate(DP_PEERS)]
    w1, w2 = w_first[...], w_second[...]
    wh = [w_head[mem * c:mem * (c + 1)].reshape(hw, rs).T for c in range(4)]
    own_w = (jnp.sum(w1 * w1), jnp.sum(w2 * w2), sum(jnp.sum(w * w) for w in wh))
    adapter_w = [jnp.sum(adapters[j] * adapters[j]) for j in range(5)]
    swap1.wait_recv()
    sbuf[:, :, :, s1, :] = (gbuf[:, :, :, core, s1, :].astype(f32) + cbuf[:, :, :, s1, :].astype(f32)).astype(bf16)
    p1 = [send(sbuf.at[z_other(z, k), :, :, s1], zed1.at[k - 1], device(z_other(z, k), y, x, core)) for k in (1, 2, 3)]
    swap0.wait_recv()
    sbuf[:, :, :, s0, :] = (gbuf[:, :, :, core, s0, :].astype(f32) + cbuf[:, :, :, s0, :].astype(f32)).astype(bf16)
    p0 = [send(sbuf.at[:, other(y, ky), other(x, kx), s0], plane0.at[i], device(z, other(y, ky), other(x, kx), core))
          for i, (ky, kx) in enumerate(PLANE)]
    head1.wait_recv()
    hsum[...] = (hb[:, y].astype(f32) + hy[...].astype(f32)).astype(bf16)
    head2 = [send(hsum.at[z_other(z, k)], hz.at[k - 1], device(z_other(z, k), y, x, core)) for k in (1, 2, 3)]
    for cp in deal:
        cp.wait_recv()
    me_d = 2 * z + y
    mine = small[me_d]
    for i in range(7):
        mine = mine + fr[i]
    gall[me_d] = mine
    spread_dp = [send(gall.at[me_d], gall.at[me_d], device(z_other(z, kz), other(y, ky), x, core)) for kz, ky in DP_PEERS]
    for cp in p1:
        cp.wait_recv()
    part = sbuf[z, :, :, s1, :].astype(f32)
    for i in range(3):
        part = part + zed1[i].astype(f32)
    held1[...] = part.astype(bf16)
    q1 = [send(held1.at[other(y, ky), other(x, kx)], plane1.at[i], device(z, other(y, ky), other(x, kx), core))
          for i, (ky, kx) in enumerate(PLANE)]
    for cp in head2:
        cp.wait_recv()
    hown = hsum[z].astype(f32)
    for i in range(3):
        hown = hown + hz[i].astype(f32)
    hcol[me_c] = hown
    head3 = [send(hcol.at[me_c], hcol.at[me_c], device(z, y, other(x, kx), other(core, kc))) for kx, kc in COL_PEERS]
    for cp in p0:
        cp.wait_recv()
    part = sbuf[:, y, x, s0, :].astype(f32)
    for i in range(3):
        part = part + plane0[i].astype(f32)
    held0[...] = part.astype(bf16)
    q0 = [send(held0.at[z_other(z, k)], zed0.at[k - 1], device(z_other(z, k), y, x, core)) for k in (1, 2, 3)]
    for cp in spread_dp:
        cp.wait_recv()
    own8 = pl.ds(pl.multiple_of(8 * me_c, 8), 8)
    ca[me_c] = gall[:, own8, :]
    cg[me_c] = gall[:, 32:40, :]
    spread_col = []
    for kx, kc in COL_PEERS:
        px, pc = other(x, kx), other(core, kc)
        theirs = pl.ds(pl.multiple_of(8 * (2 * px + pc), 8), 8)
        spread_col.append(send(gall.at[:, theirs], ca.at[me_c], device(z, y, px, pc)))
        spread_col.append(send(gall.at[:, 32:40], cg.at[me_c], device(z, y, px, pc)))
    g0 = held0[z].astype(f32)
    g1 = held1[y, x].astype(f32)
    for cp in q1:
        cp.wait_recv()
    for i in range(3):
        g1 = g1 + plane1[i].astype(f32)
    for cp in q0:
        cp.wait_recv()
    for i in range(3):
        g0 = g0 + zed0[i].astype(f32)
    first = g0[0:rf]
    second = jnp.concatenate([g0[rf:SPLIT], g1], axis=0)
    o_first_grad[...] = first
    o_second_grad[...] = second
    first_sq = first * first + EPS_SQUARE
    second_sq = second * second + EPS_SQUARE
    for cp in head3:
        cp.wait_recv()
    hg = [hcol[c] for c in range(4)]
    hsq = [g * g + EPS_SQUARE for g in hg]
    seg8 = (lax.broadcasted_iota(jnp.int32, (mem, hw), 1) // CLASSES
            == lax.broadcasted_iota(jnp.int32, (mem, hw), 0)).astype(f32)
    ones8 = jnp.ones((8, 128), f32)
    hrow = [decay * head_row[mem * c:mem * (c + 1), :]
            + (1.0 - decay) / CLASSES * hdot(seg8, hsq[c], ((1,), (1,))) for c in range(4)]
    hrowx = [hdot(hrow[c], seg8, ((0,), (0,))) for c in range(4)]
    for c in range(4):
        o_head_row[mem * c:mem * (c + 1), :] = hrow[c]
    rowmsg[:, 0:rf] = hdot(ones8, first_sq, ((1,), (1,)))
    rowmsg[:, 128:128 + rs] = hdot(ones8, second_sq, ((1,), (1,)))
    rowall[me_c] = rowmsg[...]
    def add_up(v):
        return jnp.sum(v, axis=0, keepdims=True)
    colmsg[0:1, :] = add_up(first_sq)
    colmsg[1:2, :] = add_up(second_sq)
    for c in range(4):
        colmsg[2 + c:3 + c, :] = add_up(hsq[c])
        colmsg[8 + c:9 + c, :] = add_up(hrowx[c])
    colall[me_d] = colmsg[...]
    r1 = [send(colmsg, colall.at[me_d], device(z_other(z, kz), other(y, ky), x, core)) for kz, ky in DP_PEERS]
    r1 += [send(rowmsg, rowall.at[me_c], device(z, y, other(x, kx), other(core, kc))) for kx, kc in COL_PEERS]
    for cp in spread_col:
        cp.wait_recv()
    fold = (lax.broadcasted_iota(jnp.int32, (CLASSES, hw), 1) % CLASSES
            == lax.broadcasted_iota(jnp.int32, (CLASSES, hw), 0)).astype(f32)
    to8 = (lax.broadcasted_iota(jnp.int32, (8, members), 1) // mem
           == lax.broadcasted_iota(jnp.int32, (8, members), 0)).astype(f32)
    keep = (lax.broadcasted_iota(jnp.int32, (members, hw), 1) // CLASSES
            == lax.broadcasted_iota(jnp.int32, (members, hw), 0) % mem).astype(f32)
    def to_lanes(v):
        return hdot(to8, hdot(v, fold, ((0,), (0,))) * keep)
    def from_lanes(v):
        return hdot(fold, hdot(to8, v, ((0,), (0,))) * keep, ((1,), (1,)))
    def lane_sum(v):
        return jnp.sum(v, axis=1, keepdims=True)
    def total(v):
        return lane_sum(add_up(v))
    def step_size(weight_sq, entries):
        return RELATIVE_RATE * jnp.maximum(RATE_FLOOR, jnp.sqrt(weight_sq / entries))
    def apply(weight, update, update_sq, weight_sq, entries):
        limit = jnp.maximum(1.0, jnp.sqrt(update_sq / entries) / CLIP_LIMIT)
        return weight - step_size(weight_sq, entries) * (update / limit)
    adapter_up = []
    for j in range(5):
        grad = jnp.concatenate([ca[c, :, j, :] for c in range(4)], axis=0)
        sq = decay * adapter_sq[j] + (1.0 - decay) * (grad * grad + EPS_SQUARE)
        o_adapter_grad[j] = grad
        o_adapter_sq[j] = sq
        adapter_up.append(grad * lax.rsqrt(sq))
    for c in range(4):
        for i in range(enc_w // 128):
            o_gain_grad[mem * c:mem * (c + 1), 128 * i:128 * (i + 1)] = cg[c, :, i, :]
    gain = o_gain_grad[...]
    gain_state = decay * gain_sq[...] + (1.0 - decay) * (gain * gain + EPS_SQUARE)
    o_gain_sq[...] = gain_state
    gain_up = gain * lax.rsqrt(gain_state)
    o_gain_new[...] = apply(gains[...], gain_up, total(gain_up * gain_up), total(gains[...] * gains[...]), members * enc_w)
    bias_lanes = jnp.concatenate([cg[c, 3, 7:8, :] for c in range(4)] + [jnp.zeros((4, 128), f32)], axis=0)
    bias = from_lanes(bias_lanes)
    bias_state = decay * bias_sq[...] + (1.0 - decay) * (bias * bias + EPS_SQUARE)
    o_bias_grad[...] = bias
    o_bias_sq[...] = bias_state
    bias_up = bias * lax.rsqrt(bias_state)
    o_bias_new[...] = apply(head_bias[...], bias_up, total(bias_up * bias_up), total(head_bias[...] * head_bias[...]), members * CLASSES)
    rows_total = info[1:2, 0:1]
    o_rows[...] = rows_total
    o_loss[...] = lane_sum(sum(cg[c, 0, 7:8, :] for c in range(4)))
    spread_over = rows_total * (members * width)
    o_residual[...] = jnp.sqrt(lane_sum(sum(cg[c, 1, 7:8, :] for c in range(4))) / spread_over)
    o_branch[...] = jnp.sqrt(lane_sum(sum(cg[c, 2, 7:8, :] for c in range(4))) / spread_over)
    hcol_old = to_lanes(head_col[...])
    for cp in r1:
        cp.wait_recv()
    col_sums = colall[0]
    for d in range(1, 8):
        col_sums = col_sums + colall[d]
    row_sums = (rowall[0] + rowall[1]) + (rowall[2] + rowall[3])
    first_r = decay * first_row[...] + (1.0 - decay) / width * row_sums[0:1, 0:rf]
    second_r = decay * second_row[...] + (1.0 - decay) / width * row_sums[0:1, 128:128 + rs]
    first_c = decay * first_col[...] + (1.0 - decay) / enc_w * col_sums[0:1]
    second_c = decay * second_col[...] + (1.0 - decay) / width * col_sums[1:2]
    head_c = decay * hcol_old[0:4] + (1.0 - decay) / width * col_sums[2:6]
    o_first_row[...] = first_r
    o_second_row[...] = second_r
    o_first_col[...] = first_c
    o_second_col[...] = second_c
    o_head_col[...] = from_lanes(jnp.concatenate([head_c, jnp.zeros((4, 128), f32)], axis=0))
    ones1 = jnp.ones((1, 128), f32)
    first_up = first * lax.rsqrt(hdot(first_r, ones1, ((0,), (0,))) * first_c)
    second_up = second * lax.rsqrt(hdot(second_r, ones1, ((0,), (0,))) * second_c)
    head_up = [hg[c] * lax.rsqrt(hrowx[c] * head_c[c:c + 1] / (col_sums[8 + c:9 + c] / width)) for c in range(4)]
    lane = lax.broadcasted_iota(jnp.int32, (1, 128), 1)
    scalars = [total(first_up * first_up), lane_sum(first_r), total(second_up * second_up), lane_sum(second_r),
               own_w[0], own_w[1], sum(total(u * u) for u in head_up), own_w[2]]
    scalars += [total(u * u) for u in adapter_up] + adapter_w
    line = jnp.zeros((1, 128), f32)
    for i, v in enumerate(scalars):
        line = jnp.where(lane == i, v, line)
    msg[...] = jnp.broadcast_to(line, (8, 128))
    msgall[z, y, x, core] = msg[...]
    r2 = []
    for target in everyone:
        r2.append(send(msg, msgall.at[z, y, x, core], target))
    for c in range(4):
        o_head_grad[mem * c:mem * (c + 1)] = hg[c].T.reshape(mem, CLASSES, rs)
    for cp in r2:
        cp.wait_recv()
    def over_dp(cx, cc):
        out = msgall[0, 0, cx, cc, 0:1, :]
        for d in range(1, 8):
            out = out + msgall[d // 2, d % 2, cx, cc, 0:1, :]
        return out
    s_dp = over_dp(x, core)
    s_all = (over_dp(0, 0) + over_dp(0, 1)) + (over_dp(1, 0) + over_dp(1, 1))
    s_col = (msgall[z, y, 0, 0, 0:1, :] + msgall[z, y, 0, 1, 0:1, :]) + (msgall[z, y, 1, 0, 0:1, :] + msgall[z, y, 1, 1, 0:1, :])
    def item(v, i):
        return lane_sum(jnp.where(lane == i, v, 0.0))
    first_mean = item(s_dp, 1) / enc_w
    o_first_new[...] = apply(w1, first_up * jnp.sqrt(first_mean), item(s_all, 0) * first_mean, item(s_all, 4), enc_w * width)
    second_mean = item(s_dp, 3) / width
    o_second_new[...] = apply(w2, second_up * jnp.sqrt(second_mean), item(s_all, 2) * second_mean, item(s_all, 5), width * width)
    for j in range(5):
        o_adapter_new[j] = apply(adapters[j], adapter_up[j], item(s_col, 8 + j), item(s_col, 13 + j), members * width)
    for c in range(4):
        new = apply(wh[c], head_up[c], item(s_dp, 6), item(s_dp, 7), members * width * CLASSES)
        o_head_new[mem * c:mem * (c + 1)] = new.T.reshape(mem, CLASSES, rs)
    for cp in send.all:
        cp.wait_send()


def call_reduce(gbuf, hb, small, info, w_first, w_second, w_head, adapters, gains, head_bias,
                first_row, first_col, second_row, second_col, head_row, head_col, adapter_sq, gain_sq, bias_sq):
    members, enc_w = gains.shape
    rf, rs = w_first.shape[0], w_second.shape[0]
    both = rf + rs
    late = both - SPLIT
    width = w_first.shape[1] * 4
    def like(a):
        return jax.ShapeDtypeStruct(a.shape, f32)
    def row(a):
        return jax.ShapeDtypeStruct((1, a.shape[0]), f32)
    one = jax.ShapeDtypeStruct((1, 1), f32)
    def buffer(*shape, dtype=f32):
        return pltpu.VMEM(shape, dtype)
    outs = pl.pallas_call(
        functools.partial(reduce_kernel, enc_w, width, members),
        out_shape=(like(w_first), row(first_row), row(first_col), like(w_first),
                   like(w_second), row(second_row), row(second_col), like(w_second),
                   like(w_head), like(head_row), like(head_col), like(w_head),
                   like(adapters), like(adapters), like(adapters),
                   like(gains), like(gains), like(gains),
                   like(head_bias), like(head_bias), like(head_bias), one, one, one, one),
        in_specs=[VM] * 19, out_specs=(VM,) * 25,
        scratch_shapes=[
            buffer(4, 2, 2, both, 128, dtype=bf16), buffer(4, 2, 2, both, 128, dtype=bf16),
            buffer(3, 4, SPLIT, 128, dtype=bf16), buffer(4, SPLIT, 128, dtype=bf16),
            buffer(3, SPLIT, 128, dtype=bf16), buffer(3, 2, 2, late, 128, dtype=bf16),
            buffer(2, 2, late, 128, dtype=bf16), buffer(3, late, 128, dtype=bf16),
            buffer(4, rs, 128, dtype=bf16), buffer(4, rs, 128, dtype=bf16), buffer(3, rs, 128, dtype=bf16),
            buffer(4, rs, 128),
            buffer(7, 40, 128), buffer(8, 40, 128), buffer(4, 8, 8, 128), buffer(4, 8, 8, 128),
            buffer(16, 128), buffer(8, 16, 128), buffer(8, 256), buffer(4, 8, 256),
            buffer(8, 128), buffer(4, 2, 2, 2, 8, 128),
            pltpu.SemaphoreType.DMA((100,)), pltpu.SemaphoreType.DMA((100,)),
        ],
        compiler_params=pltpu.CompilerParams(collective_id=1, has_side_effects=True, vmem_limit_bytes=16 << 20),
    )(gbuf, hb, small, info, w_first, w_second, w_head, adapters, gains, head_bias,
      first_row.reshape(1, -1), first_col.reshape(1, -1), second_row.reshape(1, -1), second_col.reshape(1, -1),
      head_row, head_col, adapter_sq, gain_sq, bias_sq)
    outs = call_store(outs)
    for i in (1, 2, 5, 6):
        outs[i] = outs[i].reshape(-1)
    for i in (21, 22, 23, 24):
        outs[i] = outs[i].reshape(())
    for i in (8, 11):
        outs[i] = outs[i].transpose(0, 2, 1)
    for i in (10, 18, 19, 20):
        outs[i] = outs[i].T
    return tuple(outs)


def store_kernel(count, *refs):
    sems = refs[2 * count]
    copies = [pltpu.make_async_copy(refs[i], refs[count + i], sems.at[i]) for i in range(count)]
    for copy in copies:
        copy.start()
    for copy in copies:
        copy.wait()


def call_store(arrays):
    count = len(arrays)
    return list(pl.pallas_call(
        functools.partial(store_kernel, count),
        out_shape=tuple(jax.ShapeDtypeStruct(a.shape, a.dtype) for a in arrays),
        in_specs=[VM] * count, out_specs=(FAR,) * count,
        scratch_shapes=[pltpu.SemaphoreType.DMA((count,))],
        compiler_params=pltpu.CompilerParams(vmem_limit_bytes=16 << 20),
    )(*arrays))


def local_blocks(bin_index, bin_fraction, row_mask, targets, w_first, w_second, w_head, adapters, gains, head_bias,
          first_row, first_col, second_row, second_col, head_row, head_col, adapter_sq, gain_sq, bias_sq):
    members = gains.shape[0]
    mem = members // 4
    w_head, head_bias, head_col, bias_sq = w_head.transpose(0, 2, 1), head_bias.T, head_col.T, bias_sq.T
    buf, hbuf, adbuf, comp, info = call_gather(
        bin_index.T, bin_fraction.T, row_mask, targets, w_first, w_second, w_head, adapters, mem)
    gbuf, hb, small = call_compute(members, buf, hbuf, adbuf, comp, info, gains, head_bias)
    return call_reduce(gbuf, hb, small, info, w_first, w_second, w_head, adapters, gains, head_bias,
                       first_row, first_col, second_row, second_col, head_row, head_col, adapter_sq, gain_sq, bias_sq)


def finish(weight, update, update_sq, weight_sq, entries):
    rms_update = jnp.sqrt(update_sq / entries)
    rms_weight = jnp.sqrt(weight_sq / entries)
    update = update / jnp.maximum(1.0, rms_update / CLIP_LIMIT)
    return weight - RELATIVE_RATE * jnp.maximum(RATE_FLOOR, rms_weight) * update


def local_any(bin_index, bin_fraction, row_mask, targets, w_first, w_second, w_head, adapters, gains, head_bias,
              first_row, first_col, second_row, second_col, head_row, head_col, adapter_sq, gain_sq, bias_sq):
    count_col = lax.axis_size("col")
    count_dp = lax.axis_size("dp")
    col_place = lax.axis_index("col")
    dp_place = lax.axis_index("dp")
    members, enc_width = gains.shape
    col_width = adapters.shape[2]
    full_width = col_width * count_col
    mem = members // count_col
    rows = row_mask.shape[0]
    decay = 1.0 - STEP ** (-0.8)
    row_total = lax.psum(jnp.sum(row_mask.astype(f32)), "dp")
    hi = bin_fraction.astype(bf16).astype(f32)
    onehot = jax.nn.one_hot(targets, CLASSES, dtype=f32) * row_mask[:, None]
    table = jnp.concatenate([bin_index.astype(f32), hi, bin_fraction - hi, onehot, row_mask[:, None].astype(f32),
                             jnp.zeros((rows, 63), f32)], axis=1).astype(bf16)
    table = table.reshape(rows // count_dp, count_dp, 128)
    table = jnp.roll(table, -dp_place, axis=1).transpose(1, 0, 2).reshape(rows, 128)
    table = lax.all_to_all(table, "dp", 0, 0, tiled=True)
    mask = table[:, 64].astype(jnp.int32)
    spot = jnp.where(mask > 0, jnp.cumsum(mask) - 1, -1)
    comp = jnp.dot((jnp.arange(rows)[:, None] == spot[None, :]).astype(bf16), table, preferred_element_type=f32).astype(bf16)
    info = jnp.zeros((8, 128), f32).at[0].set(jnp.sum(mask).astype(f32)).at[1].set(row_total)

    def whole(part):
        return lax.all_gather(lax.all_gather(part.astype(bf16), "dp", axis=0, tiled=True), "col", axis=1, tiled=True)

    def blocks(full):
        return full.reshape(8, -1, 4, 128).transpose(0, 2, 1, 3)

    def unblock(part):
        return part.astype(f32).reshape(8, 4, -1, 128).transpose(0, 2, 1, 3).reshape(-1, full_width)
    buf = jnp.concatenate([blocks(whole(w_first)), blocks(whole(w_second))], axis=2).reshape(4, 2, 2, 2, -1, 128)
    heads = lax.all_gather(w_head.astype(bf16), "dp", axis=1, tiled=True)
    heads = lax.dynamic_slice_in_dim(heads, col_place * mem, mem, 0)
    hbuf = heads.transpose(1, 0, 2).reshape(4, 2, -1, mem * CLASSES)
    adbuf = lax.dynamic_slice_in_dim(lax.all_gather(adapters, "col", axis=0), col_place * mem, mem, 2)
    gbuf, hb, small = call_compute(members, buf, hbuf, adbuf, comp, info, gains, head_bias.T)
    rf = enc_width // 8
    first_part, second_part = unblock(gbuf[..., :rf, :]), unblock(gbuf[..., rf:, :])
    head_part = hb.astype(f32).reshape(full_width, mem, CLASSES).transpose(1, 0, 2)

    def scatter(part):
        return lax.psum_scatter(lax.psum_scatter(part, "dp", scatter_dimension=0, tiled=True), "col", scatter_dimension=1, tiled=True)
    first_grad, second_grad = scatter(first_part), scatter(second_part)
    head_grad = lax.all_gather(lax.psum_scatter(head_part, "dp", scatter_dimension=1, tiled=True), "col", axis=0, tiled=True)
    adapter_part = small[:, :32].reshape(mem, 4, 8, 128)[:, :, :5].transpose(2, 0, 1, 3).reshape(5, mem, full_width)
    adapter_grad = lax.psum(lax.all_to_all(adapter_part, "col", 2, 1, tiled=True), "dp")
    gain_part = small[:, 32:32 + enc_width // 128].reshape(mem, enc_width)
    bias_part = small[3, 39].reshape(mem, CLASSES)
    gain_grad, bias_grad = lax.psum(
        (lax.all_gather(gain_part, "col", axis=0, tiled=True), lax.all_gather(bias_part, "col", axis=0, tiled=True)), "dp")
    loss_sum, residual_sq, branch_sq = lax.psum(jnp.sum(small[:3, 39], axis=1), ("dp", "col"))
    first_square = first_grad * first_grad + EPS_SQUARE
    second_square = second_grad * second_grad + EPS_SQUARE
    head_square = head_grad * head_grad + EPS_SQUARE
    first_rowsum, second_rowsum = lax.psum(
        (jnp.sum(first_square, axis=1), jnp.sum(second_square, axis=1)), "col"
    )
    first_row_new = decay * first_row + (1.0 - decay) * (first_rowsum / full_width)
    second_row_new = decay * second_row + (1.0 - decay) * (second_rowsum / full_width)
    head_row_new = decay * head_row + (1.0 - decay) * jnp.mean(head_square, axis=-1)
    stats = lax.psum(
        (
            jnp.sum(first_square, axis=0),
            jnp.sum(second_square, axis=0),
            jnp.sum(head_square, axis=1),
            jnp.sum(first_row_new),
            jnp.sum(second_row_new),
            jnp.sum(head_row_new, axis=1),
        ),
        "dp",
    )
    first_colsum, second_colsum, head_colsum, first_rowtotal, second_rowtotal, head_rowtotal = stats
    first_col_new = decay * first_col + (1.0 - decay) * (first_colsum / enc_width)
    second_col_new = decay * second_col + (1.0 - decay) * (second_colsum / full_width)
    head_col_new = decay * head_col + (1.0 - decay) * (head_colsum / full_width)
    first_estimate = first_row_new[:, None] * first_col_new[None, :] / (first_rowtotal / enc_width)
    second_estimate = (
        second_row_new[:, None] * second_col_new[None, :] / (second_rowtotal / full_width)
    )
    head_estimate = (
        head_row_new[:, :, None]
        * head_col_new[:, None, :]
        / (head_rowtotal / full_width)[:, None, None]
    )
    first_update = first_grad * lax.rsqrt(first_estimate)
    second_update = second_grad * lax.rsqrt(second_estimate)
    head_update = head_grad * lax.rsqrt(head_estimate)
    adapter_sq_new = decay * adapter_sq + (1.0 - decay) * (adapter_grad * adapter_grad + EPS_SQUARE)
    adapter_update = adapter_grad * lax.rsqrt(adapter_sq_new)
    gain_sq_new = decay * gain_sq + (1.0 - decay) * (gain_grad * gain_grad + EPS_SQUARE)
    gain_update = gain_grad * lax.rsqrt(gain_sq_new)
    bias_sq_new = decay * bias_sq + (1.0 - decay) * (bias_grad * bias_grad + EPS_SQUARE)
    bias_update = bias_grad * lax.rsqrt(bias_sq_new)
    share_col = 1.0 / count_col
    share_dp = 1.0 / count_dp
    sums = lax.psum(
        (
            jnp.sum(first_update * first_update),
            jnp.sum(w_first * w_first),
            jnp.sum(second_update * second_update),
            jnp.sum(w_second * w_second),
            jnp.sum(head_update * head_update) * share_col,
            jnp.sum(w_head * w_head) * share_col,
            jnp.sum(adapter_update * adapter_update, axis=(1, 2)) * share_dp,
            jnp.sum(adapters * adapters, axis=(1, 2)) * share_dp,
        ),
        ("dp", "col"),
    )
    first_new = finish(w_first, first_update, sums[0], sums[1], enc_width * full_width)
    second_new = finish(w_second, second_update, sums[2], sums[3], full_width * full_width)
    head_new = finish(w_head, head_update, sums[4], sums[5], members * full_width * CLASSES)
    adapter_new = finish(
        adapters,
        adapter_update,
        sums[6].reshape(5, 1, 1),
        sums[7].reshape(5, 1, 1),
        members * full_width,
    )
    gain_new = finish(
        gains,
        gain_update,
        jnp.sum(gain_update * gain_update),
        jnp.sum(gains * gains),
        members * enc_width,
    )
    bias_new = finish(
        head_bias,
        bias_update,
        jnp.sum(bias_update * bias_update),
        jnp.sum(head_bias * head_bias),
        members * CLASSES,
    )
    residual_rms = jnp.sqrt(residual_sq / (row_total * members * full_width))
    branch_rms = jnp.sqrt(branch_sq / (row_total * members * full_width))
    return (
        first_grad,
        first_row_new,
        first_col_new,
        first_new,
        second_grad,
        second_row_new,
        second_col_new,
        second_new,
        head_grad,
        head_row_new,
        head_col_new,
        head_new,
        adapter_grad,
        adapter_sq_new,
        adapter_new,
        gain_grad,
        gain_sq_new,
        gain_new,
        bias_grad,
        bias_sq_new,
        bias_new,
        loss_sum,
        row_total,
        residual_rms,
        branch_rms,
    )


def local(*args):
    if lax.axis_size("dp") == 8 and lax.axis_size("col") == 4:
        return local_blocks(*args)
    return local_any(*args)


def solution(mesh):
    placed = (
        P("dp", None),
        P("dp", None),
        P("dp"),
        P("dp"),
        P("dp", "col"),
        P("dp", "col"),
        P(None, "dp", None),
        P(None, None, "col"),
        P(),
        P(),
        P("dp"),
        P("col"),
        P("dp"),
        P("col"),
        P(None, "dp"),
        P(),
        P(None, None, "col"),
        P(),
        P(),
    )
    return jax.shard_map(
        local,
        mesh=mesh,
        in_specs=placed,
        out_specs=(
            P("dp", "col"),
            P("dp"),
            P("col"),
            P("dp", "col"),
            P("dp", "col"),
            P("dp"),
            P("col"),
            P("dp", "col"),
            P(None, "dp", None),
            P(None, "dp"),
            P(),
            P(None, "dp", None),
            P(None, None, "col"),
            P(None, None, "col"),
            P(None, None, "col"),
            P(),
            P(),
            P(),
            P(),
            P(),
            P(),
            P(),
            P(),
            P(),
            P(),
        ),
        check_vma=False,
    )
```

```python
import functools
import jax, jax.numpy as jnp
from jax import lax
from jax.experimental import pallas as pl
from jax.experimental.pallas import tpu as pltpu
from jax.sharding import PartitionSpec as P

FEATS, BINS, CLASSES = 16, 48, 16
STEP = 10
EPS_SQUARE = 1e-30
CLIP_LIMIT = 1.0
RELATIVE_RATE = 0.4
RATE_FLOOR = 0.001
R = 64
GROUPS = 2
ORDER = (0, 1, 0, 1, 0, 1, 0, 1, 0, 1, 0, 1, 0, 1, 0, 1, 0, 1, 0, 1, 0, 1)
f32, bf16 = jnp.float32, jnp.bfloat16

def dot(a, b):
    return jnp.dot(a, b, preferred_element_type=f32)
def dot_t(a, b):
    return lax.dot_general(a, b, (((1,), (1,)), ((), ())), preferred_element_type=f32)
def t_dot(a, b):
    return lax.dot_general(a, b, (((0,), (0,)), ((), ())), preferred_element_type=f32)

MESH = pl.DeviceIdType.MESH


def far(array):
    return pltpu.with_memory_space_constraint(array, pltpu.HBM)


HIGH = lax.Precision.HIGHEST
VM = pl.BlockSpec(memory_space=pltpu.VMEM)
FAR = pl.BlockSpec(memory_space=pltpu.HBM)


def place():
    d, c = lax.axis_index("dp"), lax.axis_index("col")
    return d // 2, d % 2, c // 2, c % 2


def z_other(z, k):
    if k == 0:
        return z
    return [None, z + 1 - 2 * (z % 2), (z + 2) % 4, 3 - z][k]


def other(b, k):
    return 1 - b if k else b


def device(z, y, x, core):
    return (2 * z + y, 2 * x + core)


PLANE = ((0, 1), (1, 0), (1, 1))
DP_PEERS = tuple((kz, ky) for kz in range(4) for ky in range(2))[1:]
COL_PEERS = ((0, 1), (1, 0), (1, 1))
SPLIT = 112


class Sender:
    def __init__(self, send_sem, recv_sem):
        self.send_sem, self.recv_sem, self.count = send_sem, recv_sem, 0
        self.all = []

    def __call__(self, src, dst, target):
        i = self.count
        self.count += 1
        copy = pltpu.make_async_remote_copy(
            src_ref=src, dst_ref=dst, send_sem=self.send_sem.at[i], recv_sem=self.recv_sem.at[i],
            device_id=target, device_id_type=MESH)
        copy.start()
        self.all.append(copy)
        return copy


def greet(targets):
    barrier = pltpu.get_barrier_semaphore()
    for target in targets:
        pl.semaphore_signal(barrier, inc=1, device_id=target, device_id_type=MESH)
    return barrier, len(targets)


def hdot(a, b, dims=((1,), (0,))):
    return lax.dot_general(a, b, (dims, ((), ())), precision=HIGH, preferred_element_type=f32)


def gather_kernel(bin_index, bin_fraction, row_mask, targets, w_first, w_second, w_head, adapters_far,
                  buf, hbuf, adbuf, enc, onehots, info, table, recv,
                  w_first_v, w_second_v, w_head_v, adapters, bin_index_v, bin_fraction_v, row_mask_v, targets_v,
                  load_sem, send_sem, recv_sem):
    z, y, x, core = place()
    loads = [pltpu.make_async_copy(src, dst, load_sem.at[i]) for i, (src, dst) in enumerate((
        (w_first, w_first_v), (w_second, w_second_v), (w_head, w_head_v), (adapters_far, adapters),
        (bin_index, bin_index_v), (bin_fraction, bin_fraction_v), (row_mask, row_mask_v), (targets, targets_v)))]
    for load in loads:
        load.start()
    rows = bin_index.shape[1]
    rf, rs = w_first.shape[0], w_second.shape[0]
    me_c = 2 * x + core
    mem = adbuf.shape[2]
    near = [device(z_other(z, kz), other(y, ky), x, core) for kz, ky in DP_PEERS]
    near += [device(z, y, other(x, kx), other(core, kc)) for kx, kc in COL_PEERS]
    near += [device(z, 1 - y, 1 - x, core)]
    barrier, count = greet(near)
    loads[0].wait()
    loads[1].wait()
    buf[z, y, x, core, 0:rf, :] = w_first_v[...].astype(bf16)
    buf[z, y, x, core, rf:rf + rs, :] = w_second_v[...].astype(bf16)
    pl.semaphore_wait(barrier, count)
    send = Sender(send_sem, recv_sem)
    s0, s1 = pl.ds(0, SPLIT), pl.ds(SPLIT, rf + rs - SPLIT)
    own0, own1 = buf.at[z, y, x, core, s0], buf.at[z, y, x, core, s1]
    a0 = [send(own0, own0, device(z_other(z, k), y, x, core)) for k in (1, 2, 3)]
    a1 = [send(own1, own1, device(z, other(y, ky), other(x, kx), core)) for ky, kx in PLANE]
    for load in loads[2:]:
        load.wait()
    hbuf[z, y] = w_head_v[pl.ds(me_c * mem, mem)].reshape(mem * CLASSES, rs).T.astype(bf16)
    adbuf[me_c] = adapters[:, pl.ds(pl.multiple_of(me_c * mem, mem), mem), :]
    slot = rows // 8
    i_row = lax.broadcasted_iota(jnp.int32, (rows, rows), 0)
    i_col = lax.broadcasted_iota(jnp.int32, (rows, rows), 1)
    me_d = 2 * z + y
    wanted = (i_row % slot) * 8 + (i_row // slot + me_d) % 8
    deal = (i_col == wanted).astype(bf16)
    frac = bin_fraction_v[...]
    hi = frac.astype(bf16).astype(f32)
    mask = row_mask_v[...].astype(f32)
    length = jnp.sum(mask, axis=1, keepdims=True)
    high = jnp.floor(length * (1.0 / 16.0))
    c_i = lax.broadcasted_iota(jnp.int32, (CLASSES, rows), 0)
    m_i = lax.broadcasted_iota(jnp.int32, (64, rows), 0)
    marks = jnp.where(m_i == 0, mask, jnp.where(m_i == 1, high, jnp.where(m_i == 2, length - 16.0 * high, 0.0)))
    columns = jnp.concatenate([bin_index_v[...].astype(f32), hi, frac - hi, jnp.where(c_i == targets_v[...], mask, 0.0), marks], axis=0)
    table[...] = dot_t(deal, columns.astype(bf16)).astype(bf16)
    own_rows = pl.ds(pl.multiple_of(me_d * slot, slot), slot)
    recv[own_rows, :] = table[own_rows, :]
    t = []
    for kz, ky in DP_PEERS:
        pz, py = z_other(z, kz), other(y, ky)
        theirs = pl.ds(pl.multiple_of((2 * pz + py) * slot, slot), slot)
        t.append(send(table.at[theirs], recv.at[own_rows], device(pz, py, x, core)))
    h = [send(hbuf.at[z, y], hbuf.at[z, y], device(z_other(z, k), y, x, core)) for k in (1, 2, 3)]
    for kx, kc in COL_PEERS:
        px, pc = other(x, kx), other(core, kc)
        theirs = pl.ds(pl.multiple_of((2 * px + pc) * mem, mem), mem)
        send(adapters.at[:, theirs, :], adbuf.at[me_c], device(z, y, px, pc))
    ad = send.all[-3:]
    for cp in a0:
        cp.wait_recv()
    b0 = [send(buf.at[:, y, x, core, s0], buf.at[:, y, x, core, s0], device(z, other(y, ky), other(x, kx), core))
          for ky, kx in PLANE]
    mate = device(z, y, x, 1 - core)
    for cp in a1:
        cp.wait_recv()
    b1 = [send(buf.at[z, :, :, core, s1], buf.at[z, :, :, core, s1], device(z_other(z, k), y, x, core))
          for k in (1, 2, 3)]
    last = [send(buf.at[:, y, x, core, s0], buf.at[:, y, x, core, s0], mate),
            send(buf.at[z, :, :, core, s1], buf.at[z, :, :, core, s1], mate)]
    for cp in h:
        cp.wait_recv()
    h2 = send(hbuf.at[:, y], hbuf.at[:, y], device(z, 1 - y, x, core))
    for cp in t:
        cp.wait_recv()
    lane8 = lax.broadcasted_iota(jnp.int32, (8, 128), 1)
    got = recv[...]
    mask_row = dot_t((lane8 == 64).astype(bf16), got)
    pos = dot(mask_row.astype(bf16), (i_row < i_col).astype(bf16))
    spot = jnp.where(mask_row > 0.5, pos, -1.0)[0:1]
    perm = (i_row.astype(f32) == spot).astype(bf16)
    enc_w, hw = enc.shape[1], onehots.shape[1]
    kk = lax.broadcasted_iota(jnp.int32, (128, enc_w), 1)
    ll = lax.broadcasted_iota(jnp.int32, (128, enc_w), 0)
    ff = ll & (FEATS - 1)
    spread = ((ll < 48) & (kk >= ff * BINS) & (kk < (ff + 1) * BINS)).astype(bf16)
    lev = (lax.broadcasted_iota(jnp.int32, (1, enc_w), 1) % BINS).astype(f32)
    l2 = lax.broadcasted_iota(jnp.int32, (128, hw), 0)
    c2 = lax.broadcasted_iota(jnp.int32, (128, hw), 1)
    oh_spread = (l2 == 48 + (c2 & (CLASSES - 1))).astype(bf16)
    comp = dot(perm, got).astype(bf16)
    enc[...] = jnp.clip(dot(comp, spread) - lev, 0.0, 1.0).astype(bf16)
    onehots[...] = dot(comp, oh_spread).astype(bf16)
    lane = lax.broadcasted_iota(jnp.int32, (1, 128), 1)
    per_row = jnp.where(lane == 65, 16.0, jnp.where(lane == 66, 1.0, 0.0))
    total = jnp.sum(jnp.sum(got.astype(f32), axis=0, keepdims=True) * per_row, axis=1, keepdims=True) / slot
    info[0:1, :] = jnp.zeros((1, 128), f32) + jnp.sum(mask_row[0:1], axis=1, keepdims=True)
    info[1:2, :] = jnp.zeros((1, 128), f32) + total
    info[2:8, :] = jnp.zeros((6, 128), f32)
    for cp, k in zip(b1, (1, 2, 3)):
        cp.wait_recv()
        pz = z_other(z, k)
        last.append(send(buf.at[pz, :, :, core, s1], buf.at[pz, :, :, core, s1], mate))
    for cp, (ky, kx) in zip(b0, PLANE):
        cp.wait_recv()
        py, px = other(y, ky), other(x, kx)
        last.append(send(buf.at[:, py, px, core, s0], buf.at[:, py, px, core, s0], mate))
    for cp in last + ad + [h2]:
        cp.wait_recv()
    for cp in send.all:
        cp.wait_send()


def call_gather(bin_index, bin_fraction, row_mask, targets, w_first, w_second, w_head, adapters, mem):
    rows = bin_index.shape[1]
    both = w_first.shape[0] + w_second.shape[0]
    return pl.pallas_call(
        gather_kernel,
        out_shape=(
            jax.ShapeDtypeStruct((4, 2, 2, 2, both, 128), bf16),
            jax.ShapeDtypeStruct((4, 2, w_head.shape[2], 128), bf16),
            jax.ShapeDtypeStruct((4, 5, mem, 128), f32),
            jax.ShapeDtypeStruct((rows, FEATS * BINS), bf16),
            jax.ShapeDtypeStruct((rows, mem * CLASSES), bf16),
            jax.ShapeDtypeStruct((8, 128), f32),
        ),
        in_specs=[FAR] * 8, out_specs=(VM,) * 6,
        scratch_shapes=[pltpu.VMEM((rows, 128), bf16), pltpu.VMEM((rows, 128), bf16),
                        pltpu.VMEM(w_first.shape, f32), pltpu.VMEM(w_second.shape, f32),
                        pltpu.VMEM(w_head.shape, f32), pltpu.VMEM(adapters.shape, f32),
                        pltpu.VMEM(bin_index.shape, jnp.int32), pltpu.VMEM(bin_fraction.shape, f32),
                        pltpu.VMEM((1, rows), jnp.int32), pltpu.VMEM((1, rows), jnp.int32),
                        pltpu.SemaphoreType.DMA((8,)),
                        pltpu.SemaphoreType.DMA((40,)), pltpu.SemaphoreType.DMA((40,))],
        compiler_params=pltpu.CompilerParams(collective_id=0, has_side_effects=True, vmem_limit_bytes=16 << 20),
    )(*map(far, (bin_index, bin_fraction, row_mask.reshape(1, -1), targets.reshape(1, -1),
                 w_first, w_second, w_head, adapters)))


def seg_max(x):
    lane = lax.broadcasted_iota(jnp.int32, x.shape, 1)
    n = x.shape[1]
    for s in (1, 2, 4, 8):
        up = pltpu.roll(x, n - s, 1)
        dn = pltpu.roll(x, s, 1)
        x = jnp.maximum(x, jnp.where((lane & s) == 0, up, dn))
    return x


def fold8(v):
    return sum(v[8 * i:8 * i + 8] for i in range(v.shape[0] // 8))


def compute_kernel(members, buf, hbuf, adbuf, enc_all, onehots, info, gains_far, bias_far,
                   w1, fog_all, sbuf, hb, small,
                   w2, w2t, head, headt, adapters, gains, low_gains,
                   second_acc, head_acc, adapt, sums, halves, gains_all, bias_all, load_sem):
    rows_all = enc_all.shape[0]
    enc_w, width = w1.shape
    mem = adbuf.shape[2]
    hw = mem * CLASSES
    rf, rs = enc_w // 8, width // 8
    me_c = lax.axis_index("col")
    loads = [pltpu.make_async_copy(gains_far, gains_all, load_sem.at[0]),
             pltpu.make_async_copy(bias_far, bias_all, load_sem.at[1])]
    for load in loads:
        load.start()
    for d in range(8):
        for c in range(4):
            lanes = slice(128 * c, 128 * c + 128)
            w1[rf * d:rf * (d + 1), lanes] = buf[d // 2, d % 2, c // 2, c % 2, 0:rf, :]
            w2[rs * d:rs * (d + 1), lanes] = buf[d // 2, d % 2, c // 2, c % 2, rf:rf + rs, :]
        head[rs * d:rs * (d + 1), :] = hbuf[d // 2, d % 2]
    for c in range(4):
        adapters[:, :, 128 * c:128 * c + 128] = adbuf[c]
    for j in (0, 1, 3, 4):
        halves[j] = 0.5 * adapters[j]
    w2t[...] = w2[...].T
    headt[...] = head[...].T
    for load in loads:
        load.wait()
    own = pl.ds(pl.multiple_of(me_c * mem, mem), mem)
    gains[...] = gains_all[own, :]
    low_gains[...] = gains[...].astype(bf16)
    owner = lax.broadcasted_iota(jnp.int32, (1, hw), 1) // CLASSES
    fold = (lax.broadcasted_iota(jnp.int32, (CLASSES, hw), 1) % CLASSES
            == lax.broadcasted_iota(jnp.int32, (CLASSES, hw), 0)).astype(f32)
    wide = hdot(bias_all[...], fold, ((0,), (0,)))
    at = lax.broadcasted_iota(jnp.int32, (members, hw), 0)
    bias = jnp.sum(jnp.where(at == me_c * mem + owner, wide, 0.0), axis=0, keepdims=True)
    n_rows = jnp.max(info[0:1, :]).astype(jnp.int32)
    loss_scale = 1.0 / (members * info[1:2, :])
    tiles = (n_rows + (R - 1)) // R
    fog_all[...] = jnp.zeros_like(fog_all)
    second_acc[...] = jnp.zeros_like(second_acc)
    head_acc[...] = jnp.zeros_like(head_acc)
    adapt[...] = jnp.zeros_like(adapt)
    sums[...] = jnp.zeros_like(sums)

    s_i = lax.broadcasted_iota(jnp.int32, (hw, hw), 0) // CLASSES
    s_j = lax.broadcasted_iota(jnp.int32, (hw, hw), 1) // CLASSES
    seg = (s_i == s_j).astype(bf16)

    def group(rows, pad_rows, oh, mk, enc, ms, out):
        count = len(ms)
        fin = jnp.concatenate([enc * low_gains[m:m + 1, :] for m in ms], axis=0)
        fo = dot(fin, w1[...])
        yield
        hs, us, sos, sins = [], [], [], []
        res = jnp.zeros((8, width), f32)
        res_pad = jnp.zeros((1, width), f32)
        for i, m in enumerate(ms):
            h = fo[i * R:(i + 1) * R] * halves[0, m:m + 1, :] + halves[1, m:m + 1, :]
            u = 1.0 + jnp.tanh(h)
            so = h * u
            sq = so * so
            res += fold8(sq)
            res_pad += sq[R - 1:R]
            hs.append(h)
            us.append(u)
            sos.append(so)
            sins.append((so * adapters[2, m:m + 1, :]).astype(bf16))
        sums[2] += res
        sums[4, 0:1] -= pad_rows * res_pad
        sin = jnp.concatenate(sins, axis=0)
        yield
        s2 = dot(sin, w2[...])
        yield
        h2s, u2s, brs, sts = [], [], [], []
        bres = jnp.zeros((8, width), f32)
        bres_pad = jnp.zeros((1, width), f32)
        for i, m in enumerate(ms):
            h = s2[i * R:(i + 1) * R] * halves[3, m:m + 1, :] + halves[4, m:m + 1, :]
            u = 1.0 + jnp.tanh(h)
            br = h * u
            sq = br * br
            bres += fold8(sq)
            bres_pad += sq[R - 1:R]
            h2s.append(h)
            u2s.append(u)
            brs.append(br)
            sts.append((sos[i] + br).astype(bf16))
        sums[3] += bres
        sums[4, 1:2] -= pad_rows * bres_pad
        st = jnp.concatenate(sts, axis=0)
        yield
        lo = dot(st, head[...])
        yield
        logits = bias
        for i, m in enumerate(ms):
            logits = logits + jnp.where(owner == m, lo[i * R:(i + 1) * R], 0.0)
        top = seg_max(logits)
        ex = jnp.exp(logits - top)
        exh = ex.astype(bf16)
        exl = (ex - exh.astype(f32)).astype(bf16)
        both = dot(jnp.concatenate([exh, exl], axis=0), seg)
        tot = both[:R] + both[R:]
        loss_c = (top + jnp.log(tot) - logits) * oh
        lgf = ((ex / tot * mk - oh) * loss_scale).astype(bf16).astype(f32)
        lgm = jnp.concatenate([jnp.where(owner == m, lgf, 0.0).astype(bf16) for m in ms], axis=0)
        out.append((loss_c, lgf))
        yield
        sg = dot(lgm, headt[...])
        yield
        ogs = []
        for i, m in enumerate(ms):
            pg = sg[i * R:(i + 1) * R] * (u2s[i] + brs[i] * (2.0 - u2s[i]))
            adapt[3, m] += fold8(pg * h2s[i])
            adapt[4, m] += fold8(pg)
            ogs.append((pg * halves[3, m:m + 1, :]).astype(bf16))
        og = jnp.concatenate(ogs, axis=0)
        yield
        ig = dot(og, w2t[...])
        yield
        head_acc[...] += t_dot(lgm, st)
        second_acc[...] += t_dot(sin, og)
        yield
        for i, m in enumerate(ms):
            igm = ig[i * R:(i + 1) * R]
            adapt[2, m] += fold8(igm * sos[i])
            one = sg[i * R:(i + 1) * R] + igm * adapters[2, m:m + 1, :]
            low = one * (us[i] + sos[i] * (2.0 - us[i]))
            adapt[0, m] += fold8(low * hs[i])
            adapt[1, m] += fold8(low)
            fog_all[m, rows, :] = (low * halves[0, m:m + 1, :]).astype(bf16)
        yield

    def tile(t, carry):
        rows = pl.ds(pl.multiple_of(t * R, R), R)
        enc = enc_all[rows, :]
        oh = onehots[rows, :].astype(f32)
        mk = (lax.broadcasted_iota(jnp.int32, (R, hw), 0) + t * R < n_rows).astype(f32)
        pad_rows = jnp.maximum((t + 1) * R - n_rows, 0).astype(f32)
        out = []
        per = mem // GROUPS
        runs = [group(rows, pad_rows, oh, mk, enc, tuple(range(g * per, (g + 1) * per)), out) for g in range(GROUPS)]
        for g in ORDER:
            next(runs[g])
        lane = lax.broadcasted_iota(jnp.int32, (1, hw), 1)
        loss_c, lgf = out[0]
        for g in range(1, GROUPS):
            late = lane >= g * per * CLASSES
            loss_c = jnp.where(late, out[g][0], loss_c)
            lgf = jnp.where(late, out[g][1], lgf)
        sums[0, :, :hw] += fold8(lgf)
        sums[1, :, :hw] += fold8(loss_c)
        return carry

    lax.fori_loop(0, tiles, tile, 0)
    for d in range(8):
        for c in range(4):
            lanes = slice(128 * c, 128 * c + 128)
            sbuf[d // 2, d % 2, c // 2, c % 2] = second_acc[rs * d:rs * (d + 1), lanes].astype(bf16)
    head_t = head_acc[...].T
    for d in range(8):
        hb[d // 2, d % 2] = head_t[rs * d:rs * (d + 1), :].astype(bf16)
    small[...] = jnp.zeros_like(small)
    a0, a1, a2, a3, a4 = (jnp.sum(adapt[j], axis=1) for j in range(5))
    fixed = ((a0 - 0.5 * adapters[1] * a1) / adapters[0], 0.5 * a1, a2,
             (a3 - 0.5 * adapters[4] * a4) / adapters[3], 0.5 * a4)
    for m in range(mem):
        for k in range(4):
            for j in range(5):
                small[m, 8 * k + j:8 * k + j + 1, :] = fixed[j][m:m + 1, 128 * k:128 * k + 128]
    def four(row):
        return row[:, 0:128] + row[:, 128:256] + row[:, 256:384] + row[:, 384:512]
    def rows_sum(v):
        return jnp.sum(v, axis=0, keepdims=True)
    extra = (rows_sum(sums[1, :, 0:128]), four(rows_sum(sums[2]) + sums[4, 0:1]),
             four(rows_sum(sums[3]) + sums[4, 1:2]), rows_sum(sums[0, :, 0:128]))
    for m, row in enumerate(extra):
        for k in range(4):
            small[m, 8 * k + 5:8 * k + 6, :] = row


def call_compute(members, buf, hbuf, adbuf, enc, onehots, info, gains, bias):
    rows = enc.shape[0]
    enc_w = gains.shape[1]
    mem = adbuf.shape[2]
    width = adbuf.shape[0] * 128
    hw = mem * CLASSES
    return pl.pallas_call(
        functools.partial(compute_kernel, members),
        out_shape=(
            jax.ShapeDtypeStruct((enc_w, width), bf16),
            jax.ShapeDtypeStruct((mem, rows, width), bf16),
            jax.ShapeDtypeStruct((4, 2, 2, 2, width // 8, 128), bf16),
            jax.ShapeDtypeStruct(hbuf.shape, bf16),
            jax.ShapeDtypeStruct((8, 32, 128), f32),
        ),
        in_specs=[VM] * 6 + [FAR] * 2, out_specs=(VM,) * 5,
        scratch_shapes=[
            pltpu.VMEM((width, width), bf16), pltpu.VMEM((width, width), bf16),
            pltpu.VMEM((width, hw), bf16), pltpu.VMEM((hw, width), bf16),
            pltpu.VMEM((5, mem, width), f32), pltpu.VMEM((mem, enc_w), f32),
            pltpu.VMEM((mem, enc_w), bf16),
            pltpu.VMEM((width, width), f32), pltpu.VMEM((hw, width), f32),
            pltpu.VMEM((5, mem, 8, width), f32), pltpu.VMEM((5, 8, width), f32), pltpu.VMEM((5, mem, width), f32),
            pltpu.VMEM(gains.shape, f32), pltpu.VMEM(bias.shape, f32), pltpu.SemaphoreType.DMA((2,)),
        ],
        compiler_params=pltpu.CompilerParams(vmem_limit_bytes=30 << 20),
    )(buf, hbuf, adbuf, enc, onehots, info, far(gains), far(bias))


def reduce_kernel(enc_w, width, members,
                  enc, w1_all, fog, sbuf, hb, small, info,
                  f_w_first, f_w_second, f_w_head, f_adapters, f_gains, f_head_bias,
                  f_first_row, f_first_col, f_second_row, f_second_col, f_head_row, f_head_col, f_adapter_sq, f_gain_sq, f_bias_sq,
                  o_first_grad, o_first_row, o_first_col, o_first_new,
                  o_second_grad, o_second_row, o_second_col, o_second_new,
                  o_head_grad, o_head_row, o_head_col, o_head_new,
                  o_adapter_grad, o_adapter_sq, o_adapter_new,
                  o_gain_grad, o_gain_sq, o_gain_new,
                  o_bias_grad, o_bias_sq, o_bias_new,
                  o_loss, o_rows, o_residual, o_branch,
                  w1t, own_gains, first_acc, gain_acc, far_half, own_half, far_got, own_got, far_sum, far_x, own_sum, own_pair, first_y, first_pair, first_in,
                  second_got, second_sum, second_x, second_own, second_y, second_pair, second_in,
                  hy, hsum, hz, hcol, small_y, small_sum, small_z, gall, ca, gain_part, gain_in, gain_all, gain_cols,
                  colmsg, colall, rowmsg, rowall, msg, msgall,
                  w_first, w_second, w_head, adapters, gains, head_bias,
                  first_row, first_col, second_row, second_col, head_row, head_col, adapter_sq, gain_sq, bias_sq,
                  load_sem, send_sem, recv_sem):
    z, y, x, core = place()
    me_c, me_d = 2 * x + core, 2 * z + y
    loads = [pltpu.make_async_copy(src, dst, load_sem.at[i]) for i, (src, dst) in enumerate((
        (f_gains, gains),
        (f_w_first, w_first),
        (f_w_second, w_second),
        (f_w_head, w_head),
        (f_adapters, adapters),
        (f_head_bias, head_bias),
        (f_first_row, first_row),
        (f_first_col, first_col),
        (f_second_row, second_row),
        (f_second_col, second_col),
        (f_head_row, head_row),
        (f_head_col, head_col),
        (f_adapter_sq, adapter_sq),
        (f_gain_sq, gain_sq),
        (f_bias_sq, bias_sq)))]
    for load in loads:
        load.start()
    rf, rs = w_first.shape[0], w_second.shape[0]
    mem = members // 4
    hw = mem * CLASSES
    decay = 1.0 - STEP ** (-0.8)
    everyone = []
    for kz in range(4):
        for ky in range(2):
            for kx in range(2):
                for kc in range(2):
                    if kz or ky or kx or kc:
                        everyone.append(device(z_other(z, kz), other(y, ky), other(x, kx), other(core, kc)))
    barrier, count = greet(everyone)
    send = Sender(send_sem, recv_sem)
    mate = device(z, y, x, 1 - core)
    beside = device(z, y, 1 - x, core)
    dp_peers = [(z_other(z, kz), other(y, ky)) for kz, ky in DP_PEERS]

    def received(copies):
        for cp in copies:
            cp.wait_recv()

    def quarter(side, ms):
        half = pl.ds(pl.multiple_of(256 * side, 256), 256)
        parts = jnp.concatenate([fog[m, :, half].T for m in ms], axis=0)
        g = dot(parts, enc[...])
        for i, m in enumerate(ms):
            gm = g[256 * i:256 * (i + 1)]
            gain_acc[m] += fold8(gm * w1t[half, :].astype(f32))
            scaled = gm * own_gains[m:m + 1, :]
            if m == 0:
                first_acc[...] = scaled
            else:
                first_acc[...] += scaled

    def lay_out(half):
        flipped = first_acc[...].astype(bf16).T
        for d in range(8):
            for c in range(2):
                half[d // 2, d % 2, c] = flipped[rf * d:rf * (d + 1), 128 * c:128 * c + 128]

    def to_z(ref, into, send=send):
        return [send(ref(z_other(z, k)), into(k), device(z_other(z, k), y, x, core)) for k in (1, 2, 3)]

    y_mate = device(z, 1 - y, x, core)
    w1t[...] = w1_all[...].T
    loads[0].wait()
    own_gains[...] = gains[pl.ds(pl.multiple_of(me_c * mem, mem), mem), :]
    gain_acc[...] = jnp.zeros_like(gain_acc)
    early, late = range(mem // 2), range(mem // 2, mem)
    quarter(1 - x, early)
    quarter(1 - x, late)
    lay_out(far_half)
    pl.semaphore_wait(barrier, count)
    swap_far = send(far_half.at[:, :, 1 - core], far_got, mate)
    swap_second = send(sbuf.at[:, :, :, 1 - core], second_got, mate)
    small1 = send(small.at[:, 1 - y], small_y, y_mate)
    head1 = send(hb.at[:, 1 - y], hy, y_mate)
    quarter(x, early)
    received([swap_far])
    far_sum[...] = (far_half[:, :, core].astype(f32) + far_got[...].astype(f32)).astype(bf16)
    across_far = send(far_sum, far_x, beside)
    received([swap_second])
    second_sum[...] = (sbuf[:, :, :, core].astype(f32) + second_got[...].astype(f32)).astype(bf16)
    second2 = send(second_sum.at[:, 1 - y], second_y, y_mate)
    quarter(x, late)
    lay_out(own_half)
    swap_own = send(own_half.at[:, :, 1 - core], own_got, mate)
    gain_part[...] = jnp.zeros_like(gain_part)
    for m in range(mem):
        row = jnp.sum(gain_acc[m], axis=0, keepdims=True)
        for i in range(enc_w // 128):
            gain_part[m, i:i + 1, :] = row[:, 128 * i:128 * i + 128]
    gain_deal = [send(gain_part.at[2 * pz + py], gain_in.at[i], device(pz, py, x, core)) for i, (pz, py) in enumerate(dp_peers)]
    received([small1])
    small_sum[...] = small[:, y] + small_y[...]
    small2 = to_z(lambda pz: small_sum.at[pz], lambda k: small_z.at[k - 1])
    received([head1])
    hsum[...] = (hb[:, y].astype(f32) + hy[...].astype(f32)).astype(bf16)
    head2 = to_z(lambda pz: hsum.at[pz], lambda k: hz.at[k - 1])
    for load in loads[1:]:
        load.wait()
    w1, w2 = w_first[...], w_second[...]
    wh = [w_head[mem * c:mem * (c + 1)].reshape(hw, rs).T for c in range(4)]
    own_w = (jnp.sum(w1 * w1), jnp.sum(w2 * w2), sum(jnp.sum(w * w) for w in wh))
    adapter_w = [jnp.sum(adapters[j] * adapters[j]) for j in range(5)]
    received([second2])
    second_own[...] = (second_sum[:, y].astype(f32) + second_y[...].astype(f32)).astype(bf16)
    second3 = send(second_own.at[:, 1 - x], second_x, beside)
    received([swap_own])
    own_sum[...] = own_half[:, :, core].astype(f32) + own_got[...].astype(f32)
    received([across_far])
    own_pair[...] = (own_sum[...] + far_x[...].astype(f32)).astype(bf16)
    first2 = send(own_pair.at[:, 1 - y], first_y, y_mate)
    received(gain_deal)
    mine = gain_part[me_d]
    for i in range(7):
        mine = mine + gain_in[i]
    gain_all[me_d] = mine
    gain_dp = [send(gain_all.at[me_d], gain_all.at[me_d], device(pz, py, x, core)) for pz, py in dp_peers]
    received(small2)
    gall[z, y] = ((small_sum[z] + small_z[0]) + small_z[1]) + small_z[2]
    small3 = to_z(lambda pz: gall.at[z, y], lambda k: gall.at[z, y])
    received(head2)
    hcol[me_c] = (hsum[z].astype(f32) + hz[0].astype(f32)) + (hz[1].astype(f32) + hz[2].astype(f32))
    head3 = [send(hcol.at[me_c], hcol.at[me_c], device(z, y, other(x, kx), other(core, kc))) for kx, kc in COL_PEERS]
    received([second3])
    second_pair[...] = (second_own[:, x].astype(f32) + second_x[...].astype(f32)).astype(bf16)
    second4 = to_z(lambda pz: second_pair.at[pz], lambda k: second_in.at[k - 1])
    received([first2])
    first_pair[...] = (own_pair[:, y].astype(f32) + first_y[...].astype(f32)).astype(bf16)
    first3 = to_z(lambda pz: first_pair.at[pz], lambda k: first_in.at[k - 1])
    received(small3)
    small4 = send(gall.at[:, y], gall.at[:, y], y_mate)
    received(gain_dp)
    gain_cols[me_c] = gain_all[...]
    gain_spread = [send(gain_all, gain_cols.at[me_c], device(z, y, other(x, kx), other(core, kc))) for kx, kc in COL_PEERS]
    received(second4)
    second = second_pair[z].astype(f32)
    for i in range(3):
        second = second + second_in[i].astype(f32)
    second_sq = second * second + EPS_SQUARE
    o_second_grad[...] = second
    received(head3)
    hg = [hcol[c] for c in range(4)]
    hsq = [g * g + EPS_SQUARE for g in hg]
    seg8 = (lax.broadcasted_iota(jnp.int32, (mem, hw), 1) // CLASSES
            == lax.broadcasted_iota(jnp.int32, (mem, hw), 0)).astype(f32)
    ones8 = jnp.ones((8, 128), f32)
    hrow = [decay * head_row[mem * c:mem * (c + 1), :]
            + (1.0 - decay) / CLASSES * hdot(seg8, hsq[c], ((1,), (1,))) for c in range(4)]
    hrowx = [hdot(hrow[c], seg8, ((0,), (0,))) for c in range(4)]
    def add_up(v):
        return jnp.sum(v, axis=0, keepdims=True)
    for c in range(4):
        o_head_row[mem * c:mem * (c + 1), :] = hrow[c]
        o_head_grad[mem * c:mem * (c + 1)] = hg[c].T.reshape(mem, CLASSES, rs)
        colmsg[2 + c:3 + c, :] = add_up(hsq[c])
        colmsg[8 + c:9 + c, :] = add_up(hrowx[c])
    colmsg[1:2, :] = add_up(second_sq)
    rowmsg[:, 128:128 + rs] = hdot(ones8, second_sq, ((1,), (1,)))
    received([small4])
    own8 = pl.ds(pl.multiple_of(8 * me_c, 8), 8)
    ca[me_c] = gall[:, :, own8, :]
    spread_col = []
    for kx, kc in COL_PEERS:
        px, pc = other(x, kx), other(core, kc)
        theirs = pl.ds(pl.multiple_of(8 * (2 * px + pc), 8), 8)
        spread_col.append(send(gall.at[:, :, theirs], ca.at[me_c], device(z, y, px, pc)))
    received(first3)
    first = first_pair[z].astype(f32)
    for i in range(3):
        first = first + first_in[i].astype(f32)
    o_first_grad[...] = first
    first_sq = first * first + EPS_SQUARE
    rowmsg[:, 0:rf] = hdot(ones8, first_sq, ((1,), (1,)))
    rowall[me_c] = rowmsg[...]
    colmsg[0:1, :] = add_up(first_sq)
    colall[me_d] = colmsg[...]
    r1 = [send(colmsg, colall.at[me_d], device(z_other(z, kz), other(y, ky), x, core)) for kz, ky in DP_PEERS]
    r1 += [send(rowmsg, rowall.at[me_c], device(z, y, other(x, kx), other(core, kc))) for kx, kc in COL_PEERS]
    received(spread_col)
    fold = (lax.broadcasted_iota(jnp.int32, (CLASSES, hw), 1) % CLASSES
            == lax.broadcasted_iota(jnp.int32, (CLASSES, hw), 0)).astype(f32)
    to8 = (lax.broadcasted_iota(jnp.int32, (8, members), 1) // mem
           == lax.broadcasted_iota(jnp.int32, (8, members), 0)).astype(f32)
    keep = (lax.broadcasted_iota(jnp.int32, (members, hw), 1) // CLASSES
            == lax.broadcasted_iota(jnp.int32, (members, hw), 0) % mem).astype(f32)
    def to_lanes(v):
        return hdot(to8, hdot(v, fold, ((0,), (0,))) * keep)
    def from_lanes(v):
        return hdot(fold, hdot(to8, v, ((0,), (0,))) * keep, ((1,), (1,)))
    def lane_sum(v):
        return jnp.sum(v, axis=1, keepdims=True)
    def total(v):
        return lane_sum(add_up(v))
    def step_size(weight_sq, entries):
        return RELATIVE_RATE * jnp.maximum(RATE_FLOOR, jnp.sqrt(weight_sq / entries))
    def apply(weight, update, update_sq, weight_sq, entries):
        limit = jnp.maximum(1.0, jnp.sqrt(update_sq / entries) / CLIP_LIMIT)
        return weight - step_size(weight_sq, entries) * (update / limit)
    adapter_up = []
    for j in range(5):
        grad = jnp.concatenate([ca[c, m // 2, m % 2, j:j + 1, :] for c in range(4) for m in range(mem)], axis=0)
        sq = decay * adapter_sq[j] + (1.0 - decay) * (grad * grad + EPS_SQUARE)
        o_adapter_grad[j] = grad
        o_adapter_sq[j] = sq
        adapter_up.append(grad * lax.rsqrt(sq))
    bias_lanes = jnp.concatenate([ca[c, 1, 1, 5:6, :] for c in range(4)] + [jnp.zeros((4, 128), f32)], axis=0)
    bias = from_lanes(bias_lanes)
    bias_state = decay * bias_sq[...] + (1.0 - decay) * (bias * bias + EPS_SQUARE)
    o_bias_grad[...] = bias
    o_bias_sq[...] = bias_state
    bias_up = bias * lax.rsqrt(bias_state)
    o_bias_new[...] = apply(head_bias[...], bias_up, total(bias_up * bias_up), total(head_bias[...] * head_bias[...]), members * CLASSES)
    rows_total = info[1:2, 0:1]
    o_rows[...] = rows_total
    o_loss[...] = lane_sum(sum(ca[c, 0, 0, 5:6, :] for c in range(4)))
    spread_over = rows_total * (members * width)
    o_residual[...] = jnp.sqrt(lane_sum(sum(ca[c, 0, 1, 5:6, :] for c in range(4))) / spread_over)
    o_branch[...] = jnp.sqrt(lane_sum(sum(ca[c, 1, 0, 5:6, :] for c in range(4))) / spread_over)
    hcol_old = to_lanes(head_col[...])
    for cp in r1:
        cp.wait_recv()
    col_sums = colall[0]
    for d in range(1, 8):
        col_sums = col_sums + colall[d]
    row_sums = (rowall[0] + rowall[1]) + (rowall[2] + rowall[3])
    first_r = decay * first_row[...] + (1.0 - decay) / width * row_sums[0:1, 0:rf]
    second_r = decay * second_row[...] + (1.0 - decay) / width * row_sums[0:1, 128:128 + rs]
    first_c = decay * first_col[...] + (1.0 - decay) / enc_w * col_sums[0:1]
    second_c = decay * second_col[...] + (1.0 - decay) / width * col_sums[1:2]
    head_c = decay * hcol_old[0:4] + (1.0 - decay) / width * col_sums[2:6]
    o_first_row[...] = first_r
    o_second_row[...] = second_r
    o_first_col[...] = first_c
    o_second_col[...] = second_c
    o_head_col[...] = from_lanes(jnp.concatenate([head_c, jnp.zeros((4, 128), f32)], axis=0))
    ones1 = jnp.ones((1, 128), f32)
    first_up = first * lax.rsqrt(hdot(first_r, ones1, ((0,), (0,))) * first_c)
    second_up = second * lax.rsqrt(hdot(second_r, ones1, ((0,), (0,))) * second_c)
    head_up = [hg[c] * lax.rsqrt(hrowx[c] * head_c[c:c + 1] / (col_sums[8 + c:9 + c] / width)) for c in range(4)]
    lane = lax.broadcasted_iota(jnp.int32, (1, 128), 1)
    scalars = [total(first_up * first_up), lane_sum(first_r), total(second_up * second_up), lane_sum(second_r),
               own_w[0], own_w[1], sum(total(u * u) for u in head_up), own_w[2]]
    scalars += [total(u * u) for u in adapter_up] + adapter_w
    line = jnp.zeros((1, 128), f32)
    for i, v in enumerate(scalars):
        line = jnp.where(lane == i, v, line)
    msg[...] = jnp.broadcast_to(line, (8, 128))
    msgall[z, y, x, core] = msg[...]
    r2 = []
    for target in everyone:
        r2.append(send(msg, msgall.at[z, y, x, core], target))
    received(gain_spread)
    for c in range(4):
        for i in range(enc_w // 128):
            o_gain_grad[mem * c:mem * (c + 1), 128 * i:128 * (i + 1)] = gain_cols[c, :, i, :]
    gain = o_gain_grad[...]
    gain_state = decay * gain_sq[...] + (1.0 - decay) * (gain * gain + EPS_SQUARE)
    o_gain_sq[...] = gain_state
    gain_up = gain * lax.rsqrt(gain_state)
    o_gain_new[...] = apply(gains[...], gain_up, total(gain_up * gain_up), total(gains[...] * gains[...]), members * enc_w)
    for cp in send.all[:-len(r2)]:
        cp.wait_send()
    for cp in r2:
        cp.wait_recv()
    def over_dp(cx, cc):
        out = msgall[0, 0, cx, cc, 0:1, :]
        for d in range(1, 8):
            out = out + msgall[d // 2, d % 2, cx, cc, 0:1, :]
        return out
    s_dp = over_dp(x, core)
    s_all = (over_dp(0, 0) + over_dp(0, 1)) + (over_dp(1, 0) + over_dp(1, 1))
    s_col = (msgall[z, y, 0, 0, 0:1, :] + msgall[z, y, 0, 1, 0:1, :]) + (msgall[z, y, 1, 0, 0:1, :] + msgall[z, y, 1, 1, 0:1, :])
    def item(v, i):
        return lane_sum(jnp.where(lane == i, v, 0.0))
    first_mean = item(s_dp, 1) / enc_w
    o_first_new[...] = apply(w1, first_up * jnp.sqrt(first_mean), item(s_all, 0) * first_mean, item(s_all, 4), enc_w * width)
    second_mean = item(s_dp, 3) / width
    o_second_new[...] = apply(w2, second_up * jnp.sqrt(second_mean), item(s_all, 2) * second_mean, item(s_all, 5), width * width)
    for j in range(5):
        o_adapter_new[j] = apply(adapters[j], adapter_up[j], item(s_col, 8 + j), item(s_col, 13 + j), members * width)
    for c in range(4):
        new = apply(wh[c], head_up[c], item(s_dp, 6), item(s_dp, 7), members * width * CLASSES)
        o_head_new[mem * c:mem * (c + 1)] = new.T.reshape(mem, CLASSES, rs)
    for cp in r2:
        cp.wait_send()


def call_reduce(enc, w1_all, fog, sbuf, hb, small, info, w_first, w_second, w_head, adapters, gains, head_bias,
                first_row, first_col, second_row, second_col, head_row, head_col, adapter_sq, gain_sq, bias_sq):
    members, enc_w = gains.shape
    rf, rs = w_first.shape[0], w_second.shape[0]
    width = w_first.shape[1] * 4
    mem = members // 4
    def like(a):
        return jax.ShapeDtypeStruct(a.shape, f32)
    def row(a):
        return jax.ShapeDtypeStruct((1, a.shape[0]), f32)
    one = jax.ShapeDtypeStruct((1, 1), f32)
    def buffer(*shape, dtype=f32):
        return pltpu.VMEM(shape, dtype)
    params = (w_first, w_second, w_head, adapters, gains, head_bias,
              first_row.reshape(1, -1), first_col.reshape(1, -1), second_row.reshape(1, -1), second_col.reshape(1, -1),
              head_row, head_col, adapter_sq, gain_sq, bias_sq)
    outs = pl.pallas_call(
        functools.partial(reduce_kernel, enc_w, width, members),
        out_shape=(like(w_first), row(first_row), row(first_col), like(w_first),
                   like(w_second), row(second_row), row(second_col), like(w_second),
                   like(w_head), like(head_row), like(head_col), like(w_head),
                   like(adapters), like(adapters), like(adapters),
                   like(gains), like(gains), like(gains),
                   like(head_bias), like(head_bias), like(head_bias), one, one, one, one),
        in_specs=[VM] * 7 + [FAR] * 15, out_specs=(VM,) * 25,
        scratch_shapes=[
            buffer(width, enc_w, dtype=bf16), buffer(mem, enc_w), buffer(256, enc_w), buffer(mem, 8, enc_w),
            buffer(4, 2, 2, rf, 128, dtype=bf16), buffer(4, 2, 2, rf, 128, dtype=bf16),
            buffer(4, 2, rf, 128, dtype=bf16), buffer(4, 2, rf, 128, dtype=bf16), buffer(4, 2, rf, 128, dtype=bf16),
            buffer(4, 2, rf, 128, dtype=bf16), buffer(4, 2, rf, 128), buffer(4, 2, rf, 128, dtype=bf16),
            buffer(4, rf, 128, dtype=bf16), buffer(4, rf, 128, dtype=bf16), buffer(3, rf, 128, dtype=bf16),
            buffer(4, 2, 2, rs, 128, dtype=bf16), buffer(4, 2, 2, rs, 128, dtype=bf16), buffer(4, rs, 128, dtype=bf16),
            buffer(4, 2, rs, 128, dtype=bf16), buffer(4, 2, rs, 128, dtype=bf16), buffer(4, rs, 128, dtype=bf16),
            buffer(3, rs, 128, dtype=bf16),
            buffer(4, rs, 128, dtype=bf16), buffer(4, rs, 128, dtype=bf16), buffer(3, rs, 128, dtype=bf16),
            buffer(4, rs, 128),
            buffer(4, 32, 128), buffer(4, 32, 128), buffer(3, 32, 128), buffer(4, 2, 32, 128), buffer(4, 4, 2, 8, 128),
            buffer(mem, 8, 128), buffer(7, 8, 128), buffer(8, 8, 128), buffer(4, 8, 8, 128),
            buffer(16, 128), buffer(8, 16, 128), buffer(8, 256), buffer(4, 8, 256),
            buffer(8, 128), buffer(4, 2, 2, 2, 8, 128),
            *[buffer(*p.shape) for p in params], pltpu.SemaphoreType.DMA((15,)),
            pltpu.SemaphoreType.DMA((112,)), pltpu.SemaphoreType.DMA((112,)),
        ],
        compiler_params=pltpu.CompilerParams(collective_id=1, has_side_effects=True, vmem_limit_bytes=26 << 20),
    )(enc, w1_all, fog, sbuf, hb, small.reshape(4, 2, 32, 128), info, *map(far, params))
    outs = call_store(outs)
    for i in (1, 2, 5, 6):
        outs[i] = outs[i].reshape(-1)
    for i in (21, 22, 23, 24):
        outs[i] = outs[i].reshape(())
    for i in (8, 11):
        outs[i] = outs[i].transpose(0, 2, 1)
    for i in (10, 18, 19, 20):
        outs[i] = outs[i].T
    return tuple(outs)


def store_kernel(count, *refs):
    sems = refs[2 * count]
    copies = [pltpu.make_async_copy(refs[i], refs[count + i], sems.at[i]) for i in range(count)]
    for copy in copies:
        copy.start()
    for copy in copies:
        copy.wait()


def call_store(arrays):
    count = len(arrays)
    return list(pl.pallas_call(
        functools.partial(store_kernel, count),
        out_shape=tuple(jax.ShapeDtypeStruct(a.shape, a.dtype) for a in arrays),
        in_specs=[VM] * count, out_specs=(FAR,) * count,
        scratch_shapes=[pltpu.SemaphoreType.DMA((count,))],
        compiler_params=pltpu.CompilerParams(vmem_limit_bytes=16 << 20),
    )(*arrays))


def local_blocks(bin_index, bin_fraction, row_mask, targets, w_first, w_second, w_head, adapters, gains, head_bias,
          first_row, first_col, second_row, second_col, head_row, head_col, adapter_sq, gain_sq, bias_sq):
    members = gains.shape[0]
    mem = members // 4
    w_head, head_bias, head_col, bias_sq = w_head.transpose(0, 2, 1), head_bias.T, head_col.T, bias_sq.T
    buf, hbuf, adbuf, enc, onehots, info = call_gather(
        bin_index.T, bin_fraction.T, row_mask, targets, w_first, w_second, w_head, adapters, mem)
    w1_all, fog, sbuf, hb, small = call_compute(members, buf, hbuf, adbuf, enc, onehots, info, gains, head_bias)
    return call_reduce(enc, w1_all, fog, sbuf, hb, small, info, w_first, w_second, w_head, adapters, gains, head_bias,
                       first_row, first_col, second_row, second_col, head_row, head_col, adapter_sq, gain_sq, bias_sq)


def finish(weight, update, update_sq, weight_sq, entries):
    rms_update = jnp.sqrt(update_sq / entries)
    rms_weight = jnp.sqrt(weight_sq / entries)
    update = update / jnp.maximum(1.0, rms_update / CLIP_LIMIT)
    return weight - RELATIVE_RATE * jnp.maximum(RATE_FLOOR, rms_weight) * update


def local_any(bin_index, bin_fraction, row_mask, targets, w_first, w_second, w_head, adapters, gains, head_bias,
              first_row, first_col, second_row, second_col, head_row, head_col, adapter_sq, gain_sq, bias_sq):
    count_col = lax.axis_size("col")
    count_dp = lax.axis_size("dp")
    col_place = lax.axis_index("col")
    dp_place = lax.axis_index("dp")
    members, enc_width = gains.shape
    col_width = adapters.shape[2]
    full_width = col_width * count_col
    mem = members // count_col
    rows = row_mask.shape[0]
    decay = 1.0 - STEP ** (-0.8)
    row_total = lax.psum(jnp.sum(row_mask.astype(f32)), "dp")
    hi = bin_fraction.astype(bf16).astype(f32)
    onehot = jax.nn.one_hot(targets, CLASSES, dtype=f32) * row_mask[:, None]
    table = jnp.concatenate([bin_index.astype(f32), hi, bin_fraction - hi, onehot, row_mask[:, None].astype(f32),
                             jnp.zeros((rows, 63), f32)], axis=1).astype(bf16)
    table = table.reshape(rows // count_dp, count_dp, 128)
    table = jnp.roll(table, -dp_place, axis=1).transpose(1, 0, 2).reshape(rows, 128)
    table = lax.all_to_all(table, "dp", 0, 0, tiled=True)
    mask = table[:, 64].astype(jnp.int32)
    spot = jnp.where(mask > 0, jnp.cumsum(mask) - 1, -1)
    comp = jnp.dot((jnp.arange(rows)[:, None] == spot[None, :]).astype(bf16), table, preferred_element_type=f32).astype(bf16)
    levels = jnp.arange(BINS, dtype=f32)
    where_at = (comp[:, :FEATS].astype(f32) + comp[:, FEATS:2 * FEATS].astype(f32) + comp[:, 2 * FEATS:3 * FEATS].astype(f32))
    enc = jnp.clip(where_at[:, :, None] - levels, 0.0, 1.0).reshape(rows, enc_width).astype(bf16)
    onehots = jnp.tile(comp[:, 48:48 + CLASSES], (1, mem))
    info = jnp.zeros((8, 128), f32).at[0].set(jnp.sum(mask).astype(f32)).at[1].set(row_total)

    def whole(part):
        return lax.all_gather(lax.all_gather(part.astype(bf16), "dp", axis=0, tiled=True), "col", axis=1, tiled=True)

    def blocks(full):
        return full.reshape(8, -1, 4, 128).transpose(0, 2, 1, 3)

    def unblock(part):
        return part.astype(f32).reshape(8, 4, -1, 128).transpose(0, 2, 1, 3).reshape(-1, full_width)
    buf = jnp.concatenate([blocks(whole(w_first)), blocks(whole(w_second))], axis=2).reshape(4, 2, 2, 2, -1, 128)
    heads = lax.all_gather(w_head.astype(bf16), "dp", axis=1, tiled=True)
    heads = lax.dynamic_slice_in_dim(heads, col_place * mem, mem, 0)
    hbuf = heads.transpose(1, 0, 2).reshape(4, 2, -1, mem * CLASSES)
    adbuf = lax.dynamic_slice_in_dim(lax.all_gather(adapters, "col", axis=0), col_place * mem, mem, 2)
    w1_all, fog, sbuf, hb, small = call_compute(members, buf, hbuf, adbuf, enc, onehots, info, gains, head_bias.T)
    own_gains = lax.dynamic_slice_in_dim(gains, col_place * mem, mem, 0)
    sums = jnp.einsum("rk,mrd->mkd", enc, fog, preferred_element_type=f32)
    first_part = jnp.einsum("mkd,mk->kd", sums, own_gains, precision=HIGH)
    gain_part = jnp.einsum("mkd,kd->mk", sums, w1_all.astype(f32), precision=HIGH)
    second_part = unblock(sbuf)
    head_part = hb.astype(f32).reshape(full_width, mem, CLASSES).transpose(1, 0, 2)

    def scatter(part):
        return lax.psum_scatter(lax.psum_scatter(part, "dp", scatter_dimension=0, tiled=True), "col", scatter_dimension=1, tiled=True)
    first_grad, second_grad = scatter(first_part), scatter(second_part)
    head_grad = lax.all_gather(lax.psum_scatter(head_part, "dp", scatter_dimension=1, tiled=True), "col", axis=0, tiled=True)
    adapter_part = small[:, :32].reshape(mem, 4, 8, 128)[:, :, :5].transpose(2, 0, 1, 3).reshape(5, mem, full_width)
    adapter_grad = lax.psum(lax.all_to_all(adapter_part, "col", 2, 1, tiled=True), "dp")
    bias_part = small[3, 5].reshape(mem, CLASSES)
    gain_grad, bias_grad = lax.psum(
        (lax.all_gather(gain_part, "col", axis=0, tiled=True), lax.all_gather(bias_part, "col", axis=0, tiled=True)), "dp")
    loss_sum, residual_sq, branch_sq = lax.psum(jnp.sum(small[:3, 5], axis=1), ("dp", "col"))
    first_square = first_grad * first_grad + EPS_SQUARE
    second_square = second_grad * second_grad + EPS_SQUARE
    head_square = head_grad * head_grad + EPS_SQUARE
    first_rowsum, second_rowsum = lax.psum(
        (jnp.sum(first_square, axis=1), jnp.sum(second_square, axis=1)), "col"
    )
    first_row_new = decay * first_row + (1.0 - decay) * (first_rowsum / full_width)
    second_row_new = decay * second_row + (1.0 - decay) * (second_rowsum / full_width)
    head_row_new = decay * head_row + (1.0 - decay) * jnp.mean(head_square, axis=-1)
    stats = lax.psum(
        (
            jnp.sum(first_square, axis=0),
            jnp.sum(second_square, axis=0),
            jnp.sum(head_square, axis=1),
            jnp.sum(first_row_new),
            jnp.sum(second_row_new),
            jnp.sum(head_row_new, axis=1),
        ),
        "dp",
    )
    first_colsum, second_colsum, head_colsum, first_rowtotal, second_rowtotal, head_rowtotal = stats
    first_col_new = decay * first_col + (1.0 - decay) * (first_colsum / enc_width)
    second_col_new = decay * second_col + (1.0 - decay) * (second_colsum / full_width)
    head_col_new = decay * head_col + (1.0 - decay) * (head_colsum / full_width)
    first_estimate = first_row_new[:, None] * first_col_new[None, :] / (first_rowtotal / enc_width)
    second_estimate = (
        second_row_new[:, None] * second_col_new[None, :] / (second_rowtotal / full_width)
    )
    head_estimate = (
        head_row_new[:, :, None]
        * head_col_new[:, None, :]
        / (head_rowtotal / full_width)[:, None, None]
    )
    first_update = first_grad * lax.rsqrt(first_estimate)
    second_update = second_grad * lax.rsqrt(second_estimate)
    head_update = head_grad * lax.rsqrt(head_estimate)
    adapter_sq_new = decay * adapter_sq + (1.0 - decay) * (adapter_grad * adapter_grad + EPS_SQUARE)
    adapter_update = adapter_grad * lax.rsqrt(adapter_sq_new)
    gain_sq_new = decay * gain_sq + (1.0 - decay) * (gain_grad * gain_grad + EPS_SQUARE)
    gain_update = gain_grad * lax.rsqrt(gain_sq_new)
    bias_sq_new = decay * bias_sq + (1.0 - decay) * (bias_grad * bias_grad + EPS_SQUARE)
    bias_update = bias_grad * lax.rsqrt(bias_sq_new)
    share_col = 1.0 / count_col
    share_dp = 1.0 / count_dp
    sums = lax.psum(
        (
            jnp.sum(first_update * first_update),
            jnp.sum(w_first * w_first),
            jnp.sum(second_update * second_update),
            jnp.sum(w_second * w_second),
            jnp.sum(head_update * head_update) * share_col,
            jnp.sum(w_head * w_head) * share_col,
            jnp.sum(adapter_update * adapter_update, axis=(1, 2)) * share_dp,
            jnp.sum(adapters * adapters, axis=(1, 2)) * share_dp,
        ),
        ("dp", "col"),
    )
    first_new = finish(w_first, first_update, sums[0], sums[1], enc_width * full_width)
    second_new = finish(w_second, second_update, sums[2], sums[3], full_width * full_width)
    head_new = finish(w_head, head_update, sums[4], sums[5], members * full_width * CLASSES)
    adapter_new = finish(
        adapters,
        adapter_update,
        sums[6].reshape(5, 1, 1),
        sums[7].reshape(5, 1, 1),
        members * full_width,
    )
    gain_new = finish(
        gains,
        gain_update,
        jnp.sum(gain_update * gain_update),
        jnp.sum(gains * gains),
        members * enc_width,
    )
    bias_new = finish(
        head_bias,
        bias_update,
        jnp.sum(bias_update * bias_update),
        jnp.sum(head_bias * head_bias),
        members * CLASSES,
    )
    residual_rms = jnp.sqrt(residual_sq / (row_total * members * full_width))
    branch_rms = jnp.sqrt(branch_sq / (row_total * members * full_width))
    return (
        first_grad,
        first_row_new,
        first_col_new,
        first_new,
        second_grad,
        second_row_new,
        second_col_new,
        second_new,
        head_grad,
        head_row_new,
        head_col_new,
        head_new,
        adapter_grad,
        adapter_sq_new,
        adapter_new,
        gain_grad,
        gain_sq_new,
        gain_new,
        bias_grad,
        bias_sq_new,
        bias_new,
        loss_sum,
        row_total,
        residual_rms,
        branch_rms,
    )


def local(*args):
    if lax.axis_size("dp") == 8 and lax.axis_size("col") == 4:
        return local_blocks(*args)
    return local_any(*args)


def solution(mesh):
    placed = (
        P("dp", None),
        P("dp", None),
        P("dp"),
        P("dp"),
        P("dp", "col"),
        P("dp", "col"),
        P(None, "dp", None),
        P(None, None, "col"),
        P(),
        P(),
        P("dp"),
        P("col"),
        P("dp"),
        P("col"),
        P(None, "dp"),
        P(),
        P(None, None, "col"),
        P(),
        P(),
    )
    return jax.shard_map(
        local,
        mesh=mesh,
        in_specs=placed,
        out_specs=(
            P("dp", "col"),
            P("dp"),
            P("col"),
            P("dp", "col"),
            P("dp", "col"),
            P("dp"),
            P("col"),
            P("dp", "col"),
            P(None, "dp", None),
            P(None, "dp"),
            P(),
            P(None, "dp", None),
            P(None, None, "col"),
            P(None, None, "col"),
            P(None, None, "col"),
            P(),
            P(),
            P(),
            P(),
            P(),
            P(),
            P(),
            P(),
            P(),
            P(),
        ),
        check_vma=False,
    )
```

```python
import functools
import jax, jax.numpy as jnp
from jax import lax
from jax.experimental import pallas as pl
from jax.experimental.pallas import tpu as pltpu
from jax.sharding import PartitionSpec as P

FEATS, BINS, CLASSES = 16, 48, 16
STEP = 10
EPS_SQUARE = 1e-30
CLIP_LIMIT = 1.0
RELATIVE_RATE = 0.4
RATE_FLOOR = 0.001
R = 64
GROUPS = 2
ORDER = (0, 1, 0, 1, 0, 1, 0, 1, 0, 1, 0, 1, 0, 1, 0, 1, 0, 1, 0, 1, 0, 1)
WIDE = True
f32, bf16 = jnp.float32, jnp.bfloat16

def dot(a, b):
    return jnp.dot(a, b, preferred_element_type=f32)
def dot_t(a, b):
    return lax.dot_general(a, b, (((1,), (1,)), ((), ())), preferred_element_type=f32)
def t_dot(a, b):
    return lax.dot_general(a, b, (((0,), (0,)), ((), ())), preferred_element_type=f32)

MESH = pl.DeviceIdType.MESH


def far(array):
    return pltpu.with_memory_space_constraint(array, pltpu.HBM)


HIGH = lax.Precision.HIGHEST
VM = pl.BlockSpec(memory_space=pltpu.VMEM)
FAR = pl.BlockSpec(memory_space=pltpu.HBM)


def place():
    d, c = lax.axis_index("dp"), lax.axis_index("col")
    return d // 2, d % 2, c // 2, c % 2


def z_other(z, k):
    if k == 0:
        return z
    return [None, z + 1 - 2 * (z % 2), (z + 2) % 4, 3 - z][k]


def other(b, k):
    return 1 - b if k else b


def device(z, y, x, core):
    return (2 * z + y, 2 * x + core)


PLANE = ((0, 1), (1, 0), (1, 1))
DP_PEERS = tuple((kz, ky) for kz in range(4) for ky in range(2))[1:]
COL_PEERS = ((0, 1), (1, 0), (1, 1))
NSEM1 = 28
NSEM3 = 24
CUTS = (64, 112)


class Sender:
    def __init__(self, send_sem, recv_sem):
        self.send_sem, self.recv_sem, self.count = send_sem, recv_sem, 0
        self.all = []

    def __call__(self, src, dst, target):
        i = self.count
        self.count += 1
        assert i < self.send_sem.shape[0]
        copy = pltpu.make_async_remote_copy(
            src_ref=src, dst_ref=dst, send_sem=self.send_sem.at[i], recv_sem=self.recv_sem.at[i],
            device_id=target, device_id_type=MESH)
        copy.start()
        self.all.append(copy)
        return copy

    def group(self, whole, copies):
        i = self.count
        self.count += 1
        assert i < self.send_sem.shape[0]
        for src, dst, target in copies:
            pltpu.make_async_remote_copy(
                src_ref=src, dst_ref=dst, send_sem=self.send_sem.at[i], recv_sem=self.recv_sem.at[i],
                device_id=target, device_id_type=MESH).start()
        self.all.append(Group(whole, self.send_sem.at[i], self.recv_sem.at[i]))
        return [self.all[-1]]


class Group:
    def __init__(self, whole, send_sem, recv_sem):
        self.sent = pltpu.make_async_copy(whole, whole, send_sem)
        self.landed = pltpu.make_async_copy(whole, whole, recv_sem)

    def wait_recv(self):
        self.landed.wait()

    def wait_send(self):
        self.sent.wait()


def greet(targets):
    barrier = pltpu.get_barrier_semaphore()
    for target in targets:
        pl.semaphore_signal(barrier, inc=1, device_id=target, device_id_type=MESH)
    return barrier, len(targets)


def hdot(a, b, dims=((1,), (0,))):
    return lax.dot_general(a, b, (dims, ((), ())), precision=HIGH, preferred_element_type=f32)


def gather_kernel(bin_index, bin_fraction, row_mask, targets, w_first, w_second, w_head, adapters_far,
                  buf, hbuf, adbuf, enc, onehots, info, table, recv,
                  w_first_v, w_second_v, w_head_v, adapters, bin_index_v, bin_fraction_v, row_mask_v, targets_v,
                  load_sem, send_sem, recv_sem):
    z, y, x, core = place()
    loads = [pltpu.make_async_copy(src, dst, load_sem.at[i]) for i, (src, dst) in enumerate((
        (w_first, w_first_v), (w_second, w_second_v), (w_head, w_head_v), (adapters_far, adapters),
        (bin_index, bin_index_v), (bin_fraction, bin_fraction_v), (row_mask, row_mask_v), (targets, targets_v)))]
    for load in loads:
        load.start()
    rows = bin_index.shape[1]
    rf, rs = w_first.shape[0], w_second.shape[0]
    me_c = 2 * x + core
    mem = adbuf.shape[2]
    near = [device(z_other(z, kz), other(y, ky), x, core) for kz, ky in DP_PEERS]
    near += [device(z, y, other(x, kx), other(core, kc)) for kx, kc in COL_PEERS]
    near += [device(z, 1 - y, 1 - x, core)]
    barrier, count = greet(near)
    loads[0].wait()
    loads[1].wait()
    buf[z, y, x, core, 0:rf, :] = w_first_v[...].astype(bf16)
    buf[z, y, x, core, rf:rf + rs, :] = w_second_v[...].astype(bf16)
    pl.semaphore_wait(barrier, count)
    send = Sender(send_sem, recv_sem)
    parts = [pl.ds(lo, hi - lo) for lo, hi in zip((0,) + CUTS, CUTS + (rf + rs,))]
    mine = [buf.at[z, y, x, core, part] for part in parts]
    a0, b0 = [], []
    for i in range(len(parts) - 1):
        a0.append(send.group(buf.at[0:3, 0, 0, 0, parts[i]],
                             [(mine[i], mine[i], device(z_other(z, k), y, x, core)) for k in (1, 2, 3)]))
        if i == 0:
            a1 = send.group(buf.at[0:3, 0, 0, 0, parts[-1]],
                            [(mine[-1], mine[-1], device(z, other(y, ky), other(x, kx), core)) for ky, kx in PLANE])
    for load in loads[2:]:
        load.wait()
    hbuf[z, y] = w_head_v[pl.ds(me_c * mem, mem)].reshape(mem * CLASSES, rs).T.astype(bf16)
    adbuf[me_c] = adapters[:, pl.ds(pl.multiple_of(me_c * mem, mem), mem), :]
    slot = rows // 16
    i_row = lax.broadcasted_iota(jnp.int32, (rows, rows), 0)
    i_col = lax.broadcasted_iota(jnp.int32, (rows, rows), 1)
    me_d = 2 * z + y
    p_row = lax.broadcasted_iota(jnp.int32, (rows // 2, rows), 0)
    p_col = lax.broadcasted_iota(jnp.int32, (rows // 2, rows), 1)
    wanted = (p_row % slot) * 8 + (p_row // slot + me_d) % 8
    frac = bin_fraction_v[...]
    mask = row_mask_v[...].astype(f32)
    length = jnp.sum(mask, axis=1, keepdims=True)
    high = jnp.floor(length * (1.0 / 16.0))
    c_i = lax.broadcasted_iota(jnp.int32, (CLASSES, rows), 0)
    marks = jnp.where(c_i == 0, mask, jnp.where(c_i == 1, high, jnp.where(c_i == 2, length - 16.0 * high, 0.0)))
    columns = jnp.concatenate([bin_index_v[...].astype(f32), frac, jnp.where(c_i == targets_v[...], mask, 0.0), marks], axis=0).astype(bf16)
    nothing = jnp.zeros((64, rows), bf16)
    table[...] = (dot_t((p_col == wanted).astype(bf16), jnp.concatenate([columns, nothing], axis=0))
                  + dot_t((p_col == wanted + 8 * slot).astype(bf16), jnp.concatenate([nothing, columns], axis=0))).astype(bf16)
    own_rows = pl.ds(pl.multiple_of(me_d * slot, slot), slot)
    recv[own_rows, :] = table[own_rows, :]
    t = []
    for kz, ky in DP_PEERS:
        pz, py = z_other(z, kz), other(y, ky)
        theirs = pl.ds(pl.multiple_of((2 * pz + py) * slot, slot), slot)
        t.append((table.at[theirs], recv.at[own_rows], device(pz, py, x, core)))
    t = send.group(recv.at[0:7 * slot], t)
    h = send.group(hbuf.at[0:3, 0], [(hbuf.at[z, y], hbuf.at[z, y], device(z_other(z, k), y, x, core)) for k in (1, 2, 3)])
    ad = []
    for kx, kc in COL_PEERS:
        px, pc = other(x, kx), other(core, kc)
        theirs = pl.ds(pl.multiple_of((2 * px + pc) * mem, mem), mem)
        ad.append((adapters.at[:, theirs, :], adbuf.at[me_c], device(z, y, px, pc)))
    ad = send.group(adbuf.at[0:3], ad)
    mate = device(z, y, x, 1 - core)
    last = []
    for i, part in enumerate(parts[:-1]):
        for cp in a0[i]:
            cp.wait_recv()
        column = buf.at[:, y, x, core, part]
        b0.append([send(column, column, device(z, other(y, ky), other(x, kx), core)) for ky, kx in PLANE])
        if i == 0:
            for cp in a1:
                cp.wait_recv()
            plane = buf.at[z, :, :, core, parts[-1]]
            b1 = [send(plane, plane, device(z_other(z, k), y, x, core)) for k in (1, 2, 3)]
            last.append(send(plane, plane, mate))
        last.append(send(column, column, mate))
    for cp in h:
        cp.wait_recv()
    h2 = send(hbuf.at[:, y], hbuf.at[:, y], device(z, 1 - y, x, core))
    for cp in t:
        cp.wait_recv()
    lane8 = lax.broadcasted_iota(jnp.int32, (8, 128), 1)
    got = recv[...]
    mask_row = jnp.concatenate([dot_t((lane8 == 48).astype(bf16), got), dot_t((lane8 == 112).astype(bf16), got)], axis=1)
    pos = dot(mask_row.astype(bf16), (i_row < i_col).astype(bf16))
    spot = jnp.where(mask_row > 0.5, pos, -1.0)[0:1]
    perm = (i_row.astype(f32) == spot).astype(bf16)
    lane = lax.broadcasted_iota(jnp.int32, (1, 128), 1)
    low_half = (lane < 64).astype(bf16)
    comp = (dot(perm[:, :rows // 2], got * low_half) + dot(perm[:, rows // 2:], got * (1.0 - low_half))).astype(bf16)
    enc_w, hw = enc.shape[1], onehots.shape[1]
    kk = lax.broadcasted_iota(jnp.int32, (128, enc_w), 1)
    ll = lax.broadcasted_iota(jnp.int32, (128, enc_w), 0)
    ff = ll & (FEATS - 1)
    spread = (((ll & 63) < 2 * FEATS) & (kk >= ff * BINS) & (kk < (ff + 1) * BINS)).astype(bf16)
    lev = (lax.broadcasted_iota(jnp.int32, (1, enc_w), 1) % BINS).astype(f32)
    enc[...] = jnp.clip(dot(comp, spread) - lev, 0.0, 1.0).astype(bf16)
    l2 = lax.broadcasted_iota(jnp.int32, (128, hw), 0)
    c2 = lax.broadcasted_iota(jnp.int32, (128, hw), 1)
    onehots[...] = dot(comp, ((l2 & 63) == 2 * FEATS + (c2 & (CLASSES - 1))).astype(bf16)).astype(bf16)
    per_row = jnp.where((lane & 63) == 49, 16.0, jnp.where((lane & 63) == 50, 1.0, 0.0))
    total = jnp.sum(jnp.sum(got.astype(f32), axis=0, keepdims=True) * per_row, axis=1, keepdims=True) / (2 * slot)
    info[0:1, :] = jnp.zeros((1, 128), f32) + jnp.sum(mask_row[0:1], axis=1, keepdims=True)
    info[1:2, :] = jnp.zeros((1, 128), f32) + total
    info[2:8, :] = jnp.zeros((6, 128), f32)
    for i, part in enumerate(parts[:-1]):
        for cp, (ky, kx) in zip(b0[i], PLANE):
            cp.wait_recv()
            column = buf.at[:, other(y, ky), other(x, kx), core, part]
            last.append(send(column, column, mate))
        if i == 0:
            for cp, k in zip(b1, (1, 2, 3)):
                cp.wait_recv()
                plane = buf.at[z_other(z, k), :, :, core, parts[-1]]
                last.append(send(plane, plane, mate))
    for cp in last + ad + [h2]:
        cp.wait_recv()
    for cp in send.all:
        cp.wait_send()


def call_gather(bin_index, bin_fraction, row_mask, targets, w_first, w_second, w_head, adapters, mem):
    rows = bin_index.shape[1]
    both = w_first.shape[0] + w_second.shape[0]
    return pl.pallas_call(
        gather_kernel,
        out_shape=(
            jax.ShapeDtypeStruct((4, 2, 2, 2, both, 128), bf16),
            jax.ShapeDtypeStruct((4, 2, w_head.shape[2], 128), bf16),
            jax.ShapeDtypeStruct((4, 5, mem, 128), f32),
            jax.ShapeDtypeStruct((rows, FEATS * BINS), bf16),
            jax.ShapeDtypeStruct((rows, mem * CLASSES), bf16),
            jax.ShapeDtypeStruct((8, 128), f32),
        ),
        in_specs=[FAR] * 8, out_specs=(VM,) * 6,
        scratch_shapes=[pltpu.VMEM((rows // 2, 128), bf16), pltpu.VMEM((rows // 2, 128), bf16),
                        pltpu.VMEM(w_first.shape, f32), pltpu.VMEM(w_second.shape, f32),
                        pltpu.VMEM(w_head.shape, f32), pltpu.VMEM(adapters.shape, f32),
                        pltpu.VMEM(bin_index.shape, jnp.int32), pltpu.VMEM(bin_fraction.shape, f32),
                        pltpu.VMEM((1, rows), jnp.int32), pltpu.VMEM((1, rows), jnp.int32),
                        pltpu.SemaphoreType.DMA((8,)),
                        pltpu.SemaphoreType.DMA((NSEM1,)), pltpu.SemaphoreType.DMA((NSEM1,))],
        compiler_params=pltpu.CompilerParams(collective_id=0, has_side_effects=True, vmem_limit_bytes=16 << 20),
    )(*map(far, (bin_index, bin_fraction, row_mask.reshape(1, -1), targets.reshape(1, -1),
                 w_first, w_second, w_head, adapters)))


def seg_max(x):
    lane = lax.broadcasted_iota(jnp.int32, x.shape, 1)
    n = x.shape[1]
    for s in (1, 2, 4, 8):
        up = pltpu.roll(x, n - s, 1)
        dn = pltpu.roll(x, s, 1)
        x = jnp.maximum(x, jnp.where((lane & s) == 0, up, dn))
    return x


def fold8(v):
    return sum(v[8 * i:8 * i + 8] for i in range(v.shape[0] // 8))


def compute_kernel(members, buf, hbuf, adbuf, enc_all, onehots, info, gains_far, bias_far,
                   w1, fog_all, sbuf, hb, small,
                   w2, w2t, head, headt, adapters, gains, low_gains,
                   second_acc, head_acc, adapt, sums, halves, gains_all, bias_all, load_sem):
    rows_all = enc_all.shape[0]
    enc_w, width = w1.shape
    mem = adbuf.shape[2]
    hw = mem * CLASSES
    rf, rs = enc_w // 8, width // 8
    me_c = lax.axis_index("col")
    loads = [pltpu.make_async_copy(gains_far, gains_all, load_sem.at[0]),
             pltpu.make_async_copy(bias_far, bias_all, load_sem.at[1])]
    for load in loads:
        load.start()
    for d in range(8):
        for c in range(4):
            lanes = slice(128 * c, 128 * c + 128)
            w1[rf * d:rf * (d + 1), lanes] = buf[d // 2, d % 2, c // 2, c % 2, 0:rf, :]
            w2[rs * d:rs * (d + 1), lanes] = buf[d // 2, d % 2, c // 2, c % 2, rf:rf + rs, :]
        head[rs * d:rs * (d + 1), :] = hbuf[d // 2, d % 2]
    for c in range(4):
        adapters[:, :, 128 * c:128 * c + 128] = adbuf[c]
    for j in (0, 1, 3, 4):
        halves[j] = 0.5 * adapters[j]
    w2t[...] = w2[...].T
    headt[...] = head[...].T
    for load in loads:
        load.wait()
    own = pl.ds(pl.multiple_of(me_c * mem, mem), mem)
    gains[...] = gains_all[own, :]
    low_gains[...] = gains[...].astype(bf16)
    owner = lax.broadcasted_iota(jnp.int32, (1, hw), 1) // CLASSES
    fold = (lax.broadcasted_iota(jnp.int32, (CLASSES, hw), 1) % CLASSES
            == lax.broadcasted_iota(jnp.int32, (CLASSES, hw), 0)).astype(f32)
    wide = hdot(bias_all[...], fold, ((0,), (0,)))
    at = lax.broadcasted_iota(jnp.int32, (members, hw), 0)
    bias = jnp.sum(jnp.where(at == me_c * mem + owner, wide, 0.0), axis=0, keepdims=True)
    n_rows = jnp.max(info[0:1, :]).astype(jnp.int32)
    loss_scale = 1.0 / (members * info[1:2, :])
    second_acc[...] = jnp.zeros_like(second_acc)
    head_acc[...] = jnp.zeros_like(head_acc)
    adapt[...] = jnp.zeros_like(adapt)
    sums[...] = jnp.zeros_like(sums)

    s_i = lax.broadcasted_iota(jnp.int32, (hw, hw), 0) // CLASSES
    s_j = lax.broadcasted_iota(jnp.int32, (hw, hw), 1) // CLASSES
    seg = (s_i == s_j).astype(bf16)

    def group(R, rows, pad_rows, oh, mk, enc, ms, out, grads):
        count = len(ms)
        fin = jnp.concatenate([enc * low_gains[m:m + 1, :] for m in ms], axis=0)
        fo = dot(fin, w1[...])
        yield
        hs, us, sos, sins = [], [], [], []
        res = jnp.zeros((8, width), f32)
        res_pad = jnp.zeros((1, width), f32)
        for i, m in enumerate(ms):
            h = fo[i * R:(i + 1) * R] * halves[0, m:m + 1, :] + halves[1, m:m + 1, :]
            u = 1.0 + jnp.tanh(h)
            so = h * u
            sq = so * so
            res += fold8(sq)
            res_pad += sq[R - 1:R]
            hs.append(h)
            us.append(u)
            sos.append(so)
            sins.append((so * adapters[2, m:m + 1, :]).astype(bf16))
        sums[2] += res
        sums[4, 0:1] -= pad_rows * res_pad
        sin = jnp.concatenate(sins, axis=0)
        yield
        s2 = dot(sin, w2[...])
        yield
        h2s, u2s, brs, sts = [], [], [], []
        bres = jnp.zeros((8, width), f32)
        bres_pad = jnp.zeros((1, width), f32)
        for i, m in enumerate(ms):
            h = s2[i * R:(i + 1) * R] * halves[3, m:m + 1, :] + halves[4, m:m + 1, :]
            u = 1.0 + jnp.tanh(h)
            br = h * u
            sq = br * br
            bres += fold8(sq)
            bres_pad += sq[R - 1:R]
            h2s.append(h)
            u2s.append(u)
            brs.append(br)
            sts.append((sos[i] + br).astype(bf16))
        sums[3] += bres
        sums[4, 1:2] -= pad_rows * bres_pad
        st = jnp.concatenate(sts, axis=0)
        yield
        lo = dot(st, head[...])
        yield
        logits = bias
        for i, m in enumerate(ms):
            logits = logits + jnp.where(owner == m, lo[i * R:(i + 1) * R], 0.0)
        top = seg_max(logits)
        ex = jnp.exp(logits - top)
        exh = ex.astype(bf16)
        exl = (ex - exh.astype(f32)).astype(bf16)
        both = dot(jnp.concatenate([exh, exl], axis=0), seg)
        tot = both[:R] + both[R:]
        loss_c = (top + jnp.log(tot) - logits) * oh
        lgf = ((ex / tot * mk - oh) * loss_scale).astype(bf16).astype(f32)
        lgm = jnp.concatenate([jnp.where(owner == m, lgf, 0.0).astype(bf16) for m in ms], axis=0)
        out.append((loss_c, lgf))
        yield
        sg = dot(lgm, headt[...])
        yield
        ogs = []
        for i, m in enumerate(ms):
            pg = sg[i * R:(i + 1) * R] * (u2s[i] + brs[i] * (2.0 - u2s[i]))
            adapt[3, m] += fold8(pg * h2s[i])
            adapt[4, m] += fold8(pg)
            ogs.append((pg * halves[3, m:m + 1, :]).astype(bf16))
        og = jnp.concatenate(ogs, axis=0)
        yield
        ig = dot(og, w2t[...])
        yield
        grads.append((lgm, st, sin, og))
        if len(grads) == GROUPS:
            lgms, sts_all, sins_all, ogs_all = (jnp.concatenate(v, axis=0) for v in zip(*grads))
            head_acc[...] += t_dot(lgms, sts_all)
            second_acc[...] += t_dot(sins_all, ogs_all)
        yield
        for i, m in enumerate(ms):
            igm = ig[i * R:(i + 1) * R]
            adapt[2, m] += fold8(igm * sos[i])
            one = sg[i * R:(i + 1) * R] + igm * adapters[2, m:m + 1, :]
            low = one * (us[i] + sos[i] * (2.0 - us[i]))
            adapt[0, m] += fold8(low * hs[i])
            adapt[1, m] += fold8(low)
            fog_all[m, rows, :] = (low * halves[0, m:m + 1, :]).astype(bf16)
        yield

    def tile(R, start):
        rows = pl.ds(pl.multiple_of(start, 64), R)
        enc = enc_all[rows, :]
        oh = onehots[rows, :].astype(f32)
        mk = (lax.broadcasted_iota(jnp.int32, (R, hw), 0) + start < n_rows).astype(f32)
        pad_rows = jnp.maximum(start + R - n_rows, 0).astype(f32)
        out, grads = [], []
        per = mem // GROUPS
        runs = [group(R, rows, pad_rows, oh, mk, enc, tuple(range(g * per, (g + 1) * per)), out, grads) for g in range(GROUPS)]
        for g in ORDER:
            next(runs[g])
        lane = lax.broadcasted_iota(jnp.int32, (1, hw), 1)
        loss_c, lgf = out[0]
        for g in range(1, GROUPS):
            late = lane >= g * per * CLASSES
            loss_c = jnp.where(late, out[g][0], loss_c)
            lgf = jnp.where(late, out[g][1], lgf)
        sums[0, :, :hw] += fold8(lgf)
        sums[1, :, :hw] += fold8(loss_c)

    def wide_tile(t, carry):
        tile(2 * R, t * 2 * R)
        return carry

    def narrow_tile(t, carry):
        tile(R, t * R)
        return carry

    def clear(t, carry):
        for m in range(mem):
            fog_all[m, pl.ds(pl.multiple_of(t * R, R), R), :] = jnp.zeros((R, width), bf16)
        return carry
    wide = (n_rows + (R - 1)) // (2 * R) if WIDE else 0
    lax.fori_loop(0, wide, wide_tile, 0)
    tiles = jnp.maximum((n_rows + (R - 1)) // R, 2 * wide)
    lax.fori_loop(2 * wide, tiles, narrow_tile, 0)
    lax.fori_loop(tiles, rows_all // R, clear, 0)
    for d in range(8):
        for c in range(4):
            lanes = slice(128 * c, 128 * c + 128)
            sbuf[d // 2, d % 2, c // 2, c % 2] = second_acc[rs * d:rs * (d + 1), lanes].astype(bf16)
    head_t = head_acc[...].T
    for d in range(8):
        hb[d // 2, d % 2] = head_t[rs * d:rs * (d + 1), :].astype(bf16)
    small[...] = jnp.zeros_like(small)
    a0, a1, a2, a3, a4 = (jnp.sum(adapt[j], axis=1) for j in range(5))
    fixed = ((a0 - 0.5 * adapters[1] * a1) / adapters[0], 0.5 * a1, a2,
             (a3 - 0.5 * adapters[4] * a4) / adapters[3], 0.5 * a4)
    for m in range(mem):
        for k in range(4):
            for j in range(5):
                small[m, 8 * k + j:8 * k + j + 1, :] = fixed[j][m:m + 1, 128 * k:128 * k + 128]
    def four(row):
        return row[:, 0:128] + row[:, 128:256] + row[:, 256:384] + row[:, 384:512]
    def rows_sum(v):
        return jnp.sum(v, axis=0, keepdims=True)
    extra = (rows_sum(sums[1, :, 0:128]), four(rows_sum(sums[2]) + sums[4, 0:1]),
             four(rows_sum(sums[3]) + sums[4, 1:2]), rows_sum(sums[0, :, 0:128]))
    for m, row in enumerate(extra):
        for k in range(4):
            small[m, 8 * k + 5:8 * k + 6, :] = row


def call_compute(members, buf, hbuf, adbuf, enc, onehots, info, gains, bias):
    rows = enc.shape[0]
    enc_w = gains.shape[1]
    mem = adbuf.shape[2]
    width = adbuf.shape[0] * 128
    hw = mem * CLASSES
    return pl.pallas_call(
        functools.partial(compute_kernel, members),
        out_shape=(
            jax.ShapeDtypeStruct((enc_w, width), bf16),
            jax.ShapeDtypeStruct((mem, rows, width), bf16),
            jax.ShapeDtypeStruct((4, 2, 2, 2, width // 8, 128), bf16),
            jax.ShapeDtypeStruct(hbuf.shape, bf16),
            jax.ShapeDtypeStruct((8, 32, 128), f32),
        ),
        in_specs=[VM] * 6 + [FAR] * 2, out_specs=(VM,) * 5,
        scratch_shapes=[
            pltpu.VMEM((width, width), bf16), pltpu.VMEM((width, width), bf16),
            pltpu.VMEM((width, hw), bf16), pltpu.VMEM((hw, width), bf16),
            pltpu.VMEM((5, mem, width), f32), pltpu.VMEM((mem, enc_w), f32),
            pltpu.VMEM((mem, enc_w), bf16),
            pltpu.VMEM((width, width), f32), pltpu.VMEM((hw, width), f32),
            pltpu.VMEM((5, mem, 8, width), f32), pltpu.VMEM((5, 8, width), f32), pltpu.VMEM((5, mem, width), f32),
            pltpu.VMEM(gains.shape, f32), pltpu.VMEM(bias.shape, f32), pltpu.SemaphoreType.DMA((2,)),
        ],
        compiler_params=pltpu.CompilerParams(vmem_limit_bytes=36 << 20),
    )(buf, hbuf, adbuf, enc, onehots, info, far(gains), far(bias))


def reduce_kernel(enc_w, width, members,
                  enc, w1_all, fog, sbuf, hb, small, info,
                  f_w_first, f_w_second, f_w_head, f_adapters, f_gains, f_head_bias,
                  f_first_row, f_first_col, f_second_row, f_second_col, f_head_row, f_head_col, f_adapter_sq, f_gain_sq, f_bias_sq,
                  o_first_grad, o_first_row, o_first_col, o_first_new,
                  o_second_grad, o_second_row, o_second_col, o_second_new,
                  o_head_grad, o_head_row, o_head_col, o_head_new,
                  o_adapter_grad, o_adapter_sq, o_adapter_new,
                  o_gain_grad, o_gain_sq, o_gain_new,
                  o_bias_grad, o_bias_sq, o_bias_new,
                  o_scalars,
                  w1t, own_gains, first_acc, gain_acc, far_half, own_half, far_got, own_got, far_sum, far_x, own_sum, own_pair, first_y, first_pair, first_in,
                  second_got, second_sum, second_x, second_own, second_y, second_pair, second_in,
                  hy, hsum, hz, hcol, small_y, small_sum, small_z, gall, ca, gain_part, gain_in, gain_all, gain_cols,
                  colmsg, colall, rowmsg, rowall, msg, msgall, early_line,
                  w_first, w_second, w_head, adapters, gains, head_bias,
                  first_row, first_col, second_row, second_col, head_row, head_col, adapter_sq, gain_sq, bias_sq,
                  load_sem, send_sem, recv_sem):
    z, y, x, core = place()
    me_c, me_d = 2 * x + core, 2 * z + y
    loads = [pltpu.make_async_copy(src, dst, load_sem.at[i]) for i, (src, dst) in enumerate((
        (f_gains, gains),
        (f_w_first, w_first),
        (f_w_second, w_second),
        (f_w_head, w_head),
        (f_adapters, adapters),
        (f_head_bias, head_bias),
        (f_first_row, first_row),
        (f_first_col, first_col),
        (f_second_row, second_row),
        (f_second_col, second_col),
        (f_head_row, head_row),
        (f_head_col, head_col),
        (f_adapter_sq, adapter_sq),
        (f_gain_sq, gain_sq),
        (f_bias_sq, bias_sq)))]
    for load in loads:
        load.start()
    rf, rs = w_first.shape[0], w_second.shape[0]
    mem = members // 4
    hw = mem * CLASSES
    decay = 1.0 - STEP ** (-0.8)
    everyone = []
    for kz in range(4):
        for ky in range(2):
            for kx in range(2):
                for kc in range(2):
                    if kz or ky or kx or kc:
                        everyone.append(device(z_other(z, kz), other(y, ky), other(x, kx), other(core, kc)))
    barrier, count = greet(everyone)
    send = Sender(send_sem, recv_sem)
    mate = device(z, y, x, 1 - core)
    beside = device(z, y, 1 - x, core)
    dp_peers = [(z_other(z, kz), other(y, ky)) for kz, ky in DP_PEERS]

    def received(copies):
        for cp in copies:
            cp.wait_recv()

    def quarter(side, ms):
        half = pl.ds(pl.multiple_of(256 * side, 256), 256)
        parts = jnp.concatenate([fog[m, :, half].T for m in ms], axis=0)
        g = dot(parts, enc[...])
        for i, m in enumerate(ms):
            gm = g[256 * i:256 * (i + 1)]
            gain_acc[m] += fold8(gm * w1t[half, :].astype(f32))
            scaled = gm * own_gains[m:m + 1, :]
            if m == 0:
                first_acc[...] = scaled
            else:
                first_acc[...] += scaled

    def lay_out(half):
        flipped = first_acc[...].astype(bf16).T
        for d in range(8):
            for c in range(2):
                half[d // 2, d % 2, c] = flipped[rf * d:rf * (d + 1), 128 * c:128 * c + 128]

    def to_z(whole, ref, into):
        return send.group(whole, [(ref(z_other(z, k)), into(k), device(z_other(z, k), y, x, core)) for k in (1, 2, 3)])

    def to_dp(whole, ref, into):
        return send.group(whole, [(ref(2 * pz + py), into(i), device(pz, py, x, core)) for i, (pz, py) in enumerate(dp_peers)])

    def to_col(whole, ref, into):
        return send.group(whole, [(ref(2 * other(x, kx) + other(core, kc)), into, device(z, y, other(x, kx), other(core, kc)))
                                  for kx, kc in COL_PEERS])

    y_mate = device(z, 1 - y, x, core)
    w1t[...] = w1_all[...].T
    loads[0].wait()
    own_gains[...] = gains[pl.ds(pl.multiple_of(me_c * mem, mem), mem), :]
    gain_acc[...] = jnp.zeros_like(gain_acc)
    early, late = range(mem // 2), range(mem // 2, mem)
    quarter(1 - x, early)
    quarter(1 - x, late)
    lay_out(far_half)
    pl.semaphore_wait(barrier, count)
    swap_far = send(far_half.at[:, :, 1 - core], far_got, mate)
    swap_second = send(sbuf.at[:, :, :, 1 - core], second_got, mate)
    small1 = send(small.at[:, 1 - y], small_y, y_mate)
    head1 = send(hb.at[:, 1 - y], hy, y_mate)
    received([swap_far])
    far_sum[...] = (far_half[:, :, core].astype(f32) + far_got[...].astype(f32)).astype(bf16)
    across_far = send(far_sum, far_x, beside)
    quarter(x, early)
    received([swap_second])
    second_sum[...] = (sbuf[:, :, :, core].astype(f32) + second_got[...].astype(f32)).astype(bf16)
    second2 = send(second_sum.at[:, 1 - y], second_y, y_mate)
    quarter(x, late)
    lay_out(own_half)
    swap_own = send(own_half.at[:, :, 1 - core], own_got, mate)
    gain_part[...] = jnp.zeros_like(gain_part)
    for m in range(mem):
        row = jnp.sum(gain_acc[m], axis=0, keepdims=True)
        for i in range(enc_w // 128):
            gain_part[m, i:i + 1, :] = row[:, 128 * i:128 * i + 128]
    gain_deal = to_dp(gain_in, lambda d: gain_part.at[d], lambda i: gain_in.at[i])
    received([small1])
    small_sum[...] = small[:, y] + small_y[...]
    small2 = to_z(small_z, lambda pz: small_sum.at[pz], lambda k: small_z.at[k - 1])
    received([head1])
    hsum[...] = (hb[:, y].astype(f32) + hy[...].astype(f32)).astype(bf16)
    head2 = to_z(hz, lambda pz: hsum.at[pz], lambda k: hz.at[k - 1])
    for load in loads[1:]:
        load.wait()
    w1, w2 = w_first[...], w_second[...]
    wh = [w_head[mem * c:mem * (c + 1)].reshape(hw, rs).T for c in range(4)]
    own_w = (jnp.sum(w1 * w1), jnp.sum(w2 * w2), sum(jnp.sum(w * w) for w in wh))
    adapter_w = [jnp.sum(adapters[j] * adapters[j]) for j in range(5)]
    received([second2])
    second_own[...] = (second_sum[:, y].astype(f32) + second_y[...].astype(f32)).astype(bf16)
    second3 = send(second_own.at[:, 1 - x], second_x, beside)
    received([swap_own])
    own_sum[...] = own_half[:, :, core].astype(f32) + own_got[...].astype(f32)
    received([across_far])
    own_pair[...] = (own_sum[...] + far_x[...].astype(f32)).astype(bf16)
    first2 = send(own_pair.at[:, 1 - y], first_y, y_mate)
    received(gain_deal)
    mine = gain_part[me_d]
    for i in range(7):
        mine = mine + gain_in[i]
    gain_all[me_d] = mine
    gain_dp = to_dp(gain_in, lambda d: gain_all.at[me_d], lambda i: gain_all.at[me_d])
    received(small2)
    gall[z, y] = ((small_sum[z] + small_z[0]) + small_z[1]) + small_z[2]
    small3 = to_z(gall.at[0:3, 0], lambda pz: gall.at[z, y], lambda k: gall.at[z, y])
    received(head2)
    hcol[me_c] = (hsum[z].astype(f32) + hz[0].astype(f32)) + (hz[1].astype(f32) + hz[2].astype(f32))
    head3 = to_col(hcol.at[0:3], lambda c: hcol.at[me_c], hcol.at[me_c])
    received([second3])
    second_pair[...] = (second_own[:, x].astype(f32) + second_x[...].astype(f32)).astype(bf16)
    second4 = to_z(second_in, lambda pz: second_pair.at[pz], lambda k: second_in.at[k - 1])
    received([first2])
    first_pair[...] = (own_pair[:, y].astype(f32) + first_y[...].astype(f32)).astype(bf16)
    first3 = to_z(first_in, lambda pz: first_pair.at[pz], lambda k: first_in.at[k - 1])
    received(small3)
    small4 = send(gall.at[:, y], gall.at[:, y], y_mate)
    received(gain_dp)
    gain_cols[me_c] = gain_all[...]
    gain_spread = to_col(gain_cols.at[0:3], lambda c: gain_all, gain_cols.at[me_c])
    received(second4)
    second = second_pair[z].astype(f32)
    for i in range(3):
        second = second + second_in[i].astype(f32)
    second_sq = second * second + EPS_SQUARE
    o_second_grad[...] = second
    received(head3)
    hg = [hcol[c] for c in range(4)]
    hsq = [g * g + EPS_SQUARE for g in hg]
    seg8 = (lax.broadcasted_iota(jnp.int32, (mem, hw), 1) // CLASSES
            == lax.broadcasted_iota(jnp.int32, (mem, hw), 0)).astype(f32)
    ones8 = jnp.ones((8, 128), f32)
    hrow = [decay * head_row[mem * c:mem * (c + 1), :]
            + (1.0 - decay) / CLASSES * hdot(seg8, hsq[c], ((1,), (1,))) for c in range(4)]
    hrowx = [hdot(hrow[c], seg8, ((0,), (0,))) for c in range(4)]
    def add_up(v):
        return jnp.sum(v, axis=0, keepdims=True)
    for c in range(4):
        o_head_row[mem * c:mem * (c + 1), :] = hrow[c]
        o_head_grad[mem * c:mem * (c + 1)] = hg[c].T.reshape(mem, CLASSES, rs)
        colmsg[2 + c:3 + c, :] = add_up(hsq[c])
        colmsg[8 + c:9 + c, :] = add_up(hrowx[c])
    colmsg[1:2, :] = add_up(second_sq)
    rowmsg[:, 128:128 + rs] = hdot(ones8, second_sq, ((1,), (1,)))
    received([small4])
    own8 = pl.ds(pl.multiple_of(8 * me_c, 8), 8)
    ca[me_c] = gall[:, :, own8, :]
    spread_col = to_col(ca.at[0:3], lambda c: gall.at[:, :, pl.ds(pl.multiple_of(8 * c, 8), 8)], ca.at[me_c])
    received(first3)
    first = first_pair[z].astype(f32)
    for i in range(3):
        first = first + first_in[i].astype(f32)
    o_first_grad[...] = first
    first_sq = first * first + EPS_SQUARE
    rowmsg[:, 0:rf] = hdot(ones8, first_sq, ((1,), (1,)))
    rowall[me_c] = rowmsg[...]
    colmsg[0:1, :] = add_up(first_sq)
    colall[me_d] = colmsg[...]
    r1 = to_dp(colall.at[0:7], lambda d: colmsg, lambda i: colall.at[me_d])
    r1 += to_col(rowall.at[0:3], lambda c: rowmsg, rowall.at[me_c])
    received(spread_col)
    fold = (lax.broadcasted_iota(jnp.int32, (CLASSES, hw), 1) % CLASSES
            == lax.broadcasted_iota(jnp.int32, (CLASSES, hw), 0)).astype(f32)
    to8 = (lax.broadcasted_iota(jnp.int32, (8, members), 1) // mem
           == lax.broadcasted_iota(jnp.int32, (8, members), 0)).astype(f32)
    keep = (lax.broadcasted_iota(jnp.int32, (members, hw), 1) // CLASSES
            == lax.broadcasted_iota(jnp.int32, (members, hw), 0) % mem).astype(f32)
    def to_lanes(v):
        return hdot(to8, hdot(v, fold, ((0,), (0,))) * keep)
    def from_lanes(v):
        return hdot(fold, hdot(to8, v, ((0,), (0,))) * keep, ((1,), (1,)))
    def lane_sum(v):
        return jnp.sum(v, axis=1, keepdims=True)
    def total(v):
        return lane_sum(add_up(v))
    def step_size(weight_sq, entries):
        return RELATIVE_RATE * jnp.maximum(RATE_FLOOR, jnp.sqrt(weight_sq / entries))
    def apply(weight, update, update_sq, weight_sq, entries):
        limit = jnp.maximum(1.0, jnp.sqrt(update_sq / entries) / CLIP_LIMIT)
        return weight - step_size(weight_sq, entries) * (update / limit)
    adapter_up = []
    for j in range(5):
        grad = jnp.concatenate([ca[c, m // 2, m % 2, j:j + 1, :] for c in range(4) for m in range(mem)], axis=0)
        sq = decay * adapter_sq[j] + (1.0 - decay) * (grad * grad + EPS_SQUARE)
        o_adapter_grad[j] = grad
        o_adapter_sq[j] = sq
        adapter_up.append(grad * lax.rsqrt(sq))
    bias_lanes = jnp.concatenate([ca[c, 1, 1, 5:6, :] for c in range(4)] + [jnp.zeros((4, 128), f32)], axis=0)
    bias = from_lanes(bias_lanes)
    bias_state = decay * bias_sq[...] + (1.0 - decay) * (bias * bias + EPS_SQUARE)
    o_bias_grad[...] = bias
    o_bias_sq[...] = bias_state
    bias_up = bias * lax.rsqrt(bias_state)
    o_bias_new[...] = apply(head_bias[...], bias_up, total(bias_up * bias_up), total(head_bias[...] * head_bias[...]), members * CLASSES)
    rows_total = info[1:2, 0:1]
    loss_total = lane_sum(sum(ca[c, 0, 0, 5:6, :] for c in range(4)))
    spread_over = rows_total * (members * width)
    residual = jnp.sqrt(lane_sum(sum(ca[c, 0, 1, 5:6, :] for c in range(4))) / spread_over)
    branch_size = jnp.sqrt(lane_sum(sum(ca[c, 1, 0, 5:6, :] for c in range(4))) / spread_over)
    spot = lax.broadcasted_iota(jnp.int32, (8, 128), 0)
    o_scalars[...] = jnp.where(spot == 0, loss_total, jnp.where(spot == 1, rows_total, jnp.where(spot == 2, residual, branch_size)))
    hcol_old = to_lanes(head_col[...])
    lane = lax.broadcasted_iota(jnp.int32, (1, 128), 1)
    line = jnp.zeros((1, 128), f32)
    for i, v in enumerate([total(u * u) for u in adapter_up] + adapter_w):
        line = jnp.where(lane == 8 + i, v, line)
    early_line[...] = jnp.where(lax.broadcasted_iota(jnp.int32, (8, 128), 0) == 0, line, 0.0)
    for cp in r1:
        cp.wait_recv()
    col_sums = colall[0]
    for d in range(1, 8):
        col_sums = col_sums + colall[d]
    row_sums = (rowall[0] + rowall[1]) + (rowall[2] + rowall[3])
    first_r = decay * first_row[...] + (1.0 - decay) / width * row_sums[0:1, 0:rf]
    second_r = decay * second_row[...] + (1.0 - decay) / width * row_sums[0:1, 128:128 + rs]
    first_c = decay * first_col[...] + (1.0 - decay) / enc_w * col_sums[0:1]
    second_c = decay * second_col[...] + (1.0 - decay) / width * col_sums[1:2]
    head_c = decay * hcol_old[0:4] + (1.0 - decay) / width * col_sums[2:6]
    ones1 = jnp.ones((1, 128), f32)
    first_up = first * lax.rsqrt(hdot(first_r, ones1, ((0,), (0,))) * first_c)
    second_up = second * lax.rsqrt(hdot(second_r, ones1, ((0,), (0,))) * second_c)
    head_up = [hg[c] * lax.rsqrt(hrowx[c] * head_c[c:c + 1] / (col_sums[8 + c:9 + c] / width)) for c in range(4)]
    scalars = [total(first_up * first_up), lane_sum(first_r), total(second_up * second_up), lane_sum(second_r),
               own_w[0], own_w[1], total(sum(u * u for u in head_up)), own_w[2]]
    line = jnp.sum(early_line[...], axis=0, keepdims=True)
    for i, v in enumerate(scalars):
        line = jnp.where(lane == i, v, line)
    msg[...] = jnp.broadcast_to(line, (8, 128))
    msgall[4 * me_d + me_c] = msg[...]
    r2 = send.group(msgall.at[0:31], [(msg, msgall.at[4 * me_d + me_c], target) for target in everyone[::-1]])
    o_first_row[...] = first_r
    o_second_row[...] = second_r
    o_first_col[...] = first_c
    o_second_col[...] = second_c
    o_head_col[...] = from_lanes(jnp.concatenate([head_c, jnp.zeros((4, 128), f32)], axis=0))
    received(gain_spread)
    for c in range(4):
        for i in range(enc_w // 128):
            o_gain_grad[mem * c:mem * (c + 1), 128 * i:128 * (i + 1)] = gain_cols[c, :, i, :]
    gain = o_gain_grad[...]
    gain_state = decay * gain_sq[...] + (1.0 - decay) * (gain * gain + EPS_SQUARE)
    o_gain_sq[...] = gain_state
    gain_up = gain * lax.rsqrt(gain_state)
    o_gain_new[...] = apply(gains[...], gain_up, total(gain_up * gain_up), total(gains[...] * gains[...]), members * enc_w)
    for cp in send.all[:-len(r2)]:
        cp.wait_send()
    for cp in r2:
        cp.wait_recv()
    def over_dp(c):
        out = msgall[c, 0:1, :]
        for d in range(1, 8):
            out = out + msgall[4 * d + c, 0:1, :]
        return out
    s_dp = over_dp(me_c)
    s_all = (over_dp(0) + over_dp(1)) + (over_dp(2) + over_dp(3))
    s_col = (msgall[4 * me_d, 0:1, :] + msgall[4 * me_d + 1, 0:1, :]) + (msgall[4 * me_d + 2, 0:1, :] + msgall[4 * me_d + 3, 0:1, :])
    def item(v, i):
        return lane_sum(jnp.where(lane == i, v, 0.0))
    first_mean = item(s_dp, 1) / enc_w
    o_first_new[...] = apply(w1, first_up * jnp.sqrt(first_mean), item(s_all, 0) * first_mean, item(s_all, 4), enc_w * width)
    second_mean = item(s_dp, 3) / width
    o_second_new[...] = apply(w2, second_up * jnp.sqrt(second_mean), item(s_all, 2) * second_mean, item(s_all, 5), width * width)
    for j in range(5):
        o_adapter_new[j] = apply(adapters[j], adapter_up[j], item(s_col, 8 + j), item(s_col, 13 + j), members * width)
    for c in range(4):
        new = apply(wh[c], head_up[c], item(s_dp, 6), item(s_dp, 7), members * width * CLASSES)
        o_head_new[mem * c:mem * (c + 1)] = new.T.reshape(mem, CLASSES, rs)
    for cp in r2:
        cp.wait_send()


def call_reduce(enc, w1_all, fog, sbuf, hb, small, info, w_first, w_second, w_head, adapters, gains, head_bias,
                first_row, first_col, second_row, second_col, head_row, head_col, adapter_sq, gain_sq, bias_sq):
    members, enc_w = gains.shape
    rf, rs = w_first.shape[0], w_second.shape[0]
    width = w_first.shape[1] * 4
    mem = members // 4
    def like(a):
        return jax.ShapeDtypeStruct(a.shape, f32)
    def row(a):
        return jax.ShapeDtypeStruct((1, a.shape[0]), f32)
    def buffer(*shape, dtype=f32):
        return pltpu.VMEM(shape, dtype)
    params = (w_first, w_second, w_head, adapters, gains, head_bias,
              first_row.reshape(1, -1), first_col.reshape(1, -1), second_row.reshape(1, -1), second_col.reshape(1, -1),
              head_row, head_col, adapter_sq, gain_sq, bias_sq)
    outs = pl.pallas_call(
        functools.partial(reduce_kernel, enc_w, width, members),
        out_shape=(like(w_first), row(first_row), row(first_col), like(w_first),
                   like(w_second), row(second_row), row(second_col), like(w_second),
                   like(w_head), like(head_row), like(head_col), like(w_head),
                   like(adapters), like(adapters), like(adapters),
                   like(gains), like(gains), like(gains),
                   like(head_bias), like(head_bias), like(head_bias), jax.ShapeDtypeStruct((8, 128), f32)),
        in_specs=[VM] * 7 + [FAR] * 15, out_specs=(VM,) * 22,
        scratch_shapes=[
            buffer(width, enc_w, dtype=bf16), buffer(mem, enc_w), buffer(256, enc_w), buffer(mem, 8, enc_w),
            buffer(4, 2, 2, rf, 128, dtype=bf16), buffer(4, 2, 2, rf, 128, dtype=bf16),
            buffer(4, 2, rf, 128, dtype=bf16), buffer(4, 2, rf, 128, dtype=bf16), buffer(4, 2, rf, 128, dtype=bf16),
            buffer(4, 2, rf, 128, dtype=bf16), buffer(4, 2, rf, 128), buffer(4, 2, rf, 128, dtype=bf16),
            buffer(4, rf, 128, dtype=bf16), buffer(4, rf, 128, dtype=bf16), buffer(3, rf, 128, dtype=bf16),
            buffer(4, 2, 2, rs, 128, dtype=bf16), buffer(4, 2, 2, rs, 128, dtype=bf16), buffer(4, rs, 128, dtype=bf16),
            buffer(4, 2, rs, 128, dtype=bf16), buffer(4, 2, rs, 128, dtype=bf16), buffer(4, rs, 128, dtype=bf16),
            buffer(3, rs, 128, dtype=bf16),
            buffer(4, rs, 128, dtype=bf16), buffer(4, rs, 128, dtype=bf16), buffer(3, rs, 128, dtype=bf16),
            buffer(4, rs, 128),
            buffer(4, 32, 128), buffer(4, 32, 128), buffer(3, 32, 128), buffer(4, 2, 32, 128), buffer(4, 4, 2, 8, 128),
            buffer(mem, 8, 128), buffer(7, 8, 128), buffer(8, 8, 128), buffer(4, 8, 8, 128),
            buffer(16, 128), buffer(8, 16, 128), buffer(8, 256), buffer(4, 8, 256),
            buffer(8, 128), buffer(32, 8, 128), buffer(8, 128),
            *[buffer(*p.shape) for p in params], pltpu.SemaphoreType.DMA((15,)),
            pltpu.SemaphoreType.DMA((NSEM3,)), pltpu.SemaphoreType.DMA((NSEM3,)),
        ],
        compiler_params=pltpu.CompilerParams(collective_id=1, has_side_effects=True, vmem_limit_bytes=26 << 20),
    )(enc, w1_all, fog, sbuf, hb, small.reshape(4, 2, 32, 128), info, *map(far, params))
    outs = call_store(outs)
    for i in (1, 2, 5, 6):
        outs[i] = outs[i].reshape(-1)
    for i in (21, 22, 23, 24):
        outs[i] = outs[i].reshape(())
    for i in (8, 11):
        outs[i] = outs[i].transpose(0, 2, 1)
    for i in (10, 18, 19, 20):
        outs[i] = outs[i].T
    return tuple(outs)


def store_kernel(count, *refs):
    arrays, scalars = refs[:count], refs[count]
    outs, singles = refs[count + 1:2 * count + 1], refs[2 * count + 1:2 * count + 5]
    kept, sems = refs[2 * count + 5:2 * count + 9], refs[2 * count + 9]
    copies = [pltpu.make_async_copy(src, dst, sems.at[i]) for i, (src, dst) in enumerate(zip(arrays, outs))]
    for copy in copies:
        copy.start()
    for i, (one, single) in enumerate(zip(kept, singles)):
        one[...] = scalars[i:i + 1, 0:1]
        copies.append(pltpu.make_async_copy(one, single, sems.at[count + i]))
        copies[-1].start()
    for copy in copies:
        copy.wait()


def call_store(arrays):
    count = len(arrays) - 1
    one = jax.ShapeDtypeStruct((1, 1), f32)
    return list(pl.pallas_call(
        functools.partial(store_kernel, count),
        out_shape=tuple(jax.ShapeDtypeStruct(a.shape, a.dtype) for a in arrays[:-1]) + (one,) * 4,
        in_specs=[VM] * (count + 1), out_specs=(FAR,) * (count + 4),
        scratch_shapes=[pltpu.VMEM((1, 1), f32)] * 4 + [pltpu.SemaphoreType.DMA((count + 4,))],
        compiler_params=pltpu.CompilerParams(vmem_limit_bytes=16 << 20),
    )(*arrays))


def local_blocks(bin_index, bin_fraction, row_mask, targets, w_first, w_second, w_head, adapters, gains, head_bias,
          first_row, first_col, second_row, second_col, head_row, head_col, adapter_sq, gain_sq, bias_sq):
    members = gains.shape[0]
    mem = members // 4
    w_head, head_bias, head_col, bias_sq = w_head.transpose(0, 2, 1), head_bias.T, head_col.T, bias_sq.T
    buf, hbuf, adbuf, enc, onehots, info = call_gather(
        bin_index.T, bin_fraction.T, row_mask, targets, w_first, w_second, w_head, adapters, mem)
    w1_all, fog, sbuf, hb, small = call_compute(members, buf, hbuf, adbuf, enc, onehots, info, gains, head_bias)
    return call_reduce(enc, w1_all, fog, sbuf, hb, small, info, w_first, w_second, w_head, adapters, gains, head_bias,
                       first_row, first_col, second_row, second_col, head_row, head_col, adapter_sq, gain_sq, bias_sq)


def finish(weight, update, update_sq, weight_sq, entries):
    rms_update = jnp.sqrt(update_sq / entries)
    rms_weight = jnp.sqrt(weight_sq / entries)
    update = update / jnp.maximum(1.0, rms_update / CLIP_LIMIT)
    return weight - RELATIVE_RATE * jnp.maximum(RATE_FLOOR, rms_weight) * update


def local_any(bin_index, bin_fraction, row_mask, targets, w_first, w_second, w_head, adapters, gains, head_bias,
              first_row, first_col, second_row, second_col, head_row, head_col, adapter_sq, gain_sq, bias_sq):
    count_col = lax.axis_size("col")
    count_dp = lax.axis_size("dp")
    col_place = lax.axis_index("col")
    dp_place = lax.axis_index("dp")
    members, enc_width = gains.shape
    col_width = adapters.shape[2]
    full_width = col_width * count_col
    mem = members // count_col
    rows = row_mask.shape[0]
    decay = 1.0 - STEP ** (-0.8)
    row_total = lax.psum(jnp.sum(row_mask.astype(f32)), "dp")
    hi = bin_fraction.astype(bf16).astype(f32)
    onehot = jax.nn.one_hot(targets, CLASSES, dtype=f32) * row_mask[:, None]
    table = jnp.concatenate([bin_index.astype(f32), hi, bin_fraction - hi, onehot, row_mask[:, None].astype(f32),
                             jnp.zeros((rows, 63), f32)], axis=1).astype(bf16)
    table = table.reshape(rows // count_dp, count_dp, 128)
    table = jnp.roll(table, -dp_place, axis=1).transpose(1, 0, 2).reshape(rows, 128)
    table = lax.all_to_all(table, "dp", 0, 0, tiled=True)
    mask = table[:, 64].astype(jnp.int32)
    spot = jnp.where(mask > 0, jnp.cumsum(mask) - 1, -1)
    comp = jnp.dot((jnp.arange(rows)[:, None] == spot[None, :]).astype(bf16), table, preferred_element_type=f32).astype(bf16)
    levels = jnp.arange(BINS, dtype=f32)
    where_at = (comp[:, :FEATS].astype(f32) + comp[:, FEATS:2 * FEATS].astype(f32) + comp[:, 2 * FEATS:3 * FEATS].astype(f32))
    enc = jnp.clip(where_at[:, :, None] - levels, 0.0, 1.0).reshape(rows, enc_width).astype(bf16)
    onehots = jnp.tile(comp[:, 48:48 + CLASSES], (1, mem))
    info = jnp.zeros((8, 128), f32).at[0].set(jnp.sum(mask).astype(f32)).at[1].set(row_total)

    def whole(part):
        return lax.all_gather(lax.all_gather(part.astype(bf16), "dp", axis=0, tiled=True), "col", axis=1, tiled=True)

    def blocks(full):
        return full.reshape(8, -1, 4, 128).transpose(0, 2, 1, 3)

    def unblock(part):
        return part.astype(f32).reshape(8, 4, -1, 128).transpose(0, 2, 1, 3).reshape(-1, full_width)
    buf = jnp.concatenate([blocks(whole(w_first)), blocks(whole(w_second))], axis=2).reshape(4, 2, 2, 2, -1, 128)
    heads = lax.all_gather(w_head.astype(bf16), "dp", axis=1, tiled=True)
    heads = lax.dynamic_slice_in_dim(heads, col_place * mem, mem, 0)
    hbuf = heads.transpose(1, 0, 2).reshape(4, 2, -1, mem * CLASSES)
    adbuf = lax.dynamic_slice_in_dim(lax.all_gather(adapters, "col", axis=0), col_place * mem, mem, 2)
    w1_all, fog, sbuf, hb, small = call_compute(members, buf, hbuf, adbuf, enc, onehots, info, gains, head_bias.T)
    own_gains = lax.dynamic_slice_in_dim(gains, col_place * mem, mem, 0)
    sums = jnp.einsum("rk,mrd->mkd", enc, fog, preferred_element_type=f32)
    first_part = jnp.einsum("mkd,mk->kd", sums, own_gains, precision=HIGH)
    gain_part = jnp.einsum("mkd,kd->mk", sums, w1_all.astype(f32), precision=HIGH)
    second_part = unblock(sbuf)
    head_part = hb.astype(f32).reshape(full_width, mem, CLASSES).transpose(1, 0, 2)

    def scatter(part):
        return lax.psum_scatter(lax.psum_scatter(part, "dp", scatter_dimension=0, tiled=True), "col", scatter_dimension=1, tiled=True)
    first_grad, second_grad = scatter(first_part), scatter(second_part)
    head_grad = lax.all_gather(lax.psum_scatter(head_part, "dp", scatter_dimension=1, tiled=True), "col", axis=0, tiled=True)
    adapter_part = small[:, :32].reshape(mem, 4, 8, 128)[:, :, :5].transpose(2, 0, 1, 3).reshape(5, mem, full_width)
    adapter_grad = lax.psum(lax.all_to_all(adapter_part, "col", 2, 1, tiled=True), "dp")
    bias_part = small[3, 5].reshape(mem, CLASSES)
    gain_grad, bias_grad = lax.psum(
        (lax.all_gather(gain_part, "col", axis=0, tiled=True), lax.all_gather(bias_part, "col", axis=0, tiled=True)), "dp")
    loss_sum, residual_sq, branch_sq = lax.psum(jnp.sum(small[:3, 5], axis=1), ("dp", "col"))
    first_square = first_grad * first_grad + EPS_SQUARE
    second_square = second_grad * second_grad + EPS_SQUARE
    head_square = head_grad * head_grad + EPS_SQUARE
    first_rowsum, second_rowsum = lax.psum(
        (jnp.sum(first_square, axis=1), jnp.sum(second_square, axis=1)), "col"
    )
    first_row_new = decay * first_row + (1.0 - decay) * (first_rowsum / full_width)
    second_row_new = decay * second_row + (1.0 - decay) * (second_rowsum / full_width)
    head_row_new = decay * head_row + (1.0 - decay) * jnp.mean(head_square, axis=-1)
    stats = lax.psum(
        (
            jnp.sum(first_square, axis=0),
            jnp.sum(second_square, axis=0),
            jnp.sum(head_square, axis=1),
            jnp.sum(first_row_new),
            jnp.sum(second_row_new),
            jnp.sum(head_row_new, axis=1),
        ),
        "dp",
    )
    first_colsum, second_colsum, head_colsum, first_rowtotal, second_rowtotal, head_rowtotal = stats
    first_col_new = decay * first_col + (1.0 - decay) * (first_colsum / enc_width)
    second_col_new = decay * second_col + (1.0 - decay) * (second_colsum / full_width)
    head_col_new = decay * head_col + (1.0 - decay) * (head_colsum / full_width)
    first_estimate = first_row_new[:, None] * first_col_new[None, :] / (first_rowtotal / enc_width)
    second_estimate = (
        second_row_new[:, None] * second_col_new[None, :] / (second_rowtotal / full_width)
    )
    head_estimate = (
        head_row_new[:, :, None]
        * head_col_new[:, None, :]
        / (head_rowtotal / full_width)[:, None, None]
    )
    first_update = first_grad * lax.rsqrt(first_estimate)
    second_update = second_grad * lax.rsqrt(second_estimate)
    head_update = head_grad * lax.rsqrt(head_estimate)
    adapter_sq_new = decay * adapter_sq + (1.0 - decay) * (adapter_grad * adapter_grad + EPS_SQUARE)
    adapter_update = adapter_grad * lax.rsqrt(adapter_sq_new)
    gain_sq_new = decay * gain_sq + (1.0 - decay) * (gain_grad * gain_grad + EPS_SQUARE)
    gain_update = gain_grad * lax.rsqrt(gain_sq_new)
    bias_sq_new = decay * bias_sq + (1.0 - decay) * (bias_grad * bias_grad + EPS_SQUARE)
    bias_update = bias_grad * lax.rsqrt(bias_sq_new)
    share_col = 1.0 / count_col
    share_dp = 1.0 / count_dp
    sums = lax.psum(
        (
            jnp.sum(first_update * first_update),
            jnp.sum(w_first * w_first),
            jnp.sum(second_update * second_update),
            jnp.sum(w_second * w_second),
            jnp.sum(head_update * head_update) * share_col,
            jnp.sum(w_head * w_head) * share_col,
            jnp.sum(adapter_update * adapter_update, axis=(1, 2)) * share_dp,
            jnp.sum(adapters * adapters, axis=(1, 2)) * share_dp,
        ),
        ("dp", "col"),
    )
    first_new = finish(w_first, first_update, sums[0], sums[1], enc_width * full_width)
    second_new = finish(w_second, second_update, sums[2], sums[3], full_width * full_width)
    head_new = finish(w_head, head_update, sums[4], sums[5], members * full_width * CLASSES)
    adapter_new = finish(
        adapters,
        adapter_update,
        sums[6].reshape(5, 1, 1),
        sums[7].reshape(5, 1, 1),
        members * full_width,
    )
    gain_new = finish(
        gains,
        gain_update,
        jnp.sum(gain_update * gain_update),
        jnp.sum(gains * gains),
        members * enc_width,
    )
    bias_new = finish(
        head_bias,
        bias_update,
        jnp.sum(bias_update * bias_update),
        jnp.sum(head_bias * head_bias),
        members * CLASSES,
    )
    residual_rms = jnp.sqrt(residual_sq / (row_total * members * full_width))
    branch_rms = jnp.sqrt(branch_sq / (row_total * members * full_width))
    return (
        first_grad,
        first_row_new,
        first_col_new,
        first_new,
        second_grad,
        second_row_new,
        second_col_new,
        second_new,
        head_grad,
        head_row_new,
        head_col_new,
        head_new,
        adapter_grad,
        adapter_sq_new,
        adapter_new,
        gain_grad,
        gain_sq_new,
        gain_new,
        bias_grad,
        bias_sq_new,
        bias_new,
        loss_sum,
        row_total,
        residual_rms,
        branch_rms,
    )


def local(*args):
    if lax.axis_size("dp") == 8 and lax.axis_size("col") == 4:
        return local_blocks(*args)
    return local_any(*args)


def solution(mesh):
    placed = (
        P("dp", None),
        P("dp", None),
        P("dp"),
        P("dp"),
        P("dp", "col"),
        P("dp", "col"),
        P(None, "dp", None),
        P(None, None, "col"),
        P(),
        P(),
        P("dp"),
        P("col"),
        P("dp"),
        P("col"),
        P(None, "dp"),
        P(),
        P(None, None, "col"),
        P(),
        P(),
    )
    return jax.shard_map(
        local,
        mesh=mesh,
        in_specs=placed,
        out_specs=(
            P("dp", "col"),
            P("dp"),
            P("col"),
            P("dp", "col"),
            P("dp", "col"),
            P("dp"),
            P("col"),
            P("dp", "col"),
            P(None, "dp", None),
            P(None, "dp"),
            P(),
            P(None, "dp", None),
            P(None, None, "col"),
            P(None, None, "col"),
            P(None, None, "col"),
            P(),
            P(),
            P(),
            P(),
            P(),
            P(),
            P(),
            P(),
            P(),
            P(),
        ),
        check_vma=False,
    )
```

```python
import functools
import jax, jax.numpy as jnp
from jax import lax
from jax.experimental import pallas as pl
from jax.experimental.pallas import tpu as pltpu
from jax.sharding import PartitionSpec as P

FEATS, BINS, CLASSES = 16, 48, 16
STEP = 10
EPS_SQUARE = 1e-30
CLIP_LIMIT = 1.0
RELATIVE_RATE = 0.4
RATE_FLOOR = 0.001
R = 64
GROUPS = 2
ORDER = (0, 1, 0, 1, 0, 1, 0, 1, 0, 1, 0, 1, 0, 1, 0, 1, 0, 1, 0, 1, 0, 1)
WIDE = True
f32, bf16 = jnp.float32, jnp.bfloat16

def dot(a, b):
    return jnp.dot(a, b, preferred_element_type=f32)
def dot_t(a, b):
    return lax.dot_general(a, b, (((1,), (1,)), ((), ())), preferred_element_type=f32)
def t_dot(a, b):
    return lax.dot_general(a, b, (((0,), (0,)), ((), ())), preferred_element_type=f32)

MESH = pl.DeviceIdType.MESH


def far(array):
    return pltpu.with_memory_space_constraint(array, pltpu.HBM)


HIGH = lax.Precision.HIGHEST
VM = pl.BlockSpec(memory_space=pltpu.VMEM)
FAR = pl.BlockSpec(memory_space=pltpu.HBM)


def place():
    d, c = lax.axis_index("dp"), lax.axis_index("col")
    return d // 2, d % 2, c // 2, c % 2


def z_other(z, k):
    if k == 0:
        return z
    return [None, z + 1 - 2 * (z % 2), (z + 2) % 4, 3 - z][k]


def other(b, k):
    return 1 - b if k else b


def device(z, y, x, core):
    return (2 * z + y, 2 * x + core)


PLANE = ((0, 1), (1, 0), (1, 1))
DP_PEERS = tuple((kz, ky) for kz in range(4) for ky in range(2))[1:]
COL_PEERS = ((0, 1), (1, 0), (1, 1))
NSEM1 = 29
NSEM3 = 26
CUTS = (64, 112)


class Sender:
    def __init__(self, send_sem, recv_sem):
        self.send_sem, self.recv_sem, self.count = send_sem, recv_sem, 0
        self.all = []

    def __call__(self, src, dst, target):
        i = self.count
        self.count += 1
        assert i < self.send_sem.shape[0]
        copy = pltpu.make_async_remote_copy(
            src_ref=src, dst_ref=dst, send_sem=self.send_sem.at[i], recv_sem=self.recv_sem.at[i],
            device_id=target, device_id_type=MESH)
        copy.start()
        self.all.append(copy)
        return copy

    def group(self, whole, copies):
        i = self.count
        self.count += 1
        assert i < self.send_sem.shape[0]
        for src, dst, target in copies:
            pltpu.make_async_remote_copy(
                src_ref=src, dst_ref=dst, send_sem=self.send_sem.at[i], recv_sem=self.recv_sem.at[i],
                device_id=target, device_id_type=MESH).start()
        self.all.append(Group(whole, self.send_sem.at[i], self.recv_sem.at[i]))
        return [self.all[-1]]


class Group:
    def __init__(self, whole, send_sem, recv_sem):
        self.sent = pltpu.make_async_copy(whole, whole, send_sem)
        self.landed = pltpu.make_async_copy(whole, whole, recv_sem)

    def wait_recv(self):
        self.landed.wait()

    def wait_send(self):
        self.sent.wait()


def greet(targets):
    barrier = pltpu.get_barrier_semaphore()
    for target in targets:
        pl.semaphore_signal(barrier, inc=1, device_id=target, device_id_type=MESH)
    return barrier, len(targets)


def hdot(a, b, dims=((1,), (0,))):
    return lax.dot_general(a, b, (dims, ((), ())), precision=HIGH, preferred_element_type=f32)


def gather_kernel(bin_index, bin_fraction, row_mask, targets, w_first, w_second, w_head, adapters_far,
                  buf, hbuf, adbuf, enc, onehots, info, table, recv,
                  w_first_v, w_second_v, w_head_v, adapters, bin_index_v, bin_fraction_v, row_mask_v, targets_v,
                  load_sem, send_sem, recv_sem):
    z, y, x, core = place()
    loads = [pltpu.make_async_copy(src, dst, load_sem.at[i]) for i, (src, dst) in enumerate((
        (w_first, w_first_v), (w_second, w_second_v), (w_head, w_head_v), (adapters_far, adapters),
        (bin_index, bin_index_v), (bin_fraction, bin_fraction_v), (row_mask, row_mask_v), (targets, targets_v)))]
    for load in loads:
        load.start()
    rows = bin_index.shape[1]
    rf, rs = w_first.shape[0], w_second.shape[0]
    me_c = 2 * x + core
    mem = adbuf.shape[2]
    near = [device(z_other(z, kz), other(y, ky), x, core) for kz, ky in DP_PEERS]
    near += [device(z, y, other(x, kx), other(core, kc)) for kx, kc in COL_PEERS]
    near += [device(z, 1 - y, 1 - x, core)]
    barrier, count = greet(near)
    loads[0].wait()
    loads[1].wait()
    buf[z, y, x, core, 0:rf, :] = w_first_v[...].astype(bf16)
    buf[z, y, x, core, rf:rf + rs, :] = w_second_v[...].astype(bf16)
    pl.semaphore_wait(barrier, count)
    send = Sender(send_sem, recv_sem)
    parts = [pl.ds(lo, hi - lo) for lo, hi in zip((0,) + CUTS, CUTS + (rf + rs,))]
    mine = [buf.at[z, y, x, core, part] for part in parts]
    a0, b0 = [], []
    for i in range(len(parts) - 1):
        a0.append(send.group(buf.at[0:3, 0, 0, 0, parts[i]],
                             [(mine[i], mine[i], device(z_other(z, k), y, x, core)) for k in (1, 2, 3)]))
        if i == 0:
            a1 = send.group(buf.at[0:3, 0, 0, 0, parts[-1]],
                            [(mine[-1], mine[-1], device(z, other(y, ky), other(x, kx), core)) for ky, kx in PLANE])
    for load in loads[2:]:
        load.wait()
    hbuf[z, y] = w_head_v[pl.ds(me_c * mem, mem)].reshape(mem * CLASSES, rs).T.astype(bf16)
    adbuf[me_c] = adapters[:, pl.ds(pl.multiple_of(me_c * mem, mem), mem), :]
    slot = rows // 16
    i_row = lax.broadcasted_iota(jnp.int32, (rows, rows), 0)
    i_col = lax.broadcasted_iota(jnp.int32, (rows, rows), 1)
    me_d = 2 * z + y
    p_row = lax.broadcasted_iota(jnp.int32, (rows // 2, rows), 0)
    p_col = lax.broadcasted_iota(jnp.int32, (rows // 2, rows), 1)
    wanted = (p_row % slot) * 8 + (p_row // slot + me_d) % 8
    frac = bin_fraction_v[...]
    mask = row_mask_v[...].astype(f32)
    length = jnp.sum(mask, axis=1, keepdims=True)
    high = jnp.floor(length * (1.0 / 16.0))
    c_i = lax.broadcasted_iota(jnp.int32, (CLASSES, rows), 0)
    marks = jnp.where(c_i == 0, mask, jnp.where(c_i == 1, high, jnp.where(c_i == 2, length - 16.0 * high, 0.0)))
    columns = jnp.concatenate([bin_index_v[...].astype(f32), frac, jnp.where(c_i == targets_v[...], mask, 0.0), marks], axis=0).astype(bf16)
    nothing = jnp.zeros((64, rows), bf16)
    dealt = (dot_t((p_col == wanted).astype(bf16), jnp.concatenate([columns, nothing], axis=0))
                  + dot_t((p_col == wanted + 8 * slot).astype(bf16), jnp.concatenate([nothing, columns], axis=0))).astype(bf16)
    table[...] = dealt.reshape(table.shape)
    recv[me_d] = table[me_d]
    t = []
    for kz, ky in DP_PEERS:
        pz, py = z_other(z, kz), other(y, ky)
        t.append((table.at[2 * pz + py, core], recv.at[me_d, core], device(pz, py, x, core)))
    t = send.group(recv.at[0:7, 0], t)
    h = send.group(hbuf.at[0:3, 0], [(hbuf.at[z, y], hbuf.at[z, y], device(z_other(z, k), y, x, core)) for k in (1, 2, 3)])
    ad = []
    for kx, kc in COL_PEERS:
        px, pc = other(x, kx), other(core, kc)
        theirs = pl.ds(pl.multiple_of((2 * px + pc) * mem, mem), mem)
        ad.append((adapters.at[:, theirs, :], adbuf.at[me_c], device(z, y, px, pc)))
    ad = send.group(adbuf.at[0:3], ad)
    mate = device(z, y, x, 1 - core)
    last = []
    for i, part in enumerate(parts[:-1]):
        for cp in a0[i]:
            cp.wait_recv()
        column = buf.at[:, y, x, core, part]
        b0.append([send(column, column, device(z, other(y, ky), other(x, kx), core)) for ky, kx in PLANE])
        if i == 0:
            for cp in a1:
                cp.wait_recv()
            plane = buf.at[z, :, :, core, parts[-1]]
            b1 = [send(plane, plane, device(z_other(z, k), y, x, core)) for k in (1, 2, 3)]
            last.append(send(plane, plane, mate))
        last.append(send(column, column, mate))
    for cp in h:
        cp.wait_recv()
    h2 = send(hbuf.at[:, y], hbuf.at[:, y], device(z, 1 - y, x, core))
    for cp in t:
        cp.wait_recv()
    t2 = send.group(recv.at[0:7, 0], [(recv.at[2 * pz + py, core], recv.at[2 * pz + py, core], mate)
                                      for pz, py in [(z_other(z, kz), other(y, ky)) for kz, ky in DP_PEERS]])
    for cp in t2:
        cp.wait_recv()
    lane8 = lax.broadcasted_iota(jnp.int32, (8, 128), 1)
    got = recv[...].reshape(rows // 2, 128)
    mask_row = jnp.concatenate([dot_t((lane8 == 48).astype(bf16), got), dot_t((lane8 == 112).astype(bf16), got)], axis=1)
    pos = dot(mask_row.astype(bf16), (i_row < i_col).astype(bf16))
    spot = jnp.where(mask_row > 0.5, pos, -1.0)[0:1]
    perm = (i_row.astype(f32) == spot).astype(bf16)
    lane = lax.broadcasted_iota(jnp.int32, (1, 128), 1)
    low_half = (lane < 64).astype(bf16)
    comp = (dot(perm[:, :rows // 2], got * low_half) + dot(perm[:, rows // 2:], got * (1.0 - low_half))).astype(bf16)
    enc_w, hw = enc.shape[1], onehots.shape[1]
    kk = lax.broadcasted_iota(jnp.int32, (128, enc_w), 1)
    ll = lax.broadcasted_iota(jnp.int32, (128, enc_w), 0)
    ff = ll & (FEATS - 1)
    spread = (((ll & 63) < 2 * FEATS) & (kk >= ff * BINS) & (kk < (ff + 1) * BINS)).astype(bf16)
    lev = (lax.broadcasted_iota(jnp.int32, (1, enc_w), 1) % BINS).astype(f32)
    enc[...] = jnp.clip(dot(comp, spread) - lev, 0.0, 1.0).astype(bf16)
    l2 = lax.broadcasted_iota(jnp.int32, (128, hw), 0)
    c2 = lax.broadcasted_iota(jnp.int32, (128, hw), 1)
    onehots[...] = dot(comp, ((l2 & 63) == 2 * FEATS + (c2 & (CLASSES - 1))).astype(bf16)).astype(bf16)
    per_row = jnp.where((lane & 63) == 49, 16.0, jnp.where((lane & 63) == 50, 1.0, 0.0))
    total = jnp.sum(jnp.sum(got.astype(f32), axis=0, keepdims=True) * per_row, axis=1, keepdims=True) / (2 * slot)
    info[0:1, :] = jnp.zeros((1, 128), f32) + jnp.sum(mask_row[0:1], axis=1, keepdims=True)
    info[1:2, :] = jnp.zeros((1, 128), f32) + total
    info[2:8, :] = jnp.zeros((6, 128), f32)
    for i, part in enumerate(parts[:-1]):
        for cp, (ky, kx) in zip(b0[i], PLANE):
            cp.wait_recv()
            column = buf.at[:, other(y, ky), other(x, kx), core, part]
            last.append(send(column, column, mate))
        if i == 0:
            for cp, k in zip(b1, (1, 2, 3)):
                cp.wait_recv()
                plane = buf.at[z_other(z, k), :, :, core, parts[-1]]
                last.append(send(plane, plane, mate))
    for cp in last + ad + [h2]:
        cp.wait_recv()
    for cp in send.all:
        cp.wait_send()


def call_gather(bin_index, bin_fraction, row_mask, targets, w_first, w_second, w_head, adapters, mem):
    rows = bin_index.shape[1]
    both = w_first.shape[0] + w_second.shape[0]
    return pl.pallas_call(
        gather_kernel,
        out_shape=(
            jax.ShapeDtypeStruct((4, 2, 2, 2, both, 128), bf16),
            jax.ShapeDtypeStruct((4, 2, w_head.shape[2], 128), bf16),
            jax.ShapeDtypeStruct((4, 5, mem, 128), f32),
            jax.ShapeDtypeStruct((rows, FEATS * BINS), bf16),
            jax.ShapeDtypeStruct((rows, mem * CLASSES), bf16),
            jax.ShapeDtypeStruct((8, 128), f32),
        ),
        in_specs=[FAR] * 8, out_specs=(VM,) * 6,
        scratch_shapes=[pltpu.VMEM((8, 2, rows // 32, 128), bf16), pltpu.VMEM((8, 2, rows // 32, 128), bf16),
                        pltpu.VMEM(w_first.shape, f32), pltpu.VMEM(w_second.shape, f32),
                        pltpu.VMEM(w_head.shape, f32), pltpu.VMEM(adapters.shape, f32),
                        pltpu.VMEM(bin_index.shape, jnp.int32), pltpu.VMEM(bin_fraction.shape, f32),
                        pltpu.VMEM((1, rows), jnp.int32), pltpu.VMEM((1, rows), jnp.int32),
                        pltpu.SemaphoreType.DMA((8,)),
                        pltpu.SemaphoreType.DMA((NSEM1,)), pltpu.SemaphoreType.DMA((NSEM1,))],
        compiler_params=pltpu.CompilerParams(collective_id=0, has_side_effects=True, vmem_limit_bytes=16 << 20),
    )(*map(far, (bin_index, bin_fraction, row_mask.reshape(1, -1), targets.reshape(1, -1),
                 w_first, w_second, w_head, adapters)))


def seg_max(x):
    lane = lax.broadcasted_iota(jnp.int32, x.shape, 1)
    n = x.shape[1]
    for s in (1, 2, 4, 8):
        up = pltpu.roll(x, n - s, 1)
        dn = pltpu.roll(x, s, 1)
        x = jnp.maximum(x, jnp.where((lane & s) == 0, up, dn))
    return x


def fold8(v):
    return sum(v[8 * i:8 * i + 8] for i in range(v.shape[0] // 8))


def compute_kernel(members, buf, hbuf, adbuf, enc_all, onehots, info, gains_far, bias_far,
                   w1, fog_all, sbuf, hb, small,
                   w2, w2t, head, headt, adapters, gains, low_gains,
                   second_acc, head_acc, adapt, sums, halves, gains_all, bias_all, load_sem):
    rows_all = enc_all.shape[0]
    enc_w, width = w1.shape
    mem = adbuf.shape[2]
    hw = mem * CLASSES
    rf, rs = enc_w // 8, width // 8
    me_c = lax.axis_index("col")
    loads = [pltpu.make_async_copy(gains_far, gains_all, load_sem.at[0]),
             pltpu.make_async_copy(bias_far, bias_all, load_sem.at[1])]
    for load in loads:
        load.start()
    for d in range(8):
        for c in range(4):
            lanes = slice(128 * c, 128 * c + 128)
            w1[rf * d:rf * (d + 1), lanes] = buf[d // 2, d % 2, c // 2, c % 2, 0:rf, :]
            w2[rs * d:rs * (d + 1), lanes] = buf[d // 2, d % 2, c // 2, c % 2, rf:rf + rs, :]
        head[rs * d:rs * (d + 1), :] = hbuf[d // 2, d % 2]
    for c in range(4):
        adapters[:, :, 128 * c:128 * c + 128] = adbuf[c]
    for j in (0, 1, 3, 4):
        halves[j] = 0.5 * adapters[j]
    w2t[...] = w2[...].T
    headt[...] = head[...].T
    for load in loads:
        load.wait()
    own = pl.ds(pl.multiple_of(me_c * mem, mem), mem)
    gains[...] = gains_all[own, :]
    low_gains[...] = gains[...].astype(bf16)
    owner = lax.broadcasted_iota(jnp.int32, (1, hw), 1) // CLASSES
    fold = (lax.broadcasted_iota(jnp.int32, (CLASSES, hw), 1) % CLASSES
            == lax.broadcasted_iota(jnp.int32, (CLASSES, hw), 0)).astype(f32)
    wide = hdot(bias_all[...], fold, ((0,), (0,)))
    at = lax.broadcasted_iota(jnp.int32, (members, hw), 0)
    bias = jnp.sum(jnp.where(at == me_c * mem + owner, wide, 0.0), axis=0, keepdims=True)
    n_rows = jnp.max(info[0:1, :]).astype(jnp.int32)
    loss_scale = 1.0 / (members * info[1:2, :])
    second_acc[...] = jnp.zeros_like(second_acc)
    head_acc[...] = jnp.zeros_like(head_acc)
    adapt[...] = jnp.zeros_like(adapt)
    sums[...] = jnp.zeros_like(sums)

    s_i = lax.broadcasted_iota(jnp.int32, (hw, hw), 0) // CLASSES
    s_j = lax.broadcasted_iota(jnp.int32, (hw, hw), 1) // CLASSES
    seg = (s_i == s_j).astype(bf16)

    def group(R, rows, pad_rows, oh, mk, enc, ms, out, grads):
        count = len(ms)
        fin = jnp.concatenate([enc * low_gains[m:m + 1, :] for m in ms], axis=0)
        fo = dot(fin, w1[...])
        yield
        hs, us, sos, sins = [], [], [], []
        res = jnp.zeros((8, width), f32)
        res_pad = jnp.zeros((1, width), f32)
        for i, m in enumerate(ms):
            h = fo[i * R:(i + 1) * R] * halves[0, m:m + 1, :] + halves[1, m:m + 1, :]
            u = 1.0 + jnp.tanh(h)
            so = h * u
            sq = so * so
            res += fold8(sq)
            res_pad += sq[R - 1:R]
            hs.append(h)
            us.append(u)
            sos.append(so)
            sins.append((so * adapters[2, m:m + 1, :]).astype(bf16))
        sums[2] += res
        sums[4, 0:1] -= pad_rows * res_pad
        sin = jnp.concatenate(sins, axis=0)
        yield
        s2 = dot(sin, w2[...])
        yield
        h2s, u2s, brs, sts = [], [], [], []
        bres = jnp.zeros((8, width), f32)
        bres_pad = jnp.zeros((1, width), f32)
        for i, m in enumerate(ms):
            h = s2[i * R:(i + 1) * R] * halves[3, m:m + 1, :] + halves[4, m:m + 1, :]
            u = 1.0 + jnp.tanh(h)
            br = h * u
            sq = br * br
            bres += fold8(sq)
            bres_pad += sq[R - 1:R]
            h2s.append(h)
            u2s.append(u)
            brs.append(br)
            sts.append((sos[i] + br).astype(bf16))
        sums[3] += bres
        sums[4, 1:2] -= pad_rows * bres_pad
        st = jnp.concatenate(sts, axis=0)
        yield
        lo = dot(st, head[...])
        yield
        logits = bias
        for i, m in enumerate(ms):
            logits = logits + jnp.where(owner == m, lo[i * R:(i + 1) * R], 0.0)
        top = seg_max(logits)
        ex = jnp.exp(logits - top)
        exh = ex.astype(bf16)
        exl = (ex - exh.astype(f32)).astype(bf16)
        both = dot(jnp.concatenate([exh, exl], axis=0), seg)
        tot = both[:R] + both[R:]
        loss_c = (top + jnp.log(tot) - logits) * oh
        lgf = ((ex / tot * mk - oh) * loss_scale).astype(bf16).astype(f32)
        lgm = jnp.concatenate([jnp.where(owner == m, lgf, 0.0).astype(bf16) for m in ms], axis=0)
        out.append((loss_c, lgf))
        yield
        sg = dot(lgm, headt[...])
        yield
        ogs = []
        for i, m in enumerate(ms):
            pg = sg[i * R:(i + 1) * R] * (u2s[i] + brs[i] * (2.0 - u2s[i]))
            adapt[3, m] += fold8(pg * h2s[i])
            adapt[4, m] += fold8(pg)
            ogs.append((pg * halves[3, m:m + 1, :]).astype(bf16))
        og = jnp.concatenate(ogs, axis=0)
        yield
        ig = dot(og, w2t[...])
        yield
        grads.append((lgm, st, sin, og))
        if len(grads) == GROUPS:
            lgms, sts_all, sins_all, ogs_all = (jnp.concatenate(v, axis=0) for v in zip(*grads))
            head_acc[...] += t_dot(lgms, sts_all)
            second_acc[...] += t_dot(sins_all, ogs_all)
        yield
        for i, m in enumerate(ms):
            igm = ig[i * R:(i + 1) * R]
            adapt[2, m] += fold8(igm * sos[i])
            one = sg[i * R:(i + 1) * R] + igm * adapters[2, m:m + 1, :]
            low = one * (us[i] + sos[i] * (2.0 - us[i]))
            adapt[0, m] += fold8(low * hs[i])
            adapt[1, m] += fold8(low)
            fog_all[m, rows, :] = (low * halves[0, m:m + 1, :]).astype(bf16)
        yield

    def tile(R, start):
        rows = pl.ds(pl.multiple_of(start, 64), R)
        enc = enc_all[rows, :]
        oh = onehots[rows, :].astype(f32)
        mk = (lax.broadcasted_iota(jnp.int32, (R, hw), 0) + start < n_rows).astype(f32)
        pad_rows = jnp.maximum(start + R - n_rows, 0).astype(f32)
        out, grads = [], []
        per = mem // GROUPS
        runs = [group(R, rows, pad_rows, oh, mk, enc, tuple(range(g * per, (g + 1) * per)), out, grads) for g in range(GROUPS)]
        for g in ORDER:
            next(runs[g])
        lane = lax.broadcasted_iota(jnp.int32, (1, hw), 1)
        loss_c, lgf = out[0]
        for g in range(1, GROUPS):
            late = lane >= g * per * CLASSES
            loss_c = jnp.where(late, out[g][0], loss_c)
            lgf = jnp.where(late, out[g][1], lgf)
        sums[0, :, :hw] += fold8(lgf)
        sums[1, :, :hw] += fold8(loss_c)

    def wide_tile(t, carry):
        tile(2 * R, t * 2 * R)
        return carry

    def narrow_tile(t, carry):
        tile(R, t * R)
        return carry

    def clear(t, carry):
        for m in range(mem):
            fog_all[m, pl.ds(pl.multiple_of(t * R, R), R), :] = jnp.zeros((R, width), bf16)
        return carry
    wide = (n_rows + (R - 1)) // (2 * R) if WIDE else 0
    lax.fori_loop(0, wide, wide_tile, 0)
    tiles = jnp.maximum((n_rows + (R - 1)) // R, 2 * wide)
    lax.fori_loop(2 * wide, tiles, narrow_tile, 0)
    lax.fori_loop(tiles, rows_all // R, clear, 0)
    for d in range(8):
        for c in range(4):
            lanes = slice(128 * c, 128 * c + 128)
            sbuf[d // 2, d % 2, c // 2, c % 2] = second_acc[rs * d:rs * (d + 1), lanes].astype(bf16)
    head_t = head_acc[...].T
    for d in range(8):
        hb[d // 2, d % 2] = head_t[rs * d:rs * (d + 1), :].astype(bf16)
    small[...] = jnp.zeros_like(small)
    a0, a1, a2, a3, a4 = (jnp.sum(adapt[j], axis=1) for j in range(5))
    fixed = ((a0 - 0.5 * adapters[1] * a1) / adapters[0], 0.5 * a1, a2,
             (a3 - 0.5 * adapters[4] * a4) / adapters[3], 0.5 * a4)
    for m in range(mem):
        for k in range(4):
            for j in range(5):
                small[m, 8 * k + j:8 * k + j + 1, :] = fixed[j][m:m + 1, 128 * k:128 * k + 128]
    def four(row):
        return row[:, 0:128] + row[:, 128:256] + row[:, 256:384] + row[:, 384:512]
    def rows_sum(v):
        return jnp.sum(v, axis=0, keepdims=True)
    extra = (rows_sum(sums[1, :, 0:128]), four(rows_sum(sums[2]) + sums[4, 0:1]),
             four(rows_sum(sums[3]) + sums[4, 1:2]), rows_sum(sums[0, :, 0:128]))
    for m, row in enumerate(extra):
        for k in range(4):
            small[m, 8 * k + 5:8 * k + 6, :] = row


def call_compute(members, buf, hbuf, adbuf, enc, onehots, info, gains, bias):
    rows = enc.shape[0]
    enc_w = gains.shape[1]
    mem = adbuf.shape[2]
    width = adbuf.shape[0] * 128
    hw = mem * CLASSES
    return pl.pallas_call(
        functools.partial(compute_kernel, members),
        out_shape=(
            jax.ShapeDtypeStruct((enc_w, width), bf16),
            jax.ShapeDtypeStruct((mem, rows, width), bf16),
            jax.ShapeDtypeStruct((4, 2, 2, 2, width // 8, 128), bf16),
            jax.ShapeDtypeStruct(hbuf.shape, bf16),
            jax.ShapeDtypeStruct((8, 32, 128), f32),
        ),
        in_specs=[VM] * 6 + [FAR] * 2, out_specs=(VM,) * 5,
        scratch_shapes=[
            pltpu.VMEM((width, width), bf16), pltpu.VMEM((width, width), bf16),
            pltpu.VMEM((width, hw), bf16), pltpu.VMEM((hw, width), bf16),
            pltpu.VMEM((5, mem, width), f32), pltpu.VMEM((mem, enc_w), f32),
            pltpu.VMEM((mem, enc_w), bf16),
            pltpu.VMEM((width, width), f32), pltpu.VMEM((hw, width), f32),
            pltpu.VMEM((5, mem, 8, width), f32), pltpu.VMEM((5, 8, width), f32), pltpu.VMEM((5, mem, width), f32),
            pltpu.VMEM(gains.shape, f32), pltpu.VMEM(bias.shape, f32), pltpu.SemaphoreType.DMA((2,)),
        ],
        compiler_params=pltpu.CompilerParams(vmem_limit_bytes=36 << 20),
    )(buf, hbuf, adbuf, enc, onehots, info, far(gains), far(bias))


def reduce_kernel(enc_w, width, members,
                  enc, w1_all, fog, sbuf, hb, small, info,
                  f_w_first, f_w_second, f_w_head, f_adapters, f_gains, f_head_bias,
                  f_first_row, f_first_col, f_second_row, f_second_col, f_head_row, f_head_col, f_adapter_sq, f_gain_sq, f_bias_sq,
                  o_first_grad, o_first_row, o_first_col, o_first_new,
                  o_second_grad, o_second_row, o_second_col, o_second_new,
                  o_head_grad, o_head_row, o_head_col, o_head_new,
                  o_adapter_grad, o_adapter_sq, o_adapter_new,
                  o_gain_grad, o_gain_sq, o_gain_new,
                  o_bias_grad, o_bias_sq, o_bias_new,
                  o_scalars,
                  w1t, own_gains, first_acc, gain_acc, far_half, own_half, far_got, own_got, far_sum, far_x, own_sum, own_pair, first_y, first_pair, first_in,
                  second_got, second_sum, second_x, second_own, second_y, second_pair, second_in,
                  hy, hsum, hz, hcol, small_y, small_sum, small_z, gall, ca, gain_part, gain_in, gain_all, gain_cols,
                  colmsg, colall, rowmsg, rowall, msg, msgall, early_line,
                  w_first, w_second, w_head, adapters, gains, head_bias,
                  first_row, first_col, second_row, second_col, head_row, head_col, adapter_sq, gain_sq, bias_sq,
                  load_sem, send_sem, recv_sem):
    z, y, x, core = place()
    me_c, me_d = 2 * x + core, 2 * z + y
    loads = [pltpu.make_async_copy(src, dst, load_sem.at[i]) for i, (src, dst) in enumerate((
        (f_gains, gains),
        (f_w_first, w_first),
        (f_w_second, w_second),
        (f_w_head, w_head),
        (f_adapters, adapters),
        (f_head_bias, head_bias),
        (f_first_row, first_row),
        (f_first_col, first_col),
        (f_second_row, second_row),
        (f_second_col, second_col),
        (f_head_row, head_row),
        (f_head_col, head_col),
        (f_adapter_sq, adapter_sq),
        (f_gain_sq, gain_sq),
        (f_bias_sq, bias_sq)))]
    for load in loads:
        load.start()
    rf, rs = w_first.shape[0], w_second.shape[0]
    mem = members // 4
    hw = mem * CLASSES
    decay = 1.0 - STEP ** (-0.8)
    everyone = []
    for kz in range(4):
        for ky in range(2):
            for kx in range(2):
                for kc in range(2):
                    if kz or ky or kx or kc:
                        everyone.append(device(z_other(z, kz), other(y, ky), other(x, kx), other(core, kc)))
    barrier, count = greet(everyone)
    send = Sender(send_sem, recv_sem)
    mate = device(z, y, x, 1 - core)
    beside = device(z, y, 1 - x, core)
    dp_peers = [(z_other(z, kz), other(y, ky)) for kz, ky in DP_PEERS]

    def received(copies):
        for cp in copies:
            cp.wait_recv()

    def quarter(side, ms):
        half = pl.ds(pl.multiple_of(256 * side, 256), 256)
        parts = jnp.concatenate([fog[m, :, half].T for m in ms], axis=0)
        g = dot(parts, enc[...])
        for i, m in enumerate(ms):
            gm = g[256 * i:256 * (i + 1)]
            gain_acc[m] += fold8(gm * w1t[half, :].astype(f32))
            scaled = gm * own_gains[m:m + 1, :]
            if m == 0:
                first_acc[...] = scaled
            else:
                first_acc[...] += scaled

    def lay_out(half):
        flipped = first_acc[...].astype(bf16).T
        for d in range(8):
            for c in range(2):
                half[d // 2, d % 2, c] = flipped[rf * d:rf * (d + 1), 128 * c:128 * c + 128]

    def to_z(whole, ref, into):
        return send.group(whole, [(ref(z_other(z, k)), into(k), device(z_other(z, k), y, x, core)) for k in (1, 2, 3)])

    def to_dp(whole, ref, into):
        return send.group(whole, [(ref(2 * pz + py), into(i), device(pz, py, x, core)) for i, (pz, py) in enumerate(dp_peers)])

    mate_c, beside_c, corner_c = 2 * x + 1 - core, 2 * (1 - x) + core, 2 * (1 - x) + 1 - core

    def to_near(buffer, src):
        return send.group(buffer.at[0:2], [(src, buffer.at[me_c], mate), (src, buffer.at[me_c], beside)])

    def pass_on(buffer):
        return [send(buffer.at[beside_c], buffer.at[beside_c], mate)]

    def to_col(whole, ref, into):
        return send.group(whole, [(ref(2 * other(x, kx) + other(core, kc)), into, device(z, y, other(x, kx), other(core, kc)))
                                  for kx, kc in COL_PEERS])

    y_mate = device(z, 1 - y, x, core)
    w1t[...] = w1_all[...].T
    loads[0].wait()
    own_gains[...] = gains[pl.ds(pl.multiple_of(me_c * mem, mem), mem), :]
    gain_acc[...] = jnp.zeros_like(gain_acc)
    early, late = range(mem // 2), range(mem // 2, mem)
    quarter(1 - x, early)
    quarter(1 - x, late)
    lay_out(far_half)
    pl.semaphore_wait(barrier, count)
    swap_far = send(far_half.at[:, :, 1 - core], far_got, mate)
    swap_second = send(sbuf.at[:, :, :, 1 - core], second_got, mate)
    small1 = send(small.at[:, 1 - y], small_y, y_mate)
    head1 = send(hb.at[:, 1 - y], hy, y_mate)
    received([swap_far])
    far_sum[...] = (far_half[:, :, core].astype(f32) + far_got[...].astype(f32)).astype(bf16)
    across_far = send(far_sum, far_x, beside)
    quarter(x, early)
    received([swap_second])
    second_sum[...] = (sbuf[:, :, :, core].astype(f32) + second_got[...].astype(f32)).astype(bf16)
    second2 = send(second_sum.at[:, 1 - y], second_y, y_mate)
    quarter(x, late)
    lay_out(own_half)
    swap_own = send(own_half.at[:, :, 1 - core], own_got, mate)
    gain_part[...] = jnp.zeros_like(gain_part)
    for m in range(mem):
        row = jnp.sum(gain_acc[m], axis=0, keepdims=True)
        for i in range(enc_w // 128):
            gain_part[m, i:i + 1, :] = row[:, 128 * i:128 * i + 128]
    gain_deal = to_dp(gain_in, lambda d: gain_part.at[d], lambda i: gain_in.at[i])
    received([small1])
    small_sum[...] = small[:, y] + small_y[...]
    small2 = to_z(small_z, lambda pz: small_sum.at[pz], lambda k: small_z.at[k - 1])
    received([head1])
    hsum[...] = (hb[:, y].astype(f32) + hy[...].astype(f32)).astype(bf16)
    head2 = to_z(hz, lambda pz: hsum.at[pz], lambda k: hz.at[k - 1])
    for load in loads[1:]:
        load.wait()
    w1, w2 = w_first[...], w_second[...]
    wh = [w_head[mem * c:mem * (c + 1)].reshape(hw, rs).T for c in range(4)]
    own_w = (jnp.sum(w1 * w1), jnp.sum(w2 * w2), sum(jnp.sum(w * w) for w in wh))
    adapter_w = [jnp.sum(adapters[j] * adapters[j]) for j in range(5)]
    received([second2])
    second_own[...] = (second_sum[:, y].astype(f32) + second_y[...].astype(f32)).astype(bf16)
    second3 = send(second_own.at[:, 1 - x], second_x, beside)
    received([swap_own])
    own_sum[...] = own_half[:, :, core].astype(f32) + own_got[...].astype(f32)
    received([across_far])
    own_pair[...] = (own_sum[...] + far_x[...].astype(f32)).astype(bf16)
    first2 = send(own_pair.at[:, 1 - y], first_y, y_mate)
    received(gain_deal)
    mine = gain_part[me_d]
    for i in range(7):
        mine = mine + gain_in[i]
    gain_all[me_d] = mine
    gain_dp = to_dp(gain_in, lambda d: gain_all.at[me_d], lambda i: gain_all.at[me_d])
    received(small2)
    gall[z, y] = ((small_sum[z] + small_z[0]) + small_z[1]) + small_z[2]
    small3 = to_z(gall.at[0:3, 0], lambda pz: gall.at[z, y], lambda k: gall.at[z, y])
    received(head2)
    hcol[me_c] = (hsum[z].astype(f32) + hz[0].astype(f32)) + (hz[1].astype(f32) + hz[2].astype(f32))
    head3 = to_near(hcol, hcol.at[me_c])
    received([second3])
    second_pair[...] = (second_own[:, x].astype(f32) + second_x[...].astype(f32)).astype(bf16)
    second4 = to_z(second_in, lambda pz: second_pair.at[pz], lambda k: second_in.at[k - 1])
    received([first2])
    first_pair[...] = (own_pair[:, y].astype(f32) + first_y[...].astype(f32)).astype(bf16)
    first3 = to_z(first_in, lambda pz: first_pair.at[pz], lambda k: first_in.at[k - 1])
    received(head3)
    head4 = pass_on(hcol)
    received(small3)
    small4 = send(gall.at[:, y], gall.at[:, y], y_mate)
    received(gain_dp)
    gain_cols[me_c] = gain_all[...]
    gain_spread = to_near(gain_cols, gain_cols.at[me_c])
    received(second4)
    second = second_pair[z].astype(f32)
    for i in range(3):
        second = second + second_in[i].astype(f32)
    second_sq = second * second + EPS_SQUARE
    o_second_grad[...] = second
    received(head4)
    hg = [hcol[c] for c in range(4)]
    hsq = [g * g + EPS_SQUARE for g in hg]
    seg8 = (lax.broadcasted_iota(jnp.int32, (mem, hw), 1) // CLASSES
            == lax.broadcasted_iota(jnp.int32, (mem, hw), 0)).astype(f32)
    ones8 = jnp.ones((8, 128), f32)
    hrow = [decay * head_row[mem * c:mem * (c + 1), :]
            + (1.0 - decay) / CLASSES * hdot(seg8, hsq[c], ((1,), (1,))) for c in range(4)]
    hrowx = [hdot(hrow[c], seg8, ((0,), (0,))) for c in range(4)]
    def add_up(v):
        return jnp.sum(v, axis=0, keepdims=True)
    for c in range(4):
        o_head_row[mem * c:mem * (c + 1), :] = hrow[c]
        o_head_grad[mem * c:mem * (c + 1)] = hg[c].T.reshape(mem, CLASSES, rs)
        colmsg[2 + c:3 + c, :] = add_up(hsq[c])
        colmsg[8 + c:9 + c, :] = add_up(hrowx[c])
    colmsg[1:2, :] = add_up(second_sq)
    rowmsg[:, 128:128 + rs] = hdot(ones8, second_sq, ((1,), (1,)))
    received([small4])
    own8 = pl.ds(pl.multiple_of(8 * me_c, 8), 8)
    ca[me_c] = gall[:, :, own8, :]
    spread_col = to_col(ca.at[0:3], lambda c: gall.at[:, :, pl.ds(pl.multiple_of(8 * c, 8), 8)], ca.at[me_c])
    received(gain_spread)
    gain_last = pass_on(gain_cols)
    received(first3)
    first = first_pair[z].astype(f32)
    for i in range(3):
        first = first + first_in[i].astype(f32)
    o_first_grad[...] = first
    first_sq = first * first + EPS_SQUARE
    rowmsg[:, 0:rf] = hdot(ones8, first_sq, ((1,), (1,)))
    rowall[me_c] = rowmsg[...]
    colmsg[0:1, :] = add_up(first_sq)
    colall[me_d] = colmsg[...]
    r1 = to_dp(colall.at[0:7], lambda d: colmsg, lambda i: colall.at[me_d])
    r1 += to_col(rowall.at[0:3], lambda c: rowmsg, rowall.at[me_c])
    received(spread_col)
    fold = (lax.broadcasted_iota(jnp.int32, (CLASSES, hw), 1) % CLASSES
            == lax.broadcasted_iota(jnp.int32, (CLASSES, hw), 0)).astype(f32)
    to8 = (lax.broadcasted_iota(jnp.int32, (8, members), 1) // mem
           == lax.broadcasted_iota(jnp.int32, (8, members), 0)).astype(f32)
    keep = (lax.broadcasted_iota(jnp.int32, (members, hw), 1) // CLASSES
            == lax.broadcasted_iota(jnp.int32, (members, hw), 0) % mem).astype(f32)
    def to_lanes(v):
        return hdot(to8, hdot(v, fold, ((0,), (0,))) * keep)
    def from_lanes(v):
        return hdot(fold, hdot(to8, v, ((0,), (0,))) * keep, ((1,), (1,)))
    def lane_sum(v):
        return jnp.sum(v, axis=1, keepdims=True)
    def total(v):
        return lane_sum(add_up(v))
    def step_size(weight_sq, entries):
        return RELATIVE_RATE * jnp.maximum(RATE_FLOOR, jnp.sqrt(weight_sq / entries))
    def apply(weight, update, update_sq, weight_sq, entries):
        limit = jnp.maximum(1.0, jnp.sqrt(update_sq / entries) / CLIP_LIMIT)
        return weight - step_size(weight_sq, entries) * (update / limit)
    adapter_up = []
    for j in range(5):
        grad = jnp.concatenate([ca[c, m // 2, m % 2, j:j + 1, :] for c in range(4) for m in range(mem)], axis=0)
        sq = decay * adapter_sq[j] + (1.0 - decay) * (grad * grad + EPS_SQUARE)
        o_adapter_grad[j] = grad
        o_adapter_sq[j] = sq
        adapter_up.append(grad * lax.rsqrt(sq))
    bias_lanes = jnp.concatenate([ca[c, 1, 1, 5:6, :] for c in range(4)] + [jnp.zeros((4, 128), f32)], axis=0)
    bias = from_lanes(bias_lanes)
    bias_state = decay * bias_sq[...] + (1.0 - decay) * (bias * bias + EPS_SQUARE)
    o_bias_grad[...] = bias
    o_bias_sq[...] = bias_state
    bias_up = bias * lax.rsqrt(bias_state)
    o_bias_new[...] = apply(head_bias[...], bias_up, total(bias_up * bias_up), total(head_bias[...] * head_bias[...]), members * CLASSES)
    rows_total = info[1:2, 0:1]
    loss_total = lane_sum(sum(ca[c, 0, 0, 5:6, :] for c in range(4)))
    spread_over = rows_total * (members * width)
    residual = jnp.sqrt(lane_sum(sum(ca[c, 0, 1, 5:6, :] for c in range(4))) / spread_over)
    branch_size = jnp.sqrt(lane_sum(sum(ca[c, 1, 0, 5:6, :] for c in range(4))) / spread_over)
    spot = lax.broadcasted_iota(jnp.int32, (8, 128), 0)
    o_scalars[...] = jnp.where(spot == 0, loss_total, jnp.where(spot == 1, rows_total, jnp.where(spot == 2, residual, branch_size)))
    hcol_old = to_lanes(head_col[...])
    lane = lax.broadcasted_iota(jnp.int32, (1, 128), 1)
    line = jnp.zeros((1, 128), f32)
    for i, v in enumerate([total(u * u) for u in adapter_up] + adapter_w):
        line = jnp.where(lane == 8 + i, v, line)
    early_line[...] = jnp.where(lax.broadcasted_iota(jnp.int32, (8, 128), 0) == 0, line, 0.0)
    for cp in r1:
        cp.wait_recv()
    col_sums = colall[0]
    for d in range(1, 8):
        col_sums = col_sums + colall[d]
    row_sums = (rowall[0] + rowall[1]) + (rowall[2] + rowall[3])
    first_r = decay * first_row[...] + (1.0 - decay) / width * row_sums[0:1, 0:rf]
    second_r = decay * second_row[...] + (1.0 - decay) / width * row_sums[0:1, 128:128 + rs]
    first_c = decay * first_col[...] + (1.0 - decay) / enc_w * col_sums[0:1]
    second_c = decay * second_col[...] + (1.0 - decay) / width * col_sums[1:2]
    head_c = decay * hcol_old[0:4] + (1.0 - decay) / width * col_sums[2:6]
    ones1 = jnp.ones((1, 128), f32)
    first_up = first * lax.rsqrt(hdot(first_r, ones1, ((0,), (0,))) * first_c)
    second_up = second * lax.rsqrt(hdot(second_r, ones1, ((0,), (0,))) * second_c)
    head_up = [hg[c] * lax.rsqrt(hrowx[c] * head_c[c:c + 1] / (col_sums[8 + c:9 + c] / width)) for c in range(4)]
    scalars = [total(first_up * first_up), lane_sum(first_r), total(second_up * second_up), lane_sum(second_r),
               own_w[0], own_w[1], total(sum(u * u for u in head_up)), own_w[2]]
    line = jnp.sum(early_line[...], axis=0, keepdims=True)
    for i, v in enumerate(scalars):
        line = jnp.where(lane == i, v, line)
    msg[...] = jnp.broadcast_to(line, (8, 128))
    msgall[4 * me_d + me_c] = msg[...]
    r2 = send.group(msgall.at[0:31], [(msg, msgall.at[4 * me_d + me_c], target) for target in everyone[::-1]])
    o_first_row[...] = first_r
    o_second_row[...] = second_r
    o_first_col[...] = first_c
    o_second_col[...] = second_c
    o_head_col[...] = from_lanes(jnp.concatenate([head_c, jnp.zeros((4, 128), f32)], axis=0))
    received(gain_last)
    for c in range(4):
        for i in range(enc_w // 128):
            o_gain_grad[mem * c:mem * (c + 1), 128 * i:128 * (i + 1)] = gain_cols[c, :, i, :]
    gain = o_gain_grad[...]
    gain_state = decay * gain_sq[...] + (1.0 - decay) * (gain * gain + EPS_SQUARE)
    o_gain_sq[...] = gain_state
    gain_up = gain * lax.rsqrt(gain_state)
    o_gain_new[...] = apply(gains[...], gain_up, total(gain_up * gain_up), total(gains[...] * gains[...]), members * enc_w)
    for cp in send.all[:-len(r2)]:
        cp.wait_send()
    for cp in r2:
        cp.wait_recv()
    def over_dp(c):
        out = msgall[c, 0:1, :]
        for d in range(1, 8):
            out = out + msgall[4 * d + c, 0:1, :]
        return out
    s_dp = over_dp(me_c)
    s_all = (over_dp(0) + over_dp(1)) + (over_dp(2) + over_dp(3))
    s_col = (msgall[4 * me_d, 0:1, :] + msgall[4 * me_d + 1, 0:1, :]) + (msgall[4 * me_d + 2, 0:1, :] + msgall[4 * me_d + 3, 0:1, :])
    def item(v, i):
        return lane_sum(jnp.where(lane == i, v, 0.0))
    first_mean = item(s_dp, 1) / enc_w
    o_first_new[...] = apply(w1, first_up * jnp.sqrt(first_mean), item(s_all, 0) * first_mean, item(s_all, 4), enc_w * width)
    second_mean = item(s_dp, 3) / width
    o_second_new[...] = apply(w2, second_up * jnp.sqrt(second_mean), item(s_all, 2) * second_mean, item(s_all, 5), width * width)
    for j in range(5):
        o_adapter_new[j] = apply(adapters[j], adapter_up[j], item(s_col, 8 + j), item(s_col, 13 + j), members * width)
    for c in range(4):
        new = apply(wh[c], head_up[c], item(s_dp, 6), item(s_dp, 7), members * width * CLASSES)
        o_head_new[mem * c:mem * (c + 1)] = new.T.reshape(mem, CLASSES, rs)
    for cp in r2:
        cp.wait_send()


def call_reduce(enc, w1_all, fog, sbuf, hb, small, info, w_first, w_second, w_head, adapters, gains, head_bias,
                first_row, first_col, second_row, second_col, head_row, head_col, adapter_sq, gain_sq, bias_sq):
    members, enc_w = gains.shape
    rf, rs = w_first.shape[0], w_second.shape[0]
    width = w_first.shape[1] * 4
    mem = members // 4
    def like(a):
        return jax.ShapeDtypeStruct(a.shape, f32)
    def row(a):
        return jax.ShapeDtypeStruct((1, a.shape[0]), f32)
    def buffer(*shape, dtype=f32):
        return pltpu.VMEM(shape, dtype)
    params = (w_first, w_second, w_head, adapters, gains, head_bias,
              first_row.reshape(1, -1), first_col.reshape(1, -1), second_row.reshape(1, -1), second_col.reshape(1, -1),
              head_row, head_col, adapter_sq, gain_sq, bias_sq)
    outs = pl.pallas_call(
        functools.partial(reduce_kernel, enc_w, width, members),
        out_shape=(like(w_first), row(first_row), row(first_col), like(w_first),
                   like(w_second), row(second_row), row(second_col), like(w_second),
                   like(w_head), like(head_row), like(head_col), like(w_head),
                   like(adapters), like(adapters), like(adapters),
                   like(gains), like(gains), like(gains),
                   like(head_bias), like(head_bias), like(head_bias), jax.ShapeDtypeStruct((8, 128), f32)),
        in_specs=[VM] * 7 + [FAR] * 15, out_specs=(VM,) * 22,
        scratch_shapes=[
            buffer(width, enc_w, dtype=bf16), buffer(mem, enc_w), buffer(256, enc_w), buffer(mem, 8, enc_w),
            buffer(4, 2, 2, rf, 128, dtype=bf16), buffer(4, 2, 2, rf, 128, dtype=bf16),
            buffer(4, 2, rf, 128, dtype=bf16), buffer(4, 2, rf, 128, dtype=bf16), buffer(4, 2, rf, 128, dtype=bf16),
            buffer(4, 2, rf, 128, dtype=bf16), buffer(4, 2, rf, 128), buffer(4, 2, rf, 128, dtype=bf16),
            buffer(4, rf, 128, dtype=bf16), buffer(4, rf, 128, dtype=bf16), buffer(3, rf, 128, dtype=bf16),
            buffer(4, 2, 2, rs, 128, dtype=bf16), buffer(4, 2, 2, rs, 128, dtype=bf16), buffer(4, rs, 128, dtype=bf16),
            buffer(4, 2, rs, 128, dtype=bf16), buffer(4, 2, rs, 128, dtype=bf16), buffer(4, rs, 128, dtype=bf16),
            buffer(3, rs, 128, dtype=bf16),
            buffer(4, rs, 128, dtype=bf16), buffer(4, rs, 128, dtype=bf16), buffer(3, rs, 128, dtype=bf16),
            buffer(4, rs, 128),
            buffer(4, 32, 128), buffer(4, 32, 128), buffer(3, 32, 128), buffer(4, 2, 32, 128), buffer(4, 4, 2, 8, 128),
            buffer(mem, 8, 128), buffer(7, 8, 128), buffer(8, 8, 128), buffer(4, 8, 8, 128),
            buffer(16, 128), buffer(8, 16, 128), buffer(8, 256), buffer(4, 8, 256),
            buffer(8, 128), buffer(32, 8, 128), buffer(8, 128),
            *[buffer(*p.shape) for p in params], pltpu.SemaphoreType.DMA((15,)),
            pltpu.SemaphoreType.DMA((NSEM3,)), pltpu.SemaphoreType.DMA((NSEM3,)),
        ],
        compiler_params=pltpu.CompilerParams(collective_id=1, has_side_effects=True, vmem_limit_bytes=26 << 20),
    )(enc, w1_all, fog, sbuf, hb, small.reshape(4, 2, 32, 128), info, *map(far, params))
    outs = call_store(outs)
    for i in (1, 2, 5, 6):
        outs[i] = outs[i].reshape(-1)
    for i in (21, 22, 23, 24):
        outs[i] = outs[i].reshape(())
    for i in (8, 11):
        outs[i] = outs[i].transpose(0, 2, 1)
    for i in (10, 18, 19, 20):
        outs[i] = outs[i].T
    return tuple(outs)


def store_kernel(count, *refs):
    arrays, scalars = refs[:count], refs[count]
    outs, singles = refs[count + 1:2 * count + 1], refs[2 * count + 1:2 * count + 5]
    kept, sems = refs[2 * count + 5:2 * count + 9], refs[2 * count + 9]
    copies = [pltpu.make_async_copy(src, dst, sems.at[i]) for i, (src, dst) in enumerate(zip(arrays, outs))]
    for copy in copies:
        copy.start()
    for i, (one, single) in enumerate(zip(kept, singles)):
        one[...] = scalars[i:i + 1, 0:1]
        copies.append(pltpu.make_async_copy(one, single, sems.at[count + i]))
        copies[-1].start()
    for copy in copies:
        copy.wait()


def call_store(arrays):
    count = len(arrays) - 1
    one = jax.ShapeDtypeStruct((1, 1), f32)
    return list(pl.pallas_call(
        functools.partial(store_kernel, count),
        out_shape=tuple(jax.ShapeDtypeStruct(a.shape, a.dtype) for a in arrays[:-1]) + (one,) * 4,
        in_specs=[VM] * (count + 1), out_specs=(FAR,) * (count + 4),
        scratch_shapes=[pltpu.VMEM((1, 1), f32)] * 4 + [pltpu.SemaphoreType.DMA((count + 4,))],
        compiler_params=pltpu.CompilerParams(vmem_limit_bytes=16 << 20),
    )(*arrays))


def local_blocks(bin_index, bin_fraction, row_mask, targets, w_first, w_second, w_head, adapters, gains, head_bias,
          first_row, first_col, second_row, second_col, head_row, head_col, adapter_sq, gain_sq, bias_sq):
    members = gains.shape[0]
    mem = members // 4
    w_head, head_bias, head_col, bias_sq = w_head.transpose(0, 2, 1), head_bias.T, head_col.T, bias_sq.T
    buf, hbuf, adbuf, enc, onehots, info = call_gather(
        bin_index.T, bin_fraction.T, row_mask, targets, w_first, w_second, w_head, adapters, mem)
    w1_all, fog, sbuf, hb, small = call_compute(members, buf, hbuf, adbuf, enc, onehots, info, gains, head_bias)
    return call_reduce(enc, w1_all, fog, sbuf, hb, small, info, w_first, w_second, w_head, adapters, gains, head_bias,
                       first_row, first_col, second_row, second_col, head_row, head_col, adapter_sq, gain_sq, bias_sq)


def finish(weight, update, update_sq, weight_sq, entries):
    rms_update = jnp.sqrt(update_sq / entries)
    rms_weight = jnp.sqrt(weight_sq / entries)
    update = update / jnp.maximum(1.0, rms_update / CLIP_LIMIT)
    return weight - RELATIVE_RATE * jnp.maximum(RATE_FLOOR, rms_weight) * update


def local_any(bin_index, bin_fraction, row_mask, targets, w_first, w_second, w_head, adapters, gains, head_bias,
              first_row, first_col, second_row, second_col, head_row, head_col, adapter_sq, gain_sq, bias_sq):
    count_col = lax.axis_size("col")
    count_dp = lax.axis_size("dp")
    col_place = lax.axis_index("col")
    dp_place = lax.axis_index("dp")
    members, enc_width = gains.shape
    col_width = adapters.shape[2]
    full_width = col_width * count_col
    mem = members // count_col
    rows = row_mask.shape[0]
    decay = 1.0 - STEP ** (-0.8)
    row_total = lax.psum(jnp.sum(row_mask.astype(f32)), "dp")
    hi = bin_fraction.astype(bf16).astype(f32)
    onehot = jax.nn.one_hot(targets, CLASSES, dtype=f32) * row_mask[:, None]
    table = jnp.concatenate([bin_index.astype(f32), hi, bin_fraction - hi, onehot, row_mask[:, None].astype(f32),
                             jnp.zeros((rows, 63), f32)], axis=1).astype(bf16)
    table = table.reshape(rows // count_dp, count_dp, 128)
    table = jnp.roll(table, -dp_place, axis=1).transpose(1, 0, 2).reshape(rows, 128)
    table = lax.all_to_all(table, "dp", 0, 0, tiled=True)
    mask = table[:, 64].astype(jnp.int32)
    spot = jnp.where(mask > 0, jnp.cumsum(mask) - 1, -1)
    comp = jnp.dot((jnp.arange(rows)[:, None] == spot[None, :]).astype(bf16), table, preferred_element_type=f32).astype(bf16)
    levels = jnp.arange(BINS, dtype=f32)
    where_at = (comp[:, :FEATS].astype(f32) + comp[:, FEATS:2 * FEATS].astype(f32) + comp[:, 2 * FEATS:3 * FEATS].astype(f32))
    enc = jnp.clip(where_at[:, :, None] - levels, 0.0, 1.0).reshape(rows, enc_width).astype(bf16)
    onehots = jnp.tile(comp[:, 48:48 + CLASSES], (1, mem))
    info = jnp.zeros((8, 128), f32).at[0].set(jnp.sum(mask).astype(f32)).at[1].set(row_total)

    def whole(part):
        return lax.all_gather(lax.all_gather(part.astype(bf16), "dp", axis=0, tiled=True), "col", axis=1, tiled=True)

    def blocks(full):
        return full.reshape(8, -1, 4, 128).transpose(0, 2, 1, 3)

    def unblock(part):
        return part.astype(f32).reshape(8, 4, -1, 128).transpose(0, 2, 1, 3).reshape(-1, full_width)
    buf = jnp.concatenate([blocks(whole(w_first)), blocks(whole(w_second))], axis=2).reshape(4, 2, 2, 2, -1, 128)
    heads = lax.all_gather(w_head.astype(bf16), "dp", axis=1, tiled=True)
    heads = lax.dynamic_slice_in_dim(heads, col_place * mem, mem, 0)
    hbuf = heads.transpose(1, 0, 2).reshape(4, 2, -1, mem * CLASSES)
    adbuf = lax.dynamic_slice_in_dim(lax.all_gather(adapters, "col", axis=0), col_place * mem, mem, 2)
    w1_all, fog, sbuf, hb, small = call_compute(members, buf, hbuf, adbuf, enc, onehots, info, gains, head_bias.T)
    own_gains = lax.dynamic_slice_in_dim(gains, col_place * mem, mem, 0)
    sums = jnp.einsum("rk,mrd->mkd", enc, fog, preferred_element_type=f32)
    first_part = jnp.einsum("mkd,mk->kd", sums, own_gains, precision=HIGH)
    gain_part = jnp.einsum("mkd,kd->mk", sums, w1_all.astype(f32), precision=HIGH)
    second_part = unblock(sbuf)
    head_part = hb.astype(f32).reshape(full_width, mem, CLASSES).transpose(1, 0, 2)

    def scatter(part):
        return lax.psum_scatter(lax.psum_scatter(part, "dp", scatter_dimension=0, tiled=True), "col", scatter_dimension=1, tiled=True)
    first_grad, second_grad = scatter(first_part), scatter(second_part)
    head_grad = lax.all_gather(lax.psum_scatter(head_part, "dp", scatter_dimension=1, tiled=True), "col", axis=0, tiled=True)
    adapter_part = small[:, :32].reshape(mem, 4, 8, 128)[:, :, :5].transpose(2, 0, 1, 3).reshape(5, mem, full_width)
    adapter_grad = lax.psum(lax.all_to_all(adapter_part, "col", 2, 1, tiled=True), "dp")
    bias_part = small[3, 5].reshape(mem, CLASSES)
    gain_grad, bias_grad = lax.psum(
        (lax.all_gather(gain_part, "col", axis=0, tiled=True), lax.all_gather(bias_part, "col", axis=0, tiled=True)), "dp")
    loss_sum, residual_sq, branch_sq = lax.psum(jnp.sum(small[:3, 5], axis=1), ("dp", "col"))
    first_square = first_grad * first_grad + EPS_SQUARE
    second_square = second_grad * second_grad + EPS_SQUARE
    head_square = head_grad * head_grad + EPS_SQUARE
    first_rowsum, second_rowsum = lax.psum(
        (jnp.sum(first_square, axis=1), jnp.sum(second_square, axis=1)), "col"
    )
    first_row_new = decay * first_row + (1.0 - decay) * (first_rowsum / full_width)
    second_row_new = decay * second_row + (1.0 - decay) * (second_rowsum / full_width)
    head_row_new = decay * head_row + (1.0 - decay) * jnp.mean(head_square, axis=-1)
    stats = lax.psum(
        (
            jnp.sum(first_square, axis=0),
            jnp.sum(second_square, axis=0),
            jnp.sum(head_square, axis=1),
            jnp.sum(first_row_new),
            jnp.sum(second_row_new),
            jnp.sum(head_row_new, axis=1),
        ),
        "dp",
    )
    first_colsum, second_colsum, head_colsum, first_rowtotal, second_rowtotal, head_rowtotal = stats
    first_col_new = decay * first_col + (1.0 - decay) * (first_colsum / enc_width)
    second_col_new = decay * second_col + (1.0 - decay) * (second_colsum / full_width)
    head_col_new = decay * head_col + (1.0 - decay) * (head_colsum / full_width)
    first_estimate = first_row_new[:, None] * first_col_new[None, :] / (first_rowtotal / enc_width)
    second_estimate = (
        second_row_new[:, None] * second_col_new[None, :] / (second_rowtotal / full_width)
    )
    head_estimate = (
        head_row_new[:, :, None]
        * head_col_new[:, None, :]
        / (head_rowtotal / full_width)[:, None, None]
    )
    first_update = first_grad * lax.rsqrt(first_estimate)
    second_update = second_grad * lax.rsqrt(second_estimate)
    head_update = head_grad * lax.rsqrt(head_estimate)
    adapter_sq_new = decay * adapter_sq + (1.0 - decay) * (adapter_grad * adapter_grad + EPS_SQUARE)
    adapter_update = adapter_grad * lax.rsqrt(adapter_sq_new)
    gain_sq_new = decay * gain_sq + (1.0 - decay) * (gain_grad * gain_grad + EPS_SQUARE)
    gain_update = gain_grad * lax.rsqrt(gain_sq_new)
    bias_sq_new = decay * bias_sq + (1.0 - decay) * (bias_grad * bias_grad + EPS_SQUARE)
    bias_update = bias_grad * lax.rsqrt(bias_sq_new)
    share_col = 1.0 / count_col
    share_dp = 1.0 / count_dp
    sums = lax.psum(
        (
            jnp.sum(first_update * first_update),
            jnp.sum(w_first * w_first),
            jnp.sum(second_update * second_update),
            jnp.sum(w_second * w_second),
            jnp.sum(head_update * head_update) * share_col,
            jnp.sum(w_head * w_head) * share_col,
            jnp.sum(adapter_update * adapter_update, axis=(1, 2)) * share_dp,
            jnp.sum(adapters * adapters, axis=(1, 2)) * share_dp,
        ),
        ("dp", "col"),
    )
    first_new = finish(w_first, first_update, sums[0], sums[1], enc_width * full_width)
    second_new = finish(w_second, second_update, sums[2], sums[3], full_width * full_width)
    head_new = finish(w_head, head_update, sums[4], sums[5], members * full_width * CLASSES)
    adapter_new = finish(
        adapters,
        adapter_update,
        sums[6].reshape(5, 1, 1),
        sums[7].reshape(5, 1, 1),
        members * full_width,
    )
    gain_new = finish(
        gains,
        gain_update,
        jnp.sum(gain_update * gain_update),
        jnp.sum(gains * gains),
        members * enc_width,
    )
    bias_new = finish(
        head_bias,
        bias_update,
        jnp.sum(bias_update * bias_update),
        jnp.sum(head_bias * head_bias),
        members * CLASSES,
    )
    residual_rms = jnp.sqrt(residual_sq / (row_total * members * full_width))
    branch_rms = jnp.sqrt(branch_sq / (row_total * members * full_width))
    return (
        first_grad,
        first_row_new,
        first_col_new,
        first_new,
        second_grad,
        second_row_new,
        second_col_new,
        second_new,
        head_grad,
        head_row_new,
        head_col_new,
        head_new,
        adapter_grad,
        adapter_sq_new,
        adapter_new,
        gain_grad,
        gain_sq_new,
        gain_new,
        bias_grad,
        bias_sq_new,
        bias_new,
        loss_sum,
        row_total,
        residual_rms,
        branch_rms,
    )


def local(*args):
    if lax.axis_size("dp") == 8 and lax.axis_size("col") == 4:
        return local_blocks(*args)
    return local_any(*args)


def solution(mesh):
    placed = (
        P("dp", None),
        P("dp", None),
        P("dp"),
        P("dp"),
        P("dp", "col"),
        P("dp", "col"),
        P(None, "dp", None),
        P(None, None, "col"),
        P(),
        P(),
        P("dp"),
        P("col"),
        P("dp"),
        P("col"),
        P(None, "dp"),
        P(),
        P(None, None, "col"),
        P(),
        P(),
    )
    return jax.shard_map(
        local,
        mesh=mesh,
        in_specs=placed,
        out_specs=(
            P("dp", "col"),
            P("dp"),
            P("col"),
            P("dp", "col"),
            P("dp", "col"),
            P("dp"),
            P("col"),
            P("dp", "col"),
            P(None, "dp", None),
            P(None, "dp"),
            P(),
            P(None, "dp", None),
            P(None, None, "col"),
            P(None, None, "col"),
            P(None, None, "col"),
            P(),
            P(),
            P(),
            P(),
            P(),
            P(),
            P(),
            P(),
            P(),
            P(),
        ),
        check_vma=False,
    )
```
